256 devices in a mesh: slab: 4 (over x), dom: 64 (over z, y, core).
Axes of the slice: x: 4, y: 4, z: 8, core: 2. Of those that a mesh axis runs over, the one named last changes fastest.
Arguments:
- positions: float32 [3, 98304], P(None, ('slab', 'dom')), may hold values from -9 to 9
- species: int32 [98304], P(('slab', 'dom')), may hold values from 0 to 7
- domain: int32 [98304, 1], P(('slab', 'dom')), may hold values from 0 to 63; in each aligned block of 384 rows (0 to 383, 384 to 767, ...) at most 12 rows name the same one
- neighbours: int32 [16, 196608], P(None, ('slab', 'dom')), may hold values from 0 to 1535
- ghost_lists: int32 [2, 98304], P(None, ('slab', 'dom')), may hold values from 0 to 767, as said below
- embed_weight: bfloat16 [24, 256], replicated, may hold values from -1.25 to 1.25
- tensor_weight: bfloat16 [256, 32], replicated, may hold values from -0.375 to 0.375
- env_weight: bfloat16 [2, 256, 32], replicated, may hold values from -0.375 to 0.375
- scalar_mix: float32 [64, 32], replicated, may hold values from -0.75 to 0.75
- vector_mix: float32 [32, 32], replicated, may hold values from -1 to 1
- latent_weight: bfloat16 [2, 320, 256], replicated, may hold values from -0.3125 to 0.3125
- energy_weight: bfloat16 [256], replicated, may hold values from -0.375 to 0.375
Outputs:
- forces: float32 [3, 98304], P(None, ('slab', 'dom'))
- atom_energy: float32 [98304], P(('slab', 'dom'))
- atom_features: float32 [384, 98304], P(None, ('slab', 'dom'))
The draws below stay inside these ranges and needn't reach their ends.
Inputs may be any that keep to these rules, and one draw needn't show every extreme that they name: Within the rows of one device at most 12 atoms name the same domain, and some domain takes exactly 12. `ghost_lists`: for each device, its blocks of the two rows together name each of its 768 slots exactly once.
All inputs are finite; a program needn't handle non-finite values.
Results may differ from the reference program's by a relative error of at most 0.02.
Values sent between devices are 32-bit elements; how exact they have to be, the bound alone decides.
A program may use at most 64 MiB of HBM per device.

```python
import math
import jax
import jax.numpy as jnp
import numpy as np
from jax import lax

ATOM_DEV = 384
NEIGH = 16
LATENT = 256
CHAN = 32
BASIS = 8
SPECIES = 8
ATOMS = 98304
SLOTS = 768
CAP = 12
GHOST = 384
ALL_SLOTS = 196608
INPUT = 24
N_SLAB = 4
N_DOM = 64


def draw_ghost_lists(key, part):
    key = jax.random.fold_in(key, 7)
    devices = N_SLAB * N_DOM
    keys = jax.random.split(key, devices)
    orders = jax.vmap(lambda single: jax.random.permutation(single, SLOTS))(keys)
    halves = orders.reshape(devices, 2, GHOST).transpose(1, 0, 2)
    return halves.reshape(2, devices * GHOST).astype(jnp.int32)


def place_ends(result, rng, smallest, top_value):
    index_at = [jax.random.randint(jax.random.fold_in(rng, axis), (), 0, length) for axis, length in enumerate(result.shape)]
    widest = result.shape.index(max(result.shape))
    beside = index_at[:widest] + [(index_at[widest] + 1) % result.shape[widest]] + index_at[widest + 1:]
    return result.at[tuple(index_at)].set(smallest).at[tuple(beside)].set(top_value)


def block_levels(own_key, dims, pieces, low, largest):
    loudness = 1.0
    for position, parts in pieces:
        heights = jax.random.uniform(jax.random.fold_in(jax.random.fold_in(own_key, 6), position), (parts,), jnp.float32, low / len(pieces), largest / len(pieces))
        loudness = loudness * jnp.repeat(jnp.exp(heights), dims[position] // parts).reshape((-1,) + (1,) * (len(dims) - 1 - position))
    return loudness


def shared_out(stream_key, own, number, rows, number_of, top, limit, slope):
    ranking = jax.random.permutation(stream_key, number_of)
    packed, common = load_shares(number_of, rows * top, limit, slope, True), load_shares(number_of, rows * top, limit, slope, False)
    places = jnp.arange(number_of)

    def named(sizes, rotation):
        used = int((sizes > 0).sum())
        fixed = max(1, used // 4)
        shifted = fixed + (places - fixed + rotation * (used - fixed)) % max(1, number_of - fixed)
        return jnp.zeros((number_of,), jnp.int32).at[ranking[jnp.where(places < fixed, places, shifted)]].set(jnp.asarray(sizes, jnp.int32))

    sizes = jnp.where(number % 4 == 0, named(packed, number // 4), named(common, number - number // 4 - 1))
    mixed = jax.random.permutation(jax.random.fold_in(own, 3), number_of)
    source_of, taker = mixed[0:number_of // 2 * 2:2], mixed[1:number_of // 2 * 2:2]
    margin = jnp.minimum(sizes[source_of] - 1, limit - sizes[taker]) // 2
    margin = jnp.where((source_of == ranking[0]) | (taker == ranking[0]) | (sizes[taker] == 0), 0, jnp.maximum(margin, 0))
    shifted = jax.random.randint(jax.random.fold_in(own, 4), (number_of // 2,), 0, 1 << 20) % (margin + 1)
    sizes = sizes.at[source_of].add(-shifted).at[taker].add(shifted)
    members = jnp.searchsorted(jnp.cumsum(sizes), jnp.arange(rows * top), side="right").astype(jnp.int32)
    table = members.reshape(top, rows).T
    table = table[jax.random.permutation(jax.random.fold_in(own, 1), rows)]
    rotation = jax.random.randint(jax.random.fold_in(own, 2), (rows, 1), 0, top)
    return jnp.take_along_axis(table, (jnp.arange(top)[None, :] + rotation) % top, axis=1)


def load_shares(count, total, limit, lean, full):
    weights = [(1 << 20) // math.isqrt(standing ** lean) + 1 for standing in range(1, count + 1)]
    largest = limit if full else min(limit, max(-(-total // count), total * weights[0] // sum(weights)))
    least = 1 if total - largest >= count - 1 else 0
    counts, spare = [largest] + [least] * (count - 1), total - largest - least * (count - 1)
    while spare > 0:
        movable = [i for i in range(1, count) if counts[i] < largest] or [i for i in range(1, count) if counts[i] < limit]
        whole, remaining = sum([weights[i] for i in movable]), spare
        for i in movable:
            extra = min(limit - counts[i], max(1, remaining * weights[i] // whole), spare)
            counts[i] = counts[i] + extra
            spare = spare - extra
    return np.array(counts)


def bell_draw(key, extent, width, limit, cuts=(), held_as=jnp.bfloat16):
    array = jax.random.normal(key, extent, jnp.float32) * width
    if len(cuts) > 0:
        array = block_levels(key, extent, cuts, -0.22, 0.18) * array
    return jnp.clip(array, min=-limit, max=limit).astype(held_as)


def setup_inputs(seed: int = 0) -> dict:
    streams_of = jax.random.split(jax.random.key(seed), 13)
    positions = bell_draw(streams_of[0], (3, ATOMS), 1.5, 9.0, ((1, 256),), jnp.float32)
    species = place_ends(jax.random.randint(streams_of[1], (ATOMS,), 0, SPECIES), jax.random.fold_in(streams_of[1], 1), 0, SPECIES - 1).astype(jnp.int32)
    domain_keys = jax.random.split(jax.random.fold_in(streams_of[2], 1), ATOMS // ATOM_DEV)
    domain_turns = jax.random.permutation(jax.random.fold_in(streams_of[2], 3), ATOMS // ATOM_DEV)
    domain = jax.vmap(lambda own, number: shared_out(jax.random.fold_in(streams_of[2], 2), own, number, ATOM_DEV, N_DOM, 1, CAP, 2))(domain_keys, domain_turns).reshape((ATOMS, 1))
    neighbours = place_ends(jax.random.randint(streams_of[3], (NEIGH, ALL_SLOTS), 0, 2 * SLOTS), jax.random.fold_in(streams_of[3], 1), 0, (2 * SLOTS) - 1).astype(jnp.int32)
    ghost_lists = draw_ghost_lists(jax.random.fold_in(streams_of[12], 71), 0)
    embed_weight = bell_draw(streams_of[5], (INPUT, LATENT), INPUT ** -0.5, 1.25)
    tensor_weight = bell_draw(streams_of[6], (LATENT, CHAN), LATENT ** -0.5, 0.375)
    env_weight = bell_draw(streams_of[7], (2, LATENT, CHAN), LATENT ** -0.5, 0.375)
    scalar_mix = bell_draw(streams_of[8], (2 * CHAN, CHAN), (2 * CHAN) ** -0.5, 0.75, (), jnp.float32)
    vector_mix = bell_draw(streams_of[9], (CHAN, CHAN), CHAN ** -0.5, 1.0, (), jnp.float32)
    latent_weight = bell_draw(streams_of[10], (2, LATENT + 2 * CHAN, LATENT), (LATENT + 2 * CHAN) ** -0.5, 0.3125)
    energy_weight = bell_draw(streams_of[11], (LATENT,), LATENT ** -0.5, 0.375)
    return dict(positions=positions, species=species, domain=domain, neighbours=neighbours, ghost_lists=ghost_lists, embed_weight=embed_weight, tensor_weight=tensor_weight, env_weight=env_weight, scalar_mix=scalar_mix, vector_mix=vector_mix, latent_weight=latent_weight, energy_weight=energy_weight)


cutoff_radius = 5.0
soften = 0.25
neighbour_norm = 0.25
centre_block = 128

def envelope(scaled):
    return 1.0 - 28.0 * scaled ** 6 + 48.0 * scaled ** 7 - 21.0 * scaled ** 8

def block_terms(coords, kinds, centres, near_list, weights):
    embed_weight, tensor_weight, env_weight, scalar_mix, vector_mix, latent_weight, energy_weight = weights
    neigh_count, block_count = near_list.shape
    edge_count = neigh_count * block_count
    latent_width, chan_count = tensor_weight.shape
    centre_xyz = coords[:, centres]
    other_xyz = coords[:, near_list]
    offset = other_xyz - centre_xyz[:, None, :]
    radius = jnp.sqrt(lax.optimization_barrier(jnp.sum(offset * offset, axis=0)) + soften)
    direction = offset / radius[None]
    scaled = jnp.minimum(radius / cutoff_radius, 1.0)
    smooth = envelope(scaled)
    centre_kind = kinds[centres]
    other_kind = kinds[near_list]
    live_edge = (centre_kind[None, :] >= 0) & (other_kind >= 0) & (near_list != centres[None, :])
    edge_weight = jnp.where(live_edge, smooth, jnp.zeros_like(smooth)).reshape(edge_count)
    orders = jnp.arange(1, BASIS + 1).astype(jnp.float32)
    radial_basis = jnp.sin(jnp.pi * orders * scaled[..., None]) / scaled[..., None] * smooth[..., None]
    kind_range = jnp.arange(SPECIES).astype(jnp.int32)
    centre_hot = (centre_kind[:, None] == kind_range).astype(jnp.float32)
    centre_hot = jnp.broadcast_to(centre_hot[None], (neigh_count, block_count, SPECIES))
    other_hot = (other_kind[..., None] == kind_range).astype(jnp.float32)
    inputs = jnp.concatenate([radial_basis, centre_hot, other_hot], axis=-1)
    inputs = inputs.astype(jnp.bfloat16).reshape(edge_count, BASIS + 2 * SPECIES)
    latent = jax.nn.silu(jnp.dot(inputs, embed_weight, preferred_element_type=jnp.float32)).astype(jnp.bfloat16)
    ones_row = jnp.ones((1, neigh_count, block_count), jnp.float32)
    harmonics = jnp.concatenate([ones_row, direction], axis=0).reshape(4, edge_count).T
    amplitude = jnp.dot(latent, tensor_weight, preferred_element_type=jnp.float32)
    tensor = harmonics[:, :, None] * amplitude[:, None, :]
    density = None
    for layer_index in range(2):
        env_amp = jnp.dot(latent, env_weight[layer_index], preferred_element_type=jnp.float32) * edge_weight[:, None]
        env_edge = harmonics[:, :, None] * env_amp[:, None, :]
        density = neighbour_norm * lax.optimization_barrier(jnp.sum(env_edge.reshape(neigh_count, block_count, 4, chan_count), axis=0))
        spread = jnp.broadcast_to(density[None], (neigh_count, block_count, 4, chan_count))
        spread = spread.reshape(edge_count, 4, chan_count)
        scalars = jnp.concatenate([tensor[:, 0] * spread[:, 0], lax.optimization_barrier(jnp.sum(tensor[:, 1:] * spread[:, 1:], axis=1))], axis=-1)
        if layer_index == 0:
            vectors = tensor[:, :1] * spread[:, 1:] + tensor[:, 1:] * spread[:, :1]
            fresh_scalar = jnp.dot(scalars, scalar_mix, precision=lax.Precision.HIGHEST)
            fresh_vector = jnp.einsum('emc,cd->emd', vectors, vector_mix, precision=lax.Precision.HIGHEST)
            tensor = jnp.concatenate([fresh_scalar[:, None], fresh_vector], axis=1)
        joined = jnp.concatenate([latent, scalars.astype(jnp.bfloat16)], axis=-1)
        update = jax.nn.silu(jnp.dot(joined, latent_weight[layer_index], preferred_element_type=jnp.float32))
        latent = (latent.astype(jnp.float32) + update).astype(jnp.bfloat16)
    edge_energy = jnp.dot(latent, energy_weight, preferred_element_type=jnp.float32) * edge_weight
    energy = lax.optimization_barrier(jnp.sum(edge_energy.reshape(neigh_count, block_count), axis=0))
    weighted = (latent.astype(jnp.float32) * edge_weight[:, None]).reshape(neigh_count, block_count, latent_width)
    summary = neighbour_norm * lax.optimization_barrier(jnp.sum(weighted, axis=0))
    features = jnp.concatenate([summary, density.reshape(block_count, 4 * chan_count)], axis=-1)
    return (energy, features)

def domain_forces(coords, kinds, near_lists, weights):
    slot_count = near_lists.shape[1]

    def block_step(carry, block_index):
        first_slot = block_index * centre_block
        centres = first_slot + jnp.arange(centre_block).astype(jnp.int32)
        near_list = lax.dynamic_slice_in_dim(near_lists, first_slot, centre_block, 1)

        def total_energy(positions_in):
            energy, features = block_terms(positions_in, kinds, centres, near_list, weights)
            return (jnp.sum(energy), (energy, features))
        gradient, (energy, features) = jax.grad(total_energy, has_aux=True)(coords)
        return (carry + gradient, (energy, features))
    block_ids = jnp.arange(slot_count // centre_block).astype(jnp.int32)
    gradient, (energy, features) = lax.scan(block_step, jnp.zeros_like(coords), block_ids)
    return (gradient, energy.reshape(slot_count), features.reshape(slot_count, features.shape[-1]))

def add_returns(gradient, right_part, right_index, left_part, left_index):
    return gradient.at[:, right_index].add(right_part).at[:, left_index].add(left_part)

def reference(positions, species, domain, neighbours, ghost_lists, embed_weight, tensor_weight, env_weight, scalar_mix, vector_mix, latent_weight, energy_weight):
    weights = (embed_weight, tensor_weight, env_weight, scalar_mix, vector_mix, latent_weight, energy_weight)
    devices = N_SLAB * N_DOM
    target = domain[:, 0].reshape(devices, ATOM_DEV)
    one_hot = (target[..., None] == jnp.arange(N_DOM).astype(jnp.int32)).astype(jnp.int32)
    order_rank = lax.optimization_barrier(jnp.sum(one_hot * (jnp.cumsum(one_hot, axis=1) - one_hot), axis=-1))
    block_ids = jnp.arange(devices).astype(jnp.int32)[:, None]
    owner = block_ids // N_DOM * N_DOM + target
    slot_ids = block_ids % N_DOM * CAP + order_rank
    placement = (owner * SLOTS + slot_ids).reshape(devices * ATOM_DEV)
    spatial_pos = jnp.zeros((3, devices * SLOTS), jnp.float32).at[:, placement].set(positions)
    spatial_kind = jnp.full((devices * SLOTS,), -1, jnp.int32).at[placement].set(species)
    pos_dev = spatial_pos.reshape(3, devices, SLOTS).transpose(1, 0, 2)
    kind_dev = spatial_kind.reshape(devices, SLOTS)
    ghost_sets = ghost_lists.reshape(2, devices, GHOST)
    take_pos = jax.vmap(lambda block_pos, wanted: block_pos[:, wanted])
    take_kind = jax.vmap(lambda block_kind, wanted: block_kind[wanted])
    lend_down_pos = take_pos(pos_dev, ghost_sets[0])
    lend_up_pos = take_pos(pos_dev, ghost_sets[1])
    lend_down_kind = take_kind(kind_dev, ghost_sets[0])
    lend_up_kind = take_kind(kind_dev, ghost_sets[1])
    ext_pos = jnp.concatenate([pos_dev, jnp.roll(lend_up_pos, 1, axis=0), jnp.roll(lend_down_pos, -1, axis=0)], axis=2)
    ext_kind = jnp.concatenate([kind_dev, jnp.roll(lend_up_kind, 1, axis=0), jnp.roll(lend_down_kind, -1, axis=0)], axis=1)
    near_dev = neighbours.reshape(NEIGH, devices, SLOTS).transpose(1, 0, 2)
    gradient, energy, features = lax.map(lambda items: domain_forces(items[0], items[1], items[2], weights), (ext_pos, ext_kind, near_dev))
    own_part = gradient[:, :, :SLOTS]
    lower_back = gradient[:, :, SLOTS:SLOTS + GHOST]
    upper_back = gradient[:, :, SLOTS + GHOST:]
    into_upper = jnp.roll(lower_back, -1, axis=0)
    into_lower = jnp.roll(upper_back, 1, axis=0)
    total = jax.vmap(add_returns)(own_part, into_upper, ghost_sets[1], into_lower, ghost_sets[0])
    spatial_force = -total.transpose(1, 0, 2).reshape(3, devices * SLOTS)
    forces = spatial_force[:, placement]
    atom_energy = energy.reshape(devices * SLOTS)[placement]
    atom_features = features.reshape(devices * SLOTS, features.shape[-1])[placement].T
    return (forces, atom_energy, atom_features)
```

```python
import math

import jax
import jax.numpy as jnp
from jax import lax
from jax.experimental import pallas as pl
from jax.experimental.pallas import tpu as pltpu
from jax.sharding import PartitionSpec as P

F32 = jnp.float32
BF16 = jnp.bfloat16
LANES = 128
WIDE = 256
NEIGH = 16
UNROLL = 4


def mm(a, b):
    return jnp.dot(a, b, preferred_element_type=F32)


def silu_parts(half):
    gate = jnp.tanh(half)
    rise = 1.0 + gate
    value = half * rise
    slope = rise + value * (1.0 - gate)
    return value, slope


def arrange_weights(
    embed_weight, tensor_weight, env_weight, scalar_mix, vector_mix, latent_weight, energy_weight,
    w_in, w_first, w_mix, w_second, w_third, w_energy, b_second, b_mix, b_first, b_amp, b_in, stage,
):
    width, chan = tensor_weight.shape
    lat0, lat1 = latent_weight[0].astype(F32) * 0.5, latent_weight[1].astype(F32) * 0.5
    b_first[...] = lat0.astype(BF16)
    b_second[...] = lat1.astype(BF16)
    small = jnp.concatenate(
        [tensor_weight[...], env_weight[0], env_weight[1], jnp.zeros((width, chan), BF16)], axis=1)
    b_amp[...] = small[:, :64]
    small = small.astype(F32).T.astype(BF16)
    w_first[0:64] = small[0:64]
    w_first[64:] = lat0[:width].T.astype(BF16)
    w_second[0:32] = small[64:96]
    w_second[32:] = lat1[:width].T.astype(BF16)
    w_third[...] = lat1[width:].T.astype(BF16)
    embed = embed_weight[...].astype(F32) * 0.5
    b_in[...] = embed[:16].astype(BF16)
    w_in[...] = jnp.concatenate([embed, jnp.zeros((8, width), F32)], axis=0).T.astype(BF16)
    w_energy[...] = jnp.broadcast_to(energy_weight[...].astype(F32), (8, width)).T[:, 0:1] + jnp.zeros((width, WIDE), F32)
    stage[...] = jnp.zeros_like(stage)
    stage[0:64, 0:32] = scalar_mix[...]
    for m in range(3):
        stage[64 + 32 * m:96 + 32 * m, 32 + 32 * m:64 + 32 * m] = vector_mix[...]
    core = stage[...]
    b_mix[...] = jnp.zeros_like(b_mix)
    b_mix[0:width, 0:32] = env_weight[1]
    b_mix[width:, 32:] = core[0:160].astype(BF16)
    w_mix[...] = jnp.zeros_like(w_mix)
    w_mix[0:width, 0:64] = w_third_like(lat0[width:])
    w_mix[width:] = core.T[:, 0:160].astype(BF16)


def w_third_like(part):
    return part.T.astype(BF16)


def force_kernel(
    ext, near, embed_weight, tensor_weight, env_weight, scalar_mix, vector_mix, latent_weight, energy_weight,
    grad_out, energy_out, feature_out,
    w_in, w_first, w_mix, w_second, w_third, w_energy, b_second, b_mix, b_first, b_amp, b_in, stage,
    geo, kind_hot, lat0, slope0, half0, amp, tens, envl, lat1, slope1, half1, dlat, dscal, damp, back,
    dens0, dens1, ddens0, ddens1, summary, ghost_acc, centre_acc, energy_acc,
):
    blocks = geo.shape[0]
    own = ext
    slots = blocks * WIDE
    sub = ext.shape[1] // LANES
    arrange_weights(
        embed_weight, tensor_weight, env_weight, scalar_mix, vector_mix, latent_weight, energy_weight,
        w_in, w_first, w_mix, w_second, w_third, w_energy, b_second, b_mix, b_first, b_amp, b_in, stage)
    ghost_acc[...] = jnp.zeros_like(ghost_acc)

    for piece in range(blocks * WIDE // LANES):
        b, half = piece // 2, piece % 2
        lanes = pl.ds(half * LANES, LANES)
        index = near[:, piece * LANES:(piece + 1) * LANES]
        low = jnp.bitwise_and(index, LANES - 1)
        high = jnp.right_shift(index, 7)
        got = []
        for comp in range(4):
            value = jnp.zeros((NEIGH, LANES), F32)
            for h in range(sub):
                row = jnp.broadcast_to(ext[comp:comp + 1, h * LANES:(h + 1) * LANES], (NEIGH, LANES))
                taken = jnp.take_along_axis(row, low, axis=1)
                value = jnp.where(high == h, taken, value)
            got.append(value)
        mine = [own[c:c + 1, piece * LANES:(piece + 1) * LANES] for c in range(4)]
        off = [got[c] - mine[c] for c in range(3)]
        radius = jnp.sqrt(off[0] * off[0] + off[1] * off[1] + off[2] * off[2] + 0.25)
        inv = 1.0 / radius
        x = jnp.minimum(radius * 0.2, 1.0)
        x2 = x * x
        x3 = x2 * x
        x5 = x2 * x3
        u = 1.0 + x3 * x3 * (-28.0 + x * (48.0 - 21.0 * x))
        du = -168.0 * x5 * (1.0 - x) * (1.0 - x)
        du = jnp.where(radius < 5.0, du, 0.0)
        slot = piece * LANES + lax.broadcasted_iota(jnp.int32, (NEIGH, LANES), 1)
        live = (mine[3] >= 0.0) & (got[3] >= 0.0) & (index != slot)
        w = jnp.where(live, u, 0.0)
        items = [w, off[0] * inv, off[1] * inv, off[2] * inv, x, u, du, inv, got[3],
                 jnp.where(radius < 5.0, 0.2, 0.0), jnp.where(live, du, 0.0)]
        for c, item in enumerate(items):
            geo[b, c, :, lanes] = item

    def row(b, c, k):
        return geo[b, c, pl.ds(k, 1), :]

    @pl.loop(0, blocks)
    def _(b):
        start = pl.multiple_of(b * WIDE, WIDE)
        eight = lax.broadcasted_iota(jnp.int32, (8, WIDE), 0).astype(F32)
        my_kind = own[3:4, pl.ds(start, WIDE)]
        kind_hot[...] = (jnp.broadcast_to(my_kind, (8, WIDE)) == eight).astype(F32)
        order = (eight + 1.0) * math.pi
        for ref in (dens0, dens1, ddens0, ddens1, summary, centre_acc, energy_acc):
            ref[...] = jnp.zeros_like(ref)

        def harmonics(k):
            return row(b, 0, k), [row(b, 1 + m, k) for m in range(3)]

        @pl.loop(0, NEIGH, unroll=UNROLL)
        def _(k):
            w, ys = harmonics(k)
            x = row(b, 4, k)
            scale = row(b, 5, k) / x
            basis = jnp.sin(order * x) * scale
            hot = (jnp.broadcast_to(row(b, 8, k), (8, WIDE)) == eight).astype(F32)
            inputs = jnp.concatenate([basis, kind_hot[...], hot, jnp.zeros_like(hot)], axis=0)
            half = mm(w_in[...], inputs.astype(BF16))
            value, slope = silu_parts(half)
            latent = value.astype(BF16)
            lat0[k] = latent
            slope0[k] = slope.astype(BF16)
            result = mm(w_first[...], latent)
            amp[k] = result[:64]
            half0[k] = result[64:]
            env = result[32:64] * (w * 0.25)
            dens0[0] += env
            for m in range(3):
                dens0[m + 1] += env * ys[m]

        @pl.loop(0, NEIGH, unroll=UNROLL)
        def _(k):
            w, ys = harmonics(k)
            a = amp[k, 0:32]
            d = [dens0[m] for m in range(4)]
            inner = d[1] * ys[0] + d[2] * ys[1] + d[3] * ys[2]
            pieces = [a * d[0], a * inner] + [a * (d[m + 1] + ys[m] * d[0]) for m in range(3)]
            joined = jnp.concatenate(pieces, axis=0).astype(BF16)
            result = mm(w_mix[...], joined)
            tens[k] = result[256:]
            value, slope = silu_parts(half0[k] + result[:256])
            slope1[k] = slope.astype(BF16)
            latent = (lat0[k].astype(F32) + value).astype(BF16)
            lat1[k] = latent
            result = mm(w_second[...], latent)
            envl[k] = result[:32]
            half1[k] = result[32:]
            env = result[:32] * (w * 0.25)
            dens1[0] += env
            for m in range(3):
                dens1[m + 1] += env * ys[m]

        @pl.loop(0, NEIGH, unroll=UNROLL)
        def _(k):
            w, ys = harmonics(k)
            t = [tens[k, 32 * m:32 * m + 32] for m in range(4)]
            d = [dens1[m] for m in range(4)]
            joined = jnp.concatenate(
                [t[0] * d[0], t[1] * d[1] + t[2] * d[2] + t[3] * d[3]], axis=0).astype(BF16)
            value, slope = silu_parts(half1[k] + mm(w_third[...], joined))
            latent = (lat1[k].astype(F32) + value).astype(BF16).astype(F32)
            summary[...] += latent * w
            weigh = w_energy[...]
            edge = jnp.sum(latent * weigh, axis=0, keepdims=True)
            back[k, 0:1] = edge
            energy_acc[...] += jnp.broadcast_to(edge * w, (8, WIDE))
            dl2 = weigh * w
            result = mm(b_second[...], (dl2 * slope).astype(BF16))
            dlat[k] = dl2 + result[:256]
            dscal[k] = result[256:]
            ddens1[0] += result[256:288] * t[0]
            for m in range(3):
                ddens1[m + 1] += result[288:320] * t[m + 1]

        @pl.loop(0, NEIGH, unroll=UNROLL)
        def _(k):
            w, ys = harmonics(k)
            q = [ddens1[m] * 0.25 for m in range(4)]
            env = envl[k]
            total = q[0] + q[1] * ys[0] + q[2] * ys[1] + q[3] * ys[2]
            dw = jnp.sum(env * total, axis=0, keepdims=True)
            env = env * w
            dy = [env * q[m + 1] for m in range(3)]
            da, db = dscal[k, 0:32], dscal[k, 32:64]
            pieces = [total * w, da * dens1[0]] + [db * dens1[m + 1] for m in range(3)]
            mixed = mm(b_mix[...], jnp.concatenate(pieces, axis=0).astype(BF16))
            dl1 = dlat[k] + mixed[:256]
            result = mm(b_first[...], (dl1 * slope1[k].astype(F32)).astype(BF16))
            dlat[k] = dl1 + result[:256]
            da = result[256:288] + mixed[256:288]
            db = result[288:320] + mixed[288:320]
            dv = [mixed[320 + 32 * m:352 + 32 * m] for m in range(3)]
            a = amp[k, 0:32]
            d = [dens0[m] for m in range(4)]
            inner = d[1] * ys[0] + d[2] * ys[1] + d[3] * ys[2]
            damp[k] = da * d[0] + db * inner + sum(dv[m] * (d[m + 1] + ys[m] * d[0]) for m in range(3))
            ba = db * a
            va = [dv[m] * a for m in range(3)]
            ddens0[0] += da * a + va[0] * ys[0] + va[1] * ys[1] + va[2] * ys[2]
            for m in range(3):
                ddens0[m + 1] += ba * ys[m] + va[m]
                dy[m] += ba * d[m + 1] + va[m] * d[0]
            back[k, 0:1] += dw
            for m in range(3):
                back[k, m + 1:m + 2] = jnp.sum(dy[m], axis=0, keepdims=True)

        @pl.loop(0, NEIGH, unroll=UNROLL)
        def _(k):
            w, ys = harmonics(k)
            q = [ddens0[m] * 0.25 for m in range(4)]
            env = amp[k, 32:64]
            total = q[0] + q[1] * ys[0] + q[2] * ys[1] + q[3] * ys[2]
            dw = back[k, 0:1] + jnp.sum(env * total, axis=0, keepdims=True)
            env = env * w
            dy = [back[k, m + 1:m + 2] + jnp.sum(env * q[m + 1], axis=0, keepdims=True) for m in range(3)]
            joined = jnp.concatenate([damp[k], total * w], axis=0).astype(BF16)
            dl0 = dlat[k] + mm(b_amp[...], joined)
            dbasis = mm(b_in[...], (dl0 * slope0[k].astype(F32)).astype(BF16))[:8]
            x, u, du, inv = row(b, 4, k), row(b, 5, k), row(b, 6, k), row(b, 7, k)
            ix = 1.0 / x
            angle = order * x
            slope = jnp.cos(angle) * order * (u * ix) + jnp.sin(angle) * ((du - u * ix) * ix)
            dx = jnp.sum(dbasis * slope, axis=0, keepdims=True) + dw * row(b, 10, k)
            dr = dx * row(b, 9, k)
            along = (ys[0] * dy[0] + ys[1] * dy[1] + ys[2] * dy[2]) * inv
            force = [ys[m] * (dr - along) + dy[m] * inv for m in range(3)]
            centre_acc[...] += jnp.concatenate(force + [jnp.zeros((5, WIDE), F32)], axis=0)
            index = near[pl.ds(k, 1), pl.ds(start, WIDE)]
            low = jnp.bitwise_and(index, LANES - 1)
            high = jnp.right_shift(index, 7)
            picker = (lax.broadcasted_iota(jnp.int32, (LANES, WIDE), 0) == low).astype(F32).astype(BF16)
            places = lax.broadcasted_iota(jnp.int32, (16, WIDE), 0) == high
            spread = [jnp.where(places, f, 0.0) for f in force]
            spread = jnp.concatenate(spread, axis=0)
            top = spread.astype(BF16)
            rest = (spread - top.astype(F32)).astype(BF16)
            both = jnp.concatenate([top, rest], axis=0)
            ghost_acc[...] += lax.dot_general(
                both, picker, (((1,), (1,)), ((), ())), preferred_element_type=F32)

        lanes = pl.ds(start, WIDE)
        grad_out[:, lanes] = -centre_acc[...]
        energy_out[:, lanes] = energy_acc[...]
        feature_out[0:256, lanes] = summary[...] * 0.25
        for m in range(4):
            feature_out[256 + 32 * m:288 + 32 * m, lanes] = dens1[m]

    grad_out[:, slots:] = jnp.zeros_like(grad_out[:, slots:])
    for c in range(3):
        for h in range(sub):
            lanes = slice(h * LANES, (h + 1) * LANES)
            grad_out[c:c + 1, lanes] += (
                ghost_acc[16 * c + h:16 * c + h + 1] + ghost_acc[48 + 16 * c + h:49 + 16 * c + h])


def evaluate(ext, near, embed_weight, tensor_weight, env_weight, scalar_mix, vector_mix, latent_weight, energy_weight):
    slots = near.shape[1]
    blocks = slots // WIDE
    v = lambda shape, dtype=F32: pltpu.VMEM(shape, dtype)
    scratch = [
        v((256, 32), BF16), v((320, 256), BF16), v((384, 160), BF16), v((288, 256), BF16), v((256, 64), BF16),
        v((256, WIDE)), v((320, 256), BF16), v((416, 160), BF16), v((320, 256), BF16), v((256, 64), BF16),
        v((16, 256), BF16), v((256, 128)),
        v((blocks, 11, NEIGH, WIDE)), v((8, WIDE)),
        v((NEIGH, 256, WIDE), BF16), v((NEIGH, 256, WIDE), BF16), v((NEIGH, 256, WIDE)),
        v((NEIGH, 64, WIDE)), v((NEIGH, 128, WIDE)), v((NEIGH, 32, WIDE)),
        v((NEIGH, 256, WIDE), BF16), v((NEIGH, 256, WIDE), BF16), v((NEIGH, 256, WIDE)),
        v((NEIGH, 256, WIDE)), v((NEIGH, 64, WIDE)), v((NEIGH, 32, WIDE)), v((NEIGH, 8, WIDE)),
        v((4, 32, WIDE)), v((4, 32, WIDE)), v((4, 32, WIDE)), v((4, 32, WIDE)),
        v((256, WIDE)), v((96, LANES)), v((8, WIDE)), v((8, WIDE)),
    ]
    return pl.pallas_call(
        force_kernel,
        out_shape=(
            jax.ShapeDtypeStruct(ext.shape, F32),
            jax.ShapeDtypeStruct((8, slots), F32),
            jax.ShapeDtypeStruct((384, slots), F32),
        ),
        in_specs=[pl.BlockSpec(memory_space=pltpu.VMEM)] * 9,
        out_specs=[pl.BlockSpec(memory_space=pltpu.VMEM)] * 3,
        scratch_shapes=scratch,
        compiler_params=pltpu.CompilerParams(vmem_limit_bytes=56 * 1024 * 1024),
    )(ext, near, embed_weight, tensor_weight, env_weight, scalar_mix, vector_mix, latent_weight, energy_weight[None])


MESH = pl.DeviceIdType.MESH
EXACT_PARTS = 3


def parts_of(value, count):
    found = []
    for _ in range(count):
        piece = value.astype(BF16)
        found.append(piece)
        value = value - piece.astype(F32)
    return found


def tn(a, b):
    return lax.dot_general(a, b, (((0,), (0,)), ((), ())), preferred_element_type=F32)


def nt(a, b):
    return lax.dot_general(a, b, (((1,), (1,)), ((), ())), preferred_element_type=F32)


def partners():
    slab, dom = lax.axis_index("slab"), lax.axis_index("dom")
    slabs, doms = lax.axis_size("slab"), lax.axis_size("dom")
    linear = slab * doms + dom
    after = lax.rem(linear + 1, slabs * doms)
    before = lax.rem(linear + slabs * doms - 1, slabs * doms)
    split = lambda index: (index // doms, lax.rem(index, doms))
    return slab, dom, doms, split(before), split(after)


def greet(slab, dom, doms, before, after):
    barrier = pltpu.get_barrier_semaphore()

    @pl.loop(1, doms)
    def _(step):
        pl.semaphore_signal(
            barrier, inc=1, device_id=(slab, lax.rem(dom + step, doms)), device_id_type=MESH)

    for other in (before, after):
        pl.semaphore_signal(barrier, inc=1, device_id=other, device_id_type=MESH)
    return barrier


def send(source, target, send_sem, recv_sem, device):
    copy = pltpu.make_async_remote_copy(
        src_ref=source, dst_ref=target, send_sem=send_sem, recv_sem=recv_sem,
        device_id=device, device_id_type=MESH)
    copy.start()
    return copy


def reordered(slot):
    source = jnp.right_shift(slot * 43691, 19)
    return (slot - 12 * source) * 64 + source


def front_kernel(
    positions, species, domain, neighbours, ghost_lists,
    ext_out, near_out, code_out, lists_out,
    outbox, inbox, square, lend, arrive, box_send, box_recv, ghost_send, ghost_recv,
):
    slab, dom, doms, before, after = partners()
    barrier = greet(slab, dom, doms, before, after)
    atoms = positions.shape[1]
    slots = neighbours.shape[1]
    ghosts = ghost_lists.shape[1]

    target = domain[...]
    hot = (lax.broadcasted_iota(jnp.int32, (atoms, doms), 1) == target).astype(F32)
    hot16 = hot.astype(BF16)
    lower = (lax.broadcasted_iota(jnp.int32, (atoms, atoms), 0)
             > lax.broadcasted_iota(jnp.int32, (atoms, atoms), 1)).astype(F32).astype(BF16)
    rank = jnp.sum(hot * mm(lower, hot16), axis=1, keepdims=True)
    values = jnp.concatenate(
        [positions[...], species[...].astype(F32) + 1.0, jnp.zeros((4, atoms), F32)], axis=0).T
    lane = lax.broadcasted_iota(jnp.int32, (atoms, LANES), 1)
    lane_rank = jnp.bitwise_and(lane, 15).astype(F32)
    lane_comp = jnp.right_shift(lane, 4)
    packed = jnp.zeros((atoms, LANES), F32)
    for c in range(4):
        packed = jnp.where((lane_comp == c) & (lane_rank == rank), values[:, c:c + 1], packed)
    message = sum(tn(hot16, piece) for piece in parts_of(packed, EXACT_PARTS))
    for d in range(64):
        outbox[d] = message[d:d + 1]
    inbox[dom] = outbox[dom]

    pl.semaphore_wait(barrier, doms + 1)

    @pl.loop(1, doms)
    def _(step):
        other = lax.rem(dom + step, doms)
        send(outbox.at[other], inbox.at[dom], box_send, box_recv, (slab, other))

    code = jnp.where(lane == 0, target.astype(F32), jnp.where(lane == 1, rank, 0.0))
    code_out[...] = code.T[:8]
    index = neighbours[...]
    pieces = jnp.concatenate(
        [jnp.right_shift(index, 7).astype(F32), jnp.bitwise_and(index, LANES - 1).astype(F32)], axis=0)
    place = lax.broadcasted_iota(jnp.int32, (slots, slots), 1)
    place = jnp.bitwise_and(place, 63) * 12 + jnp.right_shift(place, 6)
    mover = (lax.broadcasted_iota(jnp.int32, (slots, slots), 0) == place).astype(F32).astype(BF16)
    moved = mm(pieces.astype(BF16), mover).astype(jnp.int32)
    index = moved[:16] * LANES + moved[16:]
    near_out[...] = jnp.where(index < slots, reordered(index), index)
    lists = reordered(ghost_lists[...])
    lists_out[...] = lists
    rows = lax.broadcasted_iota(jnp.int32, (slots, ghosts), 0)
    picks = [(rows == lists[i:i + 1]).astype(F32).astype(BF16) for i in range(2)]

    arrived = pltpu.make_async_copy(inbox.at[pl.ds(0, 63)], inbox.at[pl.ds(0, 63)], box_recv)
    arrived.wait()
    square[...] = jnp.zeros_like(square)
    for s in range(64):
        square[s:s + 1] = inbox[s]
    turned = square[...].T
    rolled = pltpu.roll(turned, 64, 1)
    first = lax.broadcasted_iota(jnp.int32, (1, LANES), 1) < 64
    ext_out[4:8, 0:slots] = jnp.zeros((4, slots), F32)
    for c in range(4):
        for p in range(slots // LANES):
            even = turned[16 * c + 2 * p:16 * c + 2 * p + 1]
            odd = rolled[16 * c + 2 * p + 1:16 * c + 2 * p + 2]
            both = jnp.where(first, even, odd)
            ext_out[c:c + 1, p * LANES:(p + 1) * LANES] = both - 1.0 if c == 3 else both
    own = parts_of(ext_out[:, 0:slots], EXACT_PARTS)
    copies = []
    for i, other in ((0, before), (1, after)):
        lend[i] = sum(mm(piece, picks[i]) for piece in own)
        copies.append(send(lend.at[i], arrive.at[i], ghost_send.at[i], ghost_recv.at[i], other))
    pltpu.make_async_copy(outbox.at[pl.ds(0, 63)], outbox.at[pl.ds(0, 63)], box_send).wait()
    for copy in copies:
        copy.wait()
    ext_out[:, slots:slots + ghosts] = arrive[1]
    ext_out[:, slots + ghosts:] = arrive[0]


def front(positions, species, domain, neighbours, ghost_lists):
    slots, ghosts, atoms = neighbours.shape[1], ghost_lists.shape[1], positions.shape[1]
    v = lambda shape, dtype=F32: pltpu.VMEM(shape, dtype)
    dma = pltpu.SemaphoreType.DMA
    return pl.pallas_call(
        front_kernel,
        out_shape=(
            jax.ShapeDtypeStruct((8, 2 * slots), F32),
            jax.ShapeDtypeStruct((NEIGH, slots), jnp.int32),
            jax.ShapeDtypeStruct((8, atoms), F32),
            jax.ShapeDtypeStruct((2, ghosts), jnp.int32),
        ),
        in_specs=[pl.BlockSpec(memory_space=pltpu.VMEM)] * 5,
        out_specs=[pl.BlockSpec(memory_space=pltpu.VMEM)] * 4,
        scratch_shapes=[
            v((64, 1, LANES)), v((64, 1, LANES)), v((LANES, LANES)), v((2, 8, ghosts)), v((2, 8, ghosts)),
            dma, dma, dma((2,)), dma((2,)),
        ],
        compiler_params=pltpu.CompilerParams(
            collective_id=0, has_side_effects=True, vmem_limit_bytes=32 * 1024 * 1024),
    )(positions, species[None], domain, neighbours, ghost_lists)


ROWS = 40


def home_kernel(
    grad, energy, features, code, lists,
    force_out, energy_out, feature_out,
    outbox, inbox, back, square, box_send, box_recv, ghost_send, ghost_recv,
):
    slab, dom, doms, before, after = partners()
    barrier = greet(slab, dom, doms, before, after)
    slots, ghosts = energy.shape[1], lists.shape[1]
    atoms = code.shape[1]
    pl.semaphore_wait(barrier, doms + 1)
    copies = [
        send(grad.at[:, pl.ds(slots, ghosts)], back.at[0], ghost_send.at[0], ghost_recv.at[0], before),
        send(grad.at[:, pl.ds(slots + ghosts, ghosts)], back.at[1], ghost_send.at[1], ghost_recv.at[1], after),
    ]
    for p in range(slots // LANES):
        turned = features[:, p * LANES:(p + 1) * LANES].T
        for i in range(LANES // 8):
            place = p * LANES + 8 * i
            r, d = place // 64, place % 64
            for t in range(3):
                outbox[pl.ds(ROWS * d + 3 * r + t, 8, stride=ROWS), :] = (
                    turned[8 * i:8 * i + 8, t * LANES:(t + 1) * LANES])
    for copy in copies:
        copy.wait()
    columns = lax.broadcasted_iota(jnp.int32, (slots, ghosts), 0)
    total = grad[:, 0:slots]
    for i in range(2):
        hot = (columns == lists[1 - i:2 - i]).astype(F32).astype(BF16)
        total = total + sum(nt(piece, hot) for piece in parts_of(back[i], 2))
    square[...] = jnp.zeros_like(square)
    rows = [-total[c:c + 1] for c in range(3)] + [energy[0:1]]
    for c in range(4):
        for p in range(slots // LANES):
            piece = rows[c][:, p * LANES:(p + 1) * LANES]
            square[16 * c + 2 * p:16 * c + 2 * p + 1] = piece
            square[16 * c + 2 * p + 1:16 * c + 2 * p + 2] = pltpu.roll(piece, 64, 1)
    turned = square[...].T
    for i in range(8):
        outbox[pl.ds(ROWS * 8 * i + 36, 8, stride=ROWS), :] = turned[8 * i:8 * i + 8]
        for t in range(37, ROWS):
            outbox[pl.ds(ROWS * 8 * i + t, 8, stride=ROWS), :] = jnp.zeros((8, LANES), F32)

    @pl.loop(1, doms)
    def _(step):
        other = lax.rem(dom + step, doms)
        send(outbox.at[pl.ds(pl.multiple_of(other * ROWS, 8), ROWS)],
             inbox.at[pl.ds(pl.multiple_of(dom * ROWS, 8), ROWS)], box_send, box_recv, (slab, other))

    mine = pl.ds(pl.multiple_of(dom * ROWS, 8), ROWS)
    inbox[mine] = outbox[mine]
    target, rank = code[0:1], code[1:2]
    hot = (lax.broadcasted_iota(jnp.int32, (64, atoms), 0).astype(F32) == target).astype(F32)
    hots = jnp.concatenate([jnp.where(rank == float(r), hot, 0.0).astype(BF16) for r in range(12)], axis=0)
    most = pl.ds(0, 63 * ROWS)
    pltpu.make_async_copy(inbox.at[most], inbox.at[most], box_recv).wait()
    pltpu.make_async_copy(outbox.at[most], outbox.at[most], box_send).wait()
    for t in range(3):
        found = jnp.concatenate([inbox[pl.ds(3 * r + t, 64, stride=ROWS), :] for r in range(12)], axis=0)
        feature_out[t * LANES:(t + 1) * LANES] = sum(tn(piece, hots) for piece in parts_of(found, 2))
    found = inbox[pl.ds(36, 64, stride=ROWS), :]
    picked = sum(tn(piece, hot.astype(BF16)) for piece in parts_of(found, 2))
    right = (lax.broadcasted_iota(jnp.int32, (16, atoms), 0).astype(F32) == rank).astype(F32)
    result = [jnp.sum(picked[16 * c:16 * c + 16] * right, axis=0, keepdims=True) for c in range(4)]
    for c in range(3):
        force_out[c:c + 1] = result[c]
    energy_out[...] = result[3]


def home(grad, energy, features, code, lists):
    atoms, ghosts = code.shape[1], lists.shape[1]
    v = lambda shape, dtype=F32: pltpu.VMEM(shape, dtype)
    dma = pltpu.SemaphoreType.DMA
    return pl.pallas_call(
        home_kernel,
        out_shape=(
            jax.ShapeDtypeStruct((3, atoms), F32),
            jax.ShapeDtypeStruct((1, atoms), F32),
            jax.ShapeDtypeStruct((384, atoms), F32),
        ),
        in_specs=[pl.BlockSpec(memory_space=pltpu.VMEM)] * 5,
        out_specs=[pl.BlockSpec(memory_space=pltpu.VMEM)] * 3,
        scratch_shapes=[
            v((64 * ROWS, LANES)), v((64 * ROWS, LANES)), v((2, 8, ghosts)), v((LANES, LANES)),
            dma, dma, dma((2,)), dma((2,)),
        ],
        compiler_params=pltpu.CompilerParams(
            collective_id=1, has_side_effects=True, vmem_limit_bytes=32 * 1024 * 1024),
    )(grad, energy, features, code, lists)


def local(
    positions, species, domain, neighbours, ghost_lists,
    embed_weight, tensor_weight, env_weight, scalar_mix, vector_mix, latent_weight, energy_weight,
):
    ext, near, code, lists = front(positions, species, domain, neighbours, ghost_lists)
    grad, energy, features = evaluate(
        ext, near, embed_weight, tensor_weight, env_weight, scalar_mix, vector_mix, latent_weight, energy_weight)
    forces, atom_energy, atom_features = home(grad, energy, features, code, lists)
    return forces, atom_energy[0], atom_features


def solution(mesh):
    both = ("slab", "dom")
    in_specs = (P(None, both), P(both), P(both, None), P(None, both), P(None, both)) + (P(),) * 7
    out_specs = (P(None, both), P(both), P(None, both))
    return jax.shard_map(local, mesh=mesh, in_specs=in_specs, out_specs=out_specs, check_vma=False)
```

```python
import math

import jax
import jax.numpy as jnp
from jax import lax
from jax.experimental import pallas as pl
from jax.experimental.pallas import tpu as pltpu
from jax.sharding import PartitionSpec as P

F32 = jnp.float32
BF16 = jnp.bfloat16
LANES = 128
WIDE = 256
NEIGH = 16
UNROLL = 4
MESH = pl.DeviceIdType.MESH
EXACT_PARTS = 3
RANKS = 12
EARLY = 24
LATE = 16


def mm(a, b):
    return jnp.dot(a, b, preferred_element_type=F32)


def silu_parts(half):
    gate = jnp.tanh(half)
    rise = 1.0 + gate
    value = half * rise
    slope = rise + value * (1.0 - gate)
    return value, slope


def parts_of(value, count):
    found = []
    for _ in range(count):
        piece = value.astype(BF16)
        found.append(piece)
        value = value - piece.astype(F32)
    return found


def tn(a, b):
    return lax.dot_general(a, b, (((0,), (0,)), ((), ())), preferred_element_type=F32)


def nt(a, b):
    return lax.dot_general(a, b, (((1,), (1,)), ((), ())), preferred_element_type=F32)


def partners():
    slab, dom = lax.axis_index("slab"), lax.axis_index("dom")
    slabs, doms = lax.axis_size("slab"), lax.axis_size("dom")
    linear = slab * doms + dom
    after = lax.rem(linear + 1, slabs * doms)
    before = lax.rem(linear + slabs * doms - 1, slabs * doms)
    split = lambda index: (index // doms, lax.rem(index, doms))
    return slab, dom, doms, split(before), split(after)


def greet(slab, dom, doms, before, after):
    barrier = pltpu.get_barrier_semaphore()

    @pl.loop(1, doms)
    def _(step):
        pl.semaphore_signal(
            barrier, inc=1, device_id=(slab, lax.rem(dom + step, doms)), device_id_type=MESH)

    for other in (before, after):
        pl.semaphore_signal(barrier, inc=1, device_id=other, device_id_type=MESH)
    return barrier


def send(source, target, send_sem, recv_sem, device):
    copy = pltpu.make_async_remote_copy(
        src_ref=source, dst_ref=target, send_sem=send_sem, recv_sem=recv_sem,
        device_id=device, device_id_type=MESH)
    copy.start()
    return copy


def reordered(slot):
    source = jnp.right_shift(slot * 43691, 19)
    return (slot - 12 * source) * 64 + source


def arrange_weights(
    embed_weight, tensor_turned, env_turned, scalar_turned, vector_mix, latent_weight, energy_weight,
    w_in, w_first, w_mix, w_second, w_third, w_energy, b_second, b_mix, b_first, b_amp, b_in, stage,
):
    chan, width = tensor_turned.shape
    lat0, lat1 = latent_weight[0].astype(F32) * 0.5, latent_weight[1].astype(F32) * 0.5
    b_first[...] = lat0.astype(BF16)
    b_second[...] = lat1.astype(BF16)
    w_first[0:32] = tensor_turned[...]
    w_first[32:64] = env_turned[0]
    w_second[0:32] = env_turned[1]
    small = jnp.concatenate(
        [tensor_turned[...], env_turned[0], env_turned[1], jnp.zeros((chan, width), BF16)], axis=0)
    small = small.astype(F32).T.astype(BF16)
    b_amp[...] = small[:, :64]
    w_first[64:] = lat0[:width].T.astype(BF16)
    w_second[32:] = lat1[:width].T.astype(BF16)
    w_third[...] = lat1[width:].T.astype(BF16)
    embed = embed_weight[...].astype(F32) * 0.5
    b_in[...] = embed[:16].astype(BF16)
    w_in[...] = jnp.concatenate([embed, jnp.zeros((8, width), F32)], axis=0).T.astype(BF16)
    energy = jnp.broadcast_to(energy_weight[...].astype(F32).reshape(1, width), (8, width))
    w_energy[...] = energy.T[:, 0:1] + jnp.zeros((width, WIDE), F32)
    stage[...] = jnp.zeros_like(stage)
    stage[0:32, 0:32] = vector_mix[...]
    turned = stage[:, 0:LANES].T[0:32, 0:32]
    stage[0:32, 0:64] = scalar_turned[...]
    for m in range(3):
        stage[32 + 32 * m:64 + 32 * m, 64 + 32 * m:96 + 32 * m] = turned
    core = stage[...]
    b_mix[...] = jnp.zeros_like(b_mix)
    b_mix[0:width, 0:32] = small[:, 64:96]
    b_mix[width:, 32:] = core.T[0:160].astype(BF16)
    w_mix[...] = jnp.zeros_like(w_mix)
    w_mix[0:width, 0:64] = lat0[width:].T.astype(BF16)
    w_mix[width:] = core[:, 0:160].astype(BF16)


def whole_kernel(
    positions, species, domain, neighbours, ghost_lists,
    embed_weight, tensor_turned, env_turned, scalar_turned, vector_mix, latent_weight, energy_weight,
    force_out, energy_out, feature_out,
    outbox, inbox, square, lend, arrive, box_send, box_recv, ghost_send, ghost_recv,
    ext, near, picks, home_hot, home_hots, home_rank, flipped, grad, energies, back_in,
    early_out, early_in, late_out, late_in, force_box, force_in,
    early_send, early_recv, late_send, late_recv, force_send, force_recv, back_send, back_recv,
    w_in, w_first, w_mix, w_second, w_third, w_energy, b_second, b_mix, b_first, b_amp, b_in, stage,
    geo, kind_hot, lat0, slope0, half0, amp, tens, envl, lat1, slope1, half1, dlat, dscal, damp, back,
    dens0, dens1, ddens0, ddens1, summary, ghost_acc, centre_acc, energy_acc,
):
    slab, dom, doms, before, after = partners()
    barrier = greet(slab, dom, doms, before, after)
    atoms = positions.shape[1]
    slots = neighbours.shape[1]
    ghosts = ghost_lists.shape[1]

    spread = jnp.broadcast_to(domain[...].astype(F32), (8, atoms))
    target = spread.T[:, 0:1].astype(jnp.int32)
    hot = (lax.broadcasted_iota(jnp.int32, (atoms, doms), 1) == target).astype(F32)
    hot16 = hot.astype(BF16)
    lower = (lax.broadcasted_iota(jnp.int32, (atoms, atoms), 0)
             > lax.broadcasted_iota(jnp.int32, (atoms, atoms), 1)).astype(F32).astype(BF16)
    rank = jnp.sum(hot * mm(lower, hot16), axis=1, keepdims=True)
    values = jnp.concatenate(
        [positions[...], species[...].astype(F32).reshape(1, atoms) + 1.0, jnp.zeros((4, atoms), F32)], axis=0).T
    lane = lax.broadcasted_iota(jnp.int32, (atoms, LANES), 1)
    lane_rank = jnp.bitwise_and(lane, 15).astype(F32)
    lane_comp = jnp.right_shift(lane, 4)
    packed = jnp.zeros((atoms, LANES), F32)
    for c in range(4):
        packed = jnp.where((lane_comp == c) & (lane_rank == rank), values[:, c:c + 1], packed)
    message = sum(tn(hot16, piece) for piece in parts_of(packed, EXACT_PARTS))
    for d in range(64):
        outbox[d] = message[d:d + 1]
    inbox[dom] = outbox[dom]

    pl.semaphore_wait(barrier, doms + 1)

    @pl.loop(1, doms)
    def _(step):
        other = lax.rem(dom + step, doms)
        send(outbox.at[other], inbox.at[dom], box_send, box_recv, (slab, other))

    code = jnp.where(lane == 0, target.astype(F32), jnp.where(lane == 1, rank, 0.0))
    code = code.T
    target, rank = code[0:1], code[1:2]
    hot = (lax.broadcasted_iota(jnp.int32, (64, atoms), 0).astype(F32) == target).astype(F32)
    home_hot[...] = hot.astype(BF16)
    for r in range(RANKS):
        home_hots[64 * r:64 * r + 64] = jnp.where(rank == float(r), hot, 0.0).astype(BF16)
    home_rank[...] = (lax.broadcasted_iota(jnp.int32, (16, atoms), 0).astype(F32) == rank).astype(F32)
    arrange_weights(
        embed_weight, tensor_turned, env_turned, scalar_turned, vector_mix, latent_weight, energy_weight,
        w_in, w_first, w_mix, w_second, w_third, w_energy, b_second, b_mix, b_first, b_amp, b_in, stage)
    index = neighbours[...]
    pieces = jnp.concatenate(
        [jnp.right_shift(index, 7).astype(F32), jnp.bitwise_and(index, LANES - 1).astype(F32)], axis=0)
    place = lax.broadcasted_iota(jnp.int32, (slots, slots), 1)
    place = jnp.bitwise_and(place, 63) * 12 + jnp.right_shift(place, 6)
    mover = (lax.broadcasted_iota(jnp.int32, (slots, slots), 0) == place).astype(F32).astype(BF16)
    moved = mm(pieces.astype(BF16), mover).astype(jnp.int32)
    index = moved[:16] * LANES + moved[16:]
    near[...] = jnp.where(index < slots, reordered(index), index)
    lists = reordered(ghost_lists[...])
    rows = lax.broadcasted_iota(jnp.int32, (slots, ghosts), 0)
    for i in range(2):
        picks[i] = (rows == lists[i:i + 1]).astype(F32).astype(BF16)

    arrived = pltpu.make_async_copy(inbox.at[pl.ds(0, 63)], inbox.at[pl.ds(0, 63)], box_recv)
    arrived.wait()
    square[...] = jnp.zeros_like(square)
    for s in range(64):
        square[s:s + 1] = inbox[s]
    turned = square[...].T
    rolled = pltpu.roll(turned, 64, 1)
    first = lax.broadcasted_iota(jnp.int32, (1, LANES), 1) < 64
    ext[4:8, 0:slots] = jnp.zeros((4, slots), F32)
    for c in range(4):
        for p in range(slots // LANES):
            even = turned[16 * c + 2 * p:16 * c + 2 * p + 1]
            odd = rolled[16 * c + 2 * p + 1:16 * c + 2 * p + 2]
            both = jnp.where(first, even, odd)
            ext[c:c + 1, p * LANES:(p + 1) * LANES] = both - 1.0 if c == 3 else both
    own = parts_of(ext[:, 0:slots], EXACT_PARTS)
    copies = []
    for i, other in ((0, before), (1, after)):
        lend[i] = sum(mm(piece, picks[i]) for piece in own)
        copies.append(send(lend.at[i], arrive.at[i], ghost_send.at[i], ghost_recv.at[i], other))
    pltpu.make_async_copy(outbox.at[pl.ds(0, 63)], outbox.at[pl.ds(0, 63)], box_send).wait()
    for copy in copies:
        copy.wait()
    ext[:, slots:slots + ghosts] = arrive[1]
    ext[:, slots + ghosts:] = arrive[0]
    blocks = geo.shape[0]
    sub = ext.shape[1] // LANES
    own = ext
    ghost_acc[...] = jnp.zeros_like(ghost_acc)

    for piece in range(blocks * WIDE // LANES):
        b, half = piece // 2, piece % 2
        lanes = pl.ds(half * LANES, LANES)
        index = near[:, piece * LANES:(piece + 1) * LANES]
        low = jnp.bitwise_and(index, LANES - 1)
        high = jnp.right_shift(index, 7)
        got = []
        for comp in range(4):
            value = jnp.zeros((NEIGH, LANES), F32)
            for h in range(sub):
                row = jnp.broadcast_to(ext[comp:comp + 1, h * LANES:(h + 1) * LANES], (NEIGH, LANES))
                taken = jnp.take_along_axis(row, low, axis=1)
                value = jnp.where(high == h, taken, value)
            got.append(value)
        mine = [own[c:c + 1, piece * LANES:(piece + 1) * LANES] for c in range(4)]
        off = [got[c] - mine[c] for c in range(3)]
        radius = jnp.sqrt(off[0] * off[0] + off[1] * off[1] + off[2] * off[2] + 0.25)
        inv = 1.0 / radius
        x = jnp.minimum(radius * 0.2, 1.0)
        x2 = x * x
        x3 = x2 * x
        x5 = x2 * x3
        u = 1.0 + x3 * x3 * (-28.0 + x * (48.0 - 21.0 * x))
        du = -168.0 * x5 * (1.0 - x) * (1.0 - x)
        du = jnp.where(radius < 5.0, du, 0.0)
        slot = piece * LANES + lax.broadcasted_iota(jnp.int32, (NEIGH, LANES), 1)
        live = (mine[3] >= 0.0) & (got[3] >= 0.0) & (index != slot)
        w = jnp.where(live, u, 0.0)
        items = [w, off[0] * inv, off[1] * inv, off[2] * inv, x, u, du, inv, got[3],
                 jnp.where(radius < 5.0, 0.2, 0.0), jnp.where(live, du, 0.0)]
        for c, item in enumerate(items):
            geo[b, c, :, lanes] = item

    def row(b, c, k):
        return geo[b, c, pl.ds(k, 1), :]

    @pl.loop(0, blocks)
    def _(b):
        start = pl.multiple_of(b * WIDE, WIDE)
        eight = lax.broadcasted_iota(jnp.int32, (8, WIDE), 0).astype(F32)
        my_kind = own[3:4, pl.ds(start, WIDE)]
        kind_hot[...] = (jnp.broadcast_to(my_kind, (8, WIDE)) == eight).astype(F32)
        order = (eight + 1.0) * math.pi
        for ref in (dens0, dens1, ddens0, ddens1, summary, centre_acc, energy_acc):
            ref[...] = jnp.zeros_like(ref)

        def harmonics(k):
            return row(b, 0, k), [row(b, 1 + m, k) for m in range(3)]

        @pl.loop(0, NEIGH, unroll=UNROLL)
        def _(k):
            w, ys = harmonics(k)
            x = row(b, 4, k)
            scale = row(b, 5, k) / x
            basis = jnp.sin(order * x) * scale
            hot = (jnp.broadcast_to(row(b, 8, k), (8, WIDE)) == eight).astype(F32)
            inputs = jnp.concatenate([basis, kind_hot[...], hot, jnp.zeros_like(hot)], axis=0)
            half = mm(w_in[...], inputs.astype(BF16))
            value, slope = silu_parts(half)
            latent = value.astype(BF16)
            lat0[k] = latent
            slope0[k] = slope.astype(BF16)
            result = mm(w_first[...], latent)
            amp[k] = result[:64]
            half0[k] = result[64:]
            env = result[32:64] * (w * 0.25)
            dens0[0] += env
            for m in range(3):
                dens0[m + 1] += env * ys[m]

        @pl.loop(0, NEIGH, unroll=UNROLL)
        def _(k):
            w, ys = harmonics(k)
            a = amp[k, 0:32]
            d = [dens0[m] for m in range(4)]
            inner = d[1] * ys[0] + d[2] * ys[1] + d[3] * ys[2]
            pieces = [a * d[0], a * inner] + [a * (d[m + 1] + ys[m] * d[0]) for m in range(3)]
            joined = jnp.concatenate(pieces, axis=0).astype(BF16)
            result = mm(w_mix[...], joined)
            tens[k] = result[256:]
            value, slope = silu_parts(half0[k] + result[:256])
            slope1[k] = slope.astype(BF16)
            latent = (lat0[k].astype(F32) + value).astype(BF16)
            lat1[k] = latent
            result = mm(w_second[...], latent)
            envl[k] = result[:32]
            half1[k] = result[32:]
            env = result[:32] * (w * 0.25)
            dens1[0] += env
            for m in range(3):
                dens1[m + 1] += env * ys[m]

        @pl.loop(0, NEIGH, unroll=UNROLL)
        def _(k):
            w, ys = harmonics(k)
            t = [tens[k, 32 * m:32 * m + 32] for m in range(4)]
            d = [dens1[m] for m in range(4)]
            joined = jnp.concatenate(
                [t[0] * d[0], t[1] * d[1] + t[2] * d[2] + t[3] * d[3]], axis=0).astype(BF16)
            value, slope = silu_parts(half1[k] + mm(w_third[...], joined))
            latent = (lat1[k].astype(F32) + value).astype(BF16).astype(F32)
            summary[...] += latent * w
            weigh = w_energy[...]
            edge = jnp.sum(latent * weigh, axis=0, keepdims=True)
            back[k, 0:1] = edge
            energy_acc[...] += jnp.broadcast_to(edge * w, (8, WIDE))
            dl2 = weigh * w
            result = mm(b_second[...], (dl2 * slope).astype(BF16))
            dlat[k] = dl2 + result[:256]
            dscal[k] = result[256:]
            ddens1[0] += result[256:288] * t[0]
            for m in range(3):
                ddens1[m + 1] += result[288:320] * t[m + 1]

        for p in range(WIDE // LANES):
            lanes = slice(p * LANES, (p + 1) * LANES)
            for half in range(2):
                flipped[lanes, half * LANES:(half + 1) * LANES] = (
                    summary[half * LANES:(half + 1) * LANES, lanes] * 0.25).T
            flipped[lanes, 2 * LANES:] = jnp.concatenate([dens1[m, :, lanes] for m in range(4)], axis=0).T

        def pack(box, rows, base):
            for r in range(4):
                for i in range(8):
                    for t in range(3):
                        box[pl.ds(base + rows * 8 * i + 3 * r + t, 8, stride=rows), :] = (
                            flipped[64 * r + 8 * i:64 * r + 8 * i + 8, t * LANES:(t + 1) * LANES])

        def post(box, target, rows, send_sem, recv_sem):
            @pl.loop(1, doms)
            def _(step):
                other = lax.rem(dom + step, doms)
                send(box.at[pl.ds(pl.multiple_of(other * rows, 8), rows)],
                     target.at[pl.ds(pl.multiple_of(dom * rows, 8), rows)], send_sem, recv_sem, (slab, other))

        @pl.when(b < 2)
        def _():
            pack(early_out, EARLY, b * 12)

        @pl.when(b == 1)
        def _():
            post(early_out, early_in, EARLY, early_send, early_recv)

        @pl.when(b == 2)
        def _():
            pack(late_out, LATE, 0)
            post(late_out, late_in, LATE, late_send, late_recv)

        @pl.loop(0, NEIGH, unroll=UNROLL)
        def _(k):
            w, ys = harmonics(k)
            q = [ddens1[m] * 0.25 for m in range(4)]
            env = envl[k]
            total = q[0] + q[1] * ys[0] + q[2] * ys[1] + q[3] * ys[2]
            dw = jnp.sum(env * total, axis=0, keepdims=True)
            env = env * w
            dy = [env * q[m + 1] for m in range(3)]
            da, db = dscal[k, 0:32], dscal[k, 32:64]
            pieces = [total * w, da * dens1[0]] + [db * dens1[m + 1] for m in range(3)]
            mixed = mm(b_mix[...], jnp.concatenate(pieces, axis=0).astype(BF16))
            dl1 = dlat[k] + mixed[:256]
            result = mm(b_first[...], (dl1 * slope1[k].astype(F32)).astype(BF16))
            dlat[k] = dl1 + result[:256]
            da = result[256:288] + mixed[256:288]
            db = result[288:320] + mixed[288:320]
            dv = [mixed[320 + 32 * m:352 + 32 * m] for m in range(3)]
            a = amp[k, 0:32]
            d = [dens0[m] for m in range(4)]
            inner = d[1] * ys[0] + d[2] * ys[1] + d[3] * ys[2]
            damp[k] = da * d[0] + db * inner + sum(dv[m] * (d[m + 1] + ys[m] * d[0]) for m in range(3))
            ba = db * a
            va = [dv[m] * a for m in range(3)]
            ddens0[0] += da * a + va[0] * ys[0] + va[1] * ys[1] + va[2] * ys[2]
            for m in range(3):
                ddens0[m + 1] += ba * ys[m] + va[m]
                dy[m] += ba * d[m + 1] + va[m] * d[0]
            back[k, 0:1] += dw
            for m in range(3):
                back[k, m + 1:m + 2] = jnp.sum(dy[m], axis=0, keepdims=True)

        @pl.loop(0, NEIGH, unroll=UNROLL)
        def _(k):
            w, ys = harmonics(k)
            q = [ddens0[m] * 0.25 for m in range(4)]
            env = amp[k, 32:64]
            total = q[0] + q[1] * ys[0] + q[2] * ys[1] + q[3] * ys[2]
            dw = back[k, 0:1] + jnp.sum(env * total, axis=0, keepdims=True)
            env = env * w
            dy = [back[k, m + 1:m + 2] + jnp.sum(env * q[m + 1], axis=0, keepdims=True) for m in range(3)]
            joined = jnp.concatenate([damp[k], total * w], axis=0).astype(BF16)
            dl0 = dlat[k] + mm(b_amp[...], joined)
            dbasis = mm(b_in[...], (dl0 * slope0[k].astype(F32)).astype(BF16))[:8]
            x, u, du, inv = row(b, 4, k), row(b, 5, k), row(b, 6, k), row(b, 7, k)
            ix = 1.0 / x
            angle = order * x
            slope = jnp.cos(angle) * order * (u * ix) + jnp.sin(angle) * ((du - u * ix) * ix)
            dx = jnp.sum(dbasis * slope, axis=0, keepdims=True) + dw * row(b, 10, k)
            dr = dx * row(b, 9, k)
            along = (ys[0] * dy[0] + ys[1] * dy[1] + ys[2] * dy[2]) * inv
            force = [ys[m] * (dr - along) + dy[m] * inv for m in range(3)]
            centre_acc[...] += jnp.concatenate(force + [jnp.zeros((5, WIDE), F32)], axis=0)
            index = near[pl.ds(k, 1), pl.ds(start, WIDE)]
            low = jnp.bitwise_and(index, LANES - 1)
            high = jnp.right_shift(index, 7)
            picker = (lax.broadcasted_iota(jnp.int32, (LANES, WIDE), 0) == low).astype(F32).astype(BF16)
            places = lax.broadcasted_iota(jnp.int32, (16, WIDE), 0) == high
            spread = [jnp.where(places, f, 0.0) for f in force]
            spread = jnp.concatenate(spread, axis=0)
            top = spread.astype(BF16)
            rest = (spread - top.astype(F32)).astype(BF16)
            both = jnp.concatenate([top, rest], axis=0)
            ghost_acc[...] += lax.dot_general(
                both, picker, (((1,), (1,)), ((), ())), preferred_element_type=F32)

        lanes = pl.ds(start, WIDE)
        grad[:, lanes] = -centre_acc[...]
        energies[:, lanes] = energy_acc[...]

    grad[:, slots:] = jnp.zeros_like(grad[:, slots:])
    for comp in range(3):
        for h in range(sub):
            lanes = slice(h * LANES, (h + 1) * LANES)
            grad[comp:comp + 1, lanes] += (
                ghost_acc[16 * comp + h:16 * comp + h + 1] + ghost_acc[48 + 16 * comp + h:49 + 16 * comp + h])
    copies = [
        send(grad.at[:, pl.ds(slots, ghosts)], back_in.at[0], back_send.at[0], back_recv.at[0], before),
        send(grad.at[:, pl.ds(slots + ghosts, ghosts)], back_in.at[1], back_send.at[1], back_recv.at[1], after),
    ]

    def settle(box, rows, sem):
        most = box.at[pl.ds(0, 63 * rows)]
        pltpu.make_async_copy(most, most, sem).wait()

    early_in[pl.ds(pl.multiple_of(dom * EARLY, 8), EARLY)] = early_out[pl.ds(pl.multiple_of(dom * EARLY, 8), EARLY)]
    late_in[pl.ds(pl.multiple_of(dom * LATE, 8), LATE)] = late_out[pl.ds(pl.multiple_of(dom * LATE, 8), LATE)]

    def select(box, rows, ranks, hots):
        found = []
        for t in range(3):
            value = jnp.concatenate([box[pl.ds(3 * r + t, 64, stride=rows), :] for r in range(ranks)], axis=0)
            found.append(sum(tn(piece, hots) for piece in parts_of(value, 2)))
        return found

    settle(early_in, EARLY, early_recv)
    for t, value in enumerate(select(early_in, EARLY, 8, home_hots[0:512])):
        feature_out[t * LANES:(t + 1) * LANES] = value

    for copy in copies:
        copy.wait()
    total = grad[:, 0:slots]
    for i in range(2):
        total = total + sum(nt(piece, picks[1 - i]) for piece in parts_of(back_in[i], 2))
    square[...] = jnp.zeros_like(square)
    rows = [-total[comp:comp + 1] for comp in range(3)] + [energies[0:1]]
    for comp in range(4):
        for p in range(slots // LANES):
            piece = rows[comp][:, p * LANES:(p + 1) * LANES]
            square[16 * comp + 2 * p:16 * comp + 2 * p + 1] = piece
            square[16 * comp + 2 * p + 1:16 * comp + 2 * p + 2] = pltpu.roll(piece, 64, 1)
    flat = square[...].T
    for d in range(64):
        force_box[d] = flat[d:d + 1]
    force_in[dom] = force_box[dom]

    @pl.loop(1, doms)
    def _(step):
        other = lax.rem(dom + step, doms)
        send(force_box.at[other], force_in.at[dom], force_send, force_recv, (slab, other))

    settle(late_in, LATE, late_recv)
    for t, value in enumerate(select(late_in, LATE, 4, home_hots[512:768])):
        feature_out[t * LANES:(t + 1) * LANES] += value
    settle(early_out, EARLY, early_send)
    settle(late_out, LATE, late_send)

    settle(force_in, 1, force_recv)
    for d in range(64):
        square[d:d + 1] = force_in[d]
    picked = sum(tn(piece, home_hot[...]) for piece in parts_of(square[0:64], 2))
    right = home_rank[...]
    result = [jnp.sum(picked[16 * comp:16 * comp + 16] * right, axis=0, keepdims=True) for comp in range(4)]
    for comp in range(3):
        force_out[comp:comp + 1] = result[comp]
    energy_out[...] = result[3].reshape(atoms)
    settle(force_box, 1, force_send)


def local(
    positions, species, domain, neighbours, ghost_lists,
    embed_weight, tensor_weight, env_weight, scalar_mix, vector_mix, latent_weight, energy_weight,
):
    slots, ghosts, atoms = neighbours.shape[1], ghost_lists.shape[1], positions.shape[1]
    blocks = slots // WIDE
    v = lambda shape, dtype=F32: pltpu.VMEM(shape, dtype)
    dma = pltpu.SemaphoreType.DMA
    scratch = [
        v((64, 1, LANES)), v((64, 1, LANES)), v((LANES, LANES)), v((2, 8, ghosts)), v((2, 8, ghosts)),
        dma, dma, dma((2,)), dma((2,)),
        v((8, 2 * slots)), v((NEIGH, slots), jnp.int32), v((2, slots, ghosts), BF16),
        v((64, atoms), BF16), v((slots, atoms), BF16), v((16, atoms)), v((WIDE, 384)),
        v((8, 2 * slots)), v((8, slots)), v((2, 8, ghosts)),
        v((64 * EARLY, LANES)), v((64 * EARLY, LANES)), v((64 * LATE, LANES)), v((64 * LATE, LANES)),
        v((64, 1, LANES)), v((64, 1, LANES)),
        dma, dma, dma, dma, dma, dma, dma((2,)), dma((2,)),
        v((256, 32), BF16), v((320, 256), BF16), v((384, 160), BF16), v((288, 256), BF16), v((256, 64), BF16),
        v((256, WIDE)), v((320, 256), BF16), v((416, 160), BF16), v((320, 256), BF16), v((256, 64), BF16),
        v((16, 256), BF16), v((128, 256)),
        v((blocks, 11, NEIGH, WIDE)), v((8, WIDE)),
        v((NEIGH, 256, WIDE), BF16), v((NEIGH, 256, WIDE), BF16), v((NEIGH, 256, WIDE)),
        v((NEIGH, 64, WIDE)), v((NEIGH, 128, WIDE)), v((NEIGH, 32, WIDE)),
        v((NEIGH, 256, WIDE), BF16), v((NEIGH, 256, WIDE), BF16), v((NEIGH, 256, WIDE)),
        v((NEIGH, 256, WIDE)), v((NEIGH, 64, WIDE)), v((NEIGH, 32, WIDE)), v((NEIGH, 8, WIDE)),
        v((4, 32, WIDE)), v((4, 32, WIDE)), v((4, 32, WIDE)), v((4, 32, WIDE)),
        v((256, WIDE)), v((96, LANES)), v((8, WIDE)), v((8, WIDE)),
    ]
    forces, atom_energy, atom_features = pl.pallas_call(
        whole_kernel,
        out_shape=(
            jax.ShapeDtypeStruct((3, atoms), F32),
            jax.ShapeDtypeStruct((atoms,), F32),
            jax.ShapeDtypeStruct((384, atoms), F32),
        ),
        in_specs=[pl.BlockSpec(memory_space=pltpu.VMEM)] * 12,
        out_specs=[pl.BlockSpec(memory_space=pltpu.VMEM)] * 3,
        scratch_shapes=scratch,
        compiler_params=pltpu.CompilerParams(
            collective_id=0, has_side_effects=True, vmem_limit_bytes=56 * 1024 * 1024),
    )(positions, species, domain.T, neighbours, ghost_lists, embed_weight, tensor_weight.T,
      env_weight.transpose(0, 2, 1), scalar_mix.T, vector_mix, latent_weight, energy_weight)
    return forces, atom_energy, atom_features


def solution(mesh):
    both = ("slab", "dom")
    in_specs = (P(None, both), P(both), P(both, None), P(None, both), P(None, both)) + (P(),) * 7
    out_specs = (P(None, both), P(both), P(None, both))
    return jax.shard_map(local, mesh=mesh, in_specs=in_specs, out_specs=out_specs, check_vma=False)
```

```python
import math

import jax
import jax.numpy as jnp
from jax import lax
from jax.experimental import pallas as pl
from jax.experimental.pallas import tpu as pltpu
from jax.sharding import PartitionSpec as P

F32 = jnp.float32
BF16 = jnp.bfloat16
LANES = 128
SINE = [(-1) ** i * math.pi ** (2 * i + 1) / math.factorial(2 * i + 1) for i in range(6)]
COSINE = [(-1) ** i * math.pi ** (2 * i) / math.factorial(2 * i) for i in range(7)]
WIDE = 256
NEIGH = 16
UNROLL = 2
TOGETHER = 4
SPAN = TOGETHER * WIDE
ROUNDS = NEIGH // TOGETHER
MESH = pl.DeviceIdType.MESH
EXACT_PARTS = 3
RANKS = 12
EARLY = 24
LATE = 16


def mm(a, b):
    return jnp.dot(a, b, preferred_element_type=F32)


def sine_parts(turns):
    whole = jnp.floor(turns + 0.5)
    part = turns - whole
    sign = 1.0 - 2.0 * (whole - 2.0 * jnp.floor(whole * 0.5))
    square = part * part
    sine = jnp.full_like(part, SINE[-1])
    for coefficient in SINE[-2::-1]:
        sine = sine * square + coefficient
    cosine = jnp.full_like(part, COSINE[-1])
    for coefficient in COSINE[-2::-1]:
        cosine = cosine * square + coefficient
    return sine * part * sign, cosine * sign


def silu_parts(half):
    half = half.astype(BF16)
    gate = jnp.tanh(half)
    rise = 1.0 + gate
    value = half * rise
    slope = rise + value * (1.0 - gate)
    return value, slope


def parts_of(value, count):
    found = []
    for _ in range(count):
        piece = value.astype(BF16)
        found.append(piece)
        value = value - piece.astype(F32)
    return found


def tn(a, b):
    return lax.dot_general(a, b, (((0,), (0,)), ((), ())), preferred_element_type=F32)


def nt(a, b):
    return lax.dot_general(a, b, (((1,), (1,)), ((), ())), preferred_element_type=F32)


def partners():
    slab, dom = lax.axis_index("slab"), lax.axis_index("dom")
    slabs, doms = lax.axis_size("slab"), lax.axis_size("dom")
    linear = slab * doms + dom
    after = lax.rem(linear + 1, slabs * doms)
    before = lax.rem(linear + slabs * doms - 1, slabs * doms)
    split = lambda index: (index // doms, lax.rem(index, doms))
    return slab, dom, doms, split(before), split(after)


def greet(slab, dom, doms, before, after):
    barrier = pltpu.get_barrier_semaphore()

    @pl.loop(1, doms)
    def _(step):
        pl.semaphore_signal(
            barrier, inc=1, device_id=(slab, lax.rem(dom + step, doms)), device_id_type=MESH)

    for other in (before, after):
        pl.semaphore_signal(barrier, inc=1, device_id=other, device_id_type=MESH)
    return barrier


def send(source, target, send_sem, recv_sem, device):
    copy = pltpu.make_async_remote_copy(
        src_ref=source, dst_ref=target, send_sem=send_sem, recv_sem=recv_sem,
        device_id=device, device_id_type=MESH)
    copy.start()
    return copy


def reordered(slot):
    source = jnp.right_shift(slot * 43691, 19)
    return (slot - 12 * source) * 64 + source


def arrange_weights(
    embed_weight, tensor_turned, env_turned, scalar_turned, vector_mix, latent_weight, energy_weight,
    w_in, w_first, w_mix, w_second, w_third, w_energy, b_second, b_mix, b_first, b_amp, b_in, stage,
):
    chan, width = tensor_turned.shape
    lat0, lat1 = latent_weight[0].astype(F32) * 0.5, latent_weight[1].astype(F32) * 0.5
    b_first[...] = lat0.astype(BF16)
    b_second[...] = lat1.astype(BF16)
    w_first[0:32] = tensor_turned[...]
    w_first[32:64] = env_turned[0]
    w_second[0:32] = env_turned[1]
    small = jnp.concatenate(
        [tensor_turned[...], env_turned[0], env_turned[1], jnp.zeros((chan, width), BF16)], axis=0)
    small = small.astype(F32).T.astype(BF16)
    b_amp[...] = small[:, :64]
    w_first[64:] = lat0[:width].T.astype(BF16)
    w_second[32:] = lat1[:width].T.astype(BF16)
    w_third[...] = lat1[width:].T.astype(BF16)
    embed = embed_weight[...].astype(F32) * 0.5
    b_in[...] = embed[:16].astype(BF16)
    w_in[...] = jnp.concatenate([embed, jnp.zeros((8, width), F32)], axis=0).T.astype(BF16)
    energy = jnp.broadcast_to(energy_weight[...].astype(F32).reshape(1, width), (8, width))
    w_energy[...] = energy.T[:, 0:1] + jnp.zeros((width, WIDE), F32)
    stage[...] = jnp.zeros_like(stage)
    stage[0:32, 0:32] = vector_mix[...]
    turned = stage[:, 0:LANES].T[0:32, 0:32]
    stage[0:32, 0:64] = scalar_turned[...]
    for m in range(3):
        stage[32 + 32 * m:64 + 32 * m, 64 + 32 * m:96 + 32 * m] = turned
    core = stage[...]
    b_mix[...] = jnp.zeros_like(b_mix)
    b_mix[0:width, 0:32] = small[:, 64:96]
    b_mix[width:, 32:] = core.T[0:160].astype(BF16)
    w_mix[...] = jnp.zeros_like(w_mix)
    w_mix[0:width, 0:64] = lat0[width:].T.astype(BF16)
    w_mix[width:] = core[:, 0:160].astype(BF16)


def whole_kernel(
    positions, species, domain, neighbours, ghost_lists,
    embed_weight, tensor_turned, env_turned, scalar_turned, vector_mix, latent_weight, energy_weight,
    force_out, energy_out, feature_out,
    outbox, inbox, square, lend, arrive, box_send, box_recv, ghost_send, ghost_recv,
    ext, near, picks, home_hot, home_hots, home_rank, flipped, grad, energies, back_in,
    early_out, early_in, late_out, late_in, force_box, force_in,
    early_send, early_recv, late_send, late_recv, force_send, force_recv, back_send, back_recv,
    w_in, w_first, w_mix, w_second, w_third, w_energy, b_second, b_mix, b_first, b_amp, b_in, stage,
    geo, kind_hot, lat0, slope0, half0, amp, tens, envl, lat1, slope1, half1, dlat, dscal, damp, back,
    dens0, dens1, ddens0, ddens1, summary, ghost_acc, centre_acc, energy_acc,
):
    slab, dom, doms, before, after = partners()
    barrier = greet(slab, dom, doms, before, after)
    atoms = positions.shape[1]
    slots = neighbours.shape[1]
    ghosts = ghost_lists.shape[1]

    spread = jnp.broadcast_to(domain[...].astype(F32), (8, atoms))
    target = spread.T[:, 0:1].astype(jnp.int32)
    hot = (lax.broadcasted_iota(jnp.int32, (atoms, doms), 1) == target).astype(F32)
    hot16 = hot.astype(BF16)
    lower = (lax.broadcasted_iota(jnp.int32, (atoms, atoms), 0)
             > lax.broadcasted_iota(jnp.int32, (atoms, atoms), 1)).astype(F32).astype(BF16)
    rank = jnp.sum(hot * mm(lower, hot16), axis=1, keepdims=True)
    values = jnp.concatenate(
        [positions[...], species[...].astype(F32).reshape(1, atoms) + 1.0, jnp.zeros((4, atoms), F32)], axis=0).T
    lane = lax.broadcasted_iota(jnp.int32, (atoms, LANES), 1)
    lane_rank = jnp.bitwise_and(lane, 15).astype(F32)
    lane_comp = jnp.right_shift(lane, 4)
    packed = jnp.zeros((atoms, LANES), F32)
    for c in range(4):
        packed = jnp.where((lane_comp == c) & (lane_rank == rank), values[:, c:c + 1], packed)
    message = sum(tn(hot16, piece) for piece in parts_of(packed, EXACT_PARTS))
    for d in range(64):
        outbox[d] = message[d:d + 1]
    inbox[dom] = outbox[dom]

    pl.semaphore_wait(barrier, doms + 1)

    @pl.loop(1, doms)
    def _(step):
        other = lax.rem(dom + step, doms)
        send(outbox.at[other], inbox.at[dom], box_send, box_recv, (slab, other))

    code = jnp.where(lane == 0, target.astype(F32), jnp.where(lane == 1, rank, 0.0))
    code = code.T
    target, rank = code[0:1], code[1:2]
    hot = (lax.broadcasted_iota(jnp.int32, (64, atoms), 0).astype(F32) == target).astype(F32)
    home_hot[...] = hot.astype(BF16)
    for r in range(RANKS):
        home_hots[64 * r:64 * r + 64] = jnp.where(rank == float(r), hot, 0.0).astype(BF16)
    home_rank[...] = (lax.broadcasted_iota(jnp.int32, (16, atoms), 0).astype(F32) == rank).astype(F32)
    arrange_weights(
        embed_weight, tensor_turned, env_turned, scalar_turned, vector_mix, latent_weight, energy_weight,
        w_in, w_first, w_mix, w_second, w_third, w_energy, b_second, b_mix, b_first, b_amp, b_in, stage)
    index = neighbours[...]
    pieces = jnp.concatenate(
        [jnp.right_shift(index, 7).astype(F32), jnp.bitwise_and(index, LANES - 1).astype(F32)], axis=0)
    place = lax.broadcasted_iota(jnp.int32, (slots, slots), 1)
    place = jnp.bitwise_and(place, 63) * 12 + jnp.right_shift(place, 6)
    mover = (lax.broadcasted_iota(jnp.int32, (slots, slots), 0) == place).astype(F32).astype(BF16)
    moved = mm(pieces.astype(BF16), mover).astype(jnp.int32)
    index = moved[:16] * LANES + moved[16:]
    near[...] = jnp.where(index < slots, reordered(index), index)
    lists = reordered(ghost_lists[...])
    rows = lax.broadcasted_iota(jnp.int32, (slots, ghosts), 0)
    for i in range(2):
        picks[i] = (rows == lists[i:i + 1]).astype(F32).astype(BF16)

    arrived = pltpu.make_async_copy(inbox.at[pl.ds(0, 63)], inbox.at[pl.ds(0, 63)], box_recv)
    arrived.wait()
    square[...] = jnp.zeros_like(square)
    for s in range(64):
        square[s:s + 1] = inbox[s]
    turned = square[...].T
    rolled = pltpu.roll(turned, 64, 1)
    first = lax.broadcasted_iota(jnp.int32, (1, LANES), 1) < 64
    ext[4:8, 0:slots] = jnp.zeros((4, slots), F32)
    for c in range(4):
        for p in range(slots // LANES):
            even = turned[16 * c + 2 * p:16 * c + 2 * p + 1]
            odd = rolled[16 * c + 2 * p + 1:16 * c + 2 * p + 2]
            both = jnp.where(first, even, odd)
            ext[c:c + 1, p * LANES:(p + 1) * LANES] = both - 1.0 if c == 3 else both
    own = parts_of(ext[:, 0:slots], EXACT_PARTS)
    copies = []
    for i, other in ((0, before), (1, after)):
        lend[i] = sum(mm(piece, picks[i]) for piece in own)
        copies.append(send(lend.at[i], arrive.at[i], ghost_send.at[i], ghost_recv.at[i], other))
    pltpu.make_async_copy(outbox.at[pl.ds(0, 63)], outbox.at[pl.ds(0, 63)], box_send).wait()
    for copy in copies:
        copy.wait()
    ext[:, slots:slots + ghosts] = arrive[1]
    ext[:, slots + ghosts:] = arrive[0]
    blocks = geo.shape[0]
    sub = ext.shape[1] // LANES
    own = ext
    ghost_acc[...] = jnp.zeros_like(ghost_acc)

    for piece in range(blocks * WIDE // LANES):
        b, half = piece // 2, piece % 2
        lanes = pl.ds(half * LANES, LANES)
        index = near[:, piece * LANES:(piece + 1) * LANES]
        low = jnp.bitwise_and(index, LANES - 1)
        high = jnp.right_shift(index, 7)
        got = []
        for comp in range(4):
            value = jnp.zeros((NEIGH, LANES), F32)
            for h in range(sub):
                row = jnp.broadcast_to(ext[comp:comp + 1, h * LANES:(h + 1) * LANES], (NEIGH, LANES))
                taken = jnp.take_along_axis(row, low, axis=1)
                value = jnp.where(high == h, taken, value)
            got.append(value)
        mine = [own[c:c + 1, piece * LANES:(piece + 1) * LANES] for c in range(4)]
        off = [got[c] - mine[c] for c in range(3)]
        radius = jnp.sqrt(off[0] * off[0] + off[1] * off[1] + off[2] * off[2] + 0.25)
        inv = 1.0 / radius
        x = jnp.minimum(radius * 0.2, 1.0)
        x2 = x * x
        x3 = x2 * x
        x5 = x2 * x3
        u = 1.0 + x3 * x3 * (-28.0 + x * (48.0 - 21.0 * x))
        du = -168.0 * x5 * (1.0 - x) * (1.0 - x)
        du = jnp.where(radius < 5.0, du, 0.0)
        slot = piece * LANES + lax.broadcasted_iota(jnp.int32, (NEIGH, LANES), 1)
        live = (mine[3] >= 0.0) & (got[3] >= 0.0) & (index != slot)
        w = jnp.where(live, u, 0.0)
        items = [w, off[0] * inv, off[1] * inv, off[2] * inv, x, u, du, inv, got[3],
                 jnp.where(radius < 5.0, 0.2, 0.0), jnp.where(live, du, 0.0)]
        for c, item in enumerate(items):
            geo[b, c, :, lanes] = item

    def side_by_side(pieces):
        return jnp.concatenate(pieces, axis=1)

    def row(b, c, k):
        return side_by_side([geo[b, c, pl.ds(k * TOGETHER + i, 1), :] for i in range(TOGETHER)])

    def tiled(value):
        return side_by_side([value] * TOGETHER)

    def folded(value):
        return sum(value[:, i * WIDE:(i + 1) * WIDE] for i in range(TOGETHER))

    @pl.loop(0, blocks)
    def _(b):
        start = pl.multiple_of(b * WIDE, WIDE)
        eight = lax.broadcasted_iota(jnp.int32, (8, SPAN), 0).astype(F32)
        my_kind = tiled(own[3:4, pl.ds(start, WIDE)])
        kind_hot[...] = (jnp.broadcast_to(my_kind, (8, SPAN)) == eight).astype(F32)
        order = eight + 1.0
        for ref in (dens0, dens1, ddens0, ddens1, summary, centre_acc, energy_acc):
            ref[...] = jnp.zeros_like(ref)

        def harmonics(k):
            return row(b, 0, k), [row(b, 1 + m, k) for m in range(3)]

        @pl.loop(0, ROUNDS, unroll=UNROLL)
        def _(k):
            w, ys = harmonics(k)
            x = row(b, 4, k)
            scale = row(b, 5, k) / x
            basis = sine_parts(order * x)[0] * scale
            hot = (jnp.broadcast_to(row(b, 8, k), (8, SPAN)) == eight).astype(F32)
            inputs = jnp.concatenate([basis, kind_hot[...], hot, jnp.zeros_like(hot)], axis=0)
            half = mm(w_in[...], inputs.astype(BF16))
            value, slope = silu_parts(half)
            latent = value.astype(BF16)
            lat0[k] = latent
            slope0[k] = slope.astype(BF16)
            result = mm(w_first[...], latent)
            amp[k] = result[:64]
            half0[k] = result[64:].astype(BF16)
            env = result[32:64] * (w * 0.25)
            dens0[0] += folded(env)
            for m in range(3):
                dens0[m + 1] += folded(env * ys[m])

        @pl.loop(0, ROUNDS, unroll=UNROLL)
        def _(k):
            w, ys = harmonics(k)
            a = amp[k, 0:32]
            d = [tiled(dens0[m]) for m in range(4)]
            inner = d[1] * ys[0] + d[2] * ys[1] + d[3] * ys[2]
            pieces = [a * d[0], a * inner] + [a * (d[m + 1] + ys[m] * d[0]) for m in range(3)]
            joined = jnp.concatenate(pieces, axis=0).astype(BF16)
            result = mm(w_mix[...], joined)
            tens[k] = result[256:]
            value, slope = silu_parts(half0[k] + result[:256].astype(BF16))
            slope1[k] = slope.astype(BF16)
            latent = lat0[k] + value
            lat1[k] = latent
            result = mm(w_second[...], latent)
            envl[k] = result[:32]
            half1[k] = result[32:].astype(BF16)
            env = result[:32] * (w * 0.25)
            dens1[0] += folded(env)
            for m in range(3):
                dens1[m + 1] += folded(env * ys[m])

        @pl.loop(0, ROUNDS, unroll=UNROLL)
        def _(k):
            w, ys = harmonics(k)
            t = [tens[k, 32 * m:32 * m + 32] for m in range(4)]
            d = [tiled(dens1[m]) for m in range(4)]
            joined = jnp.concatenate(
                [t[0] * d[0], t[1] * d[1] + t[2] * d[2] + t[3] * d[3]], axis=0).astype(BF16)
            value, slope = silu_parts(half1[k] + mm(w_third[...], joined).astype(BF16))
            latent = (lat1[k] + value).astype(BF16).astype(F32)
            summary[...] += folded(latent * w)
            weigh = tiled(w_energy[...])
            edge = jnp.sum(latent * weigh, axis=0, keepdims=True)
            back[k, 0:1] = edge
            energy_acc[...] += jnp.broadcast_to(folded(edge * w), (8, WIDE))
            dl2 = (weigh * w).astype(BF16)
            result = mm(b_second[...], (dl2 * slope).astype(BF16))
            dlat[k] = dl2 + result[:256].astype(BF16)
            dscal[k] = result[256:]
            ddens1[0] += folded(result[256:288] * t[0])
            for m in range(3):
                ddens1[m + 1] += folded(result[288:320] * t[m + 1])

        for p in range(WIDE // LANES):
            lanes = slice(p * LANES, (p + 1) * LANES)
            for half in range(2):
                flipped[lanes, half * LANES:(half + 1) * LANES] = (
                    summary[half * LANES:(half + 1) * LANES, lanes] * 0.25).T
            flipped[lanes, 2 * LANES:] = jnp.concatenate([dens1[m, :, lanes] for m in range(4)], axis=0).T

        def pack(box, rows, base):
            for r in range(4):
                for i in range(8):
                    for t in range(3):
                        box[pl.ds(base + rows * 8 * i + 3 * r + t, 8, stride=rows), :] = (
                            flipped[64 * r + 8 * i:64 * r + 8 * i + 8, t * LANES:(t + 1) * LANES])

        def post(box, target, rows, send_sem, recv_sem):
            @pl.loop(1, doms)
            def _(step):
                other = lax.rem(dom + step, doms)
                send(box.at[pl.ds(pl.multiple_of(other * rows, 8), rows)],
                     target.at[pl.ds(pl.multiple_of(dom * rows, 8), rows)], send_sem, recv_sem, (slab, other))

        @pl.when(b < 2)
        def _():
            pack(early_out, EARLY, b * 12)

        @pl.when(b == 1)
        def _():
            post(early_out, early_in, EARLY, early_send, early_recv)

        @pl.when(b == 2)
        def _():
            pack(late_out, LATE, 0)
            post(late_out, late_in, LATE, late_send, late_recv)

        @pl.loop(0, ROUNDS, unroll=UNROLL)
        def _(k):
            w, ys = harmonics(k)
            q = [tiled(ddens1[m] * 0.25) for m in range(4)]
            env = envl[k]
            total = q[0] + q[1] * ys[0] + q[2] * ys[1] + q[3] * ys[2]
            dw = jnp.sum(env * total, axis=0, keepdims=True)
            env = env * w
            dy = [env * q[m + 1] for m in range(3)]
            da, db = dscal[k, 0:32], dscal[k, 32:64]
            pieces = [total * w, da * tiled(dens1[0])] + [db * tiled(dens1[m + 1]) for m in range(3)]
            mixed = mm(b_mix[...], jnp.concatenate(pieces, axis=0).astype(BF16))
            dl1 = dlat[k] + mixed[:256].astype(BF16)
            result = mm(b_first[...], (dl1 * slope1[k]))
            dlat[k] = dl1 + result[:256].astype(BF16)
            da = result[256:288] + mixed[256:288]
            db = result[288:320] + mixed[288:320]
            dv = [mixed[320 + 32 * m:352 + 32 * m] for m in range(3)]
            a = amp[k, 0:32]
            d = [tiled(dens0[m]) for m in range(4)]
            inner = d[1] * ys[0] + d[2] * ys[1] + d[3] * ys[2]
            damp[k] = da * d[0] + db * inner + sum(dv[m] * (d[m + 1] + ys[m] * d[0]) for m in range(3))
            ba = db * a
            va = [dv[m] * a for m in range(3)]
            ddens0[0] += folded(da * a + va[0] * ys[0] + va[1] * ys[1] + va[2] * ys[2])
            for m in range(3):
                ddens0[m + 1] += folded(ba * ys[m] + va[m])
                dy[m] += ba * d[m + 1] + va[m] * d[0]
            back[k, 0:1] += dw
            for m in range(3):
                back[k, m + 1:m + 2] = jnp.sum(dy[m], axis=0, keepdims=True)

        @pl.loop(0, ROUNDS, unroll=UNROLL)
        def _(k):
            w, ys = harmonics(k)
            q = [tiled(ddens0[m] * 0.25) for m in range(4)]
            env = amp[k, 32:64]
            total = q[0] + q[1] * ys[0] + q[2] * ys[1] + q[3] * ys[2]
            dw = back[k, 0:1] + jnp.sum(env * total, axis=0, keepdims=True)
            env = env * w
            dy = [back[k, m + 1:m + 2] + jnp.sum(env * q[m + 1], axis=0, keepdims=True) for m in range(3)]
            joined = jnp.concatenate([damp[k], total * w], axis=0).astype(BF16)
            dl0 = dlat[k] + mm(b_amp[...], joined).astype(BF16)
            dbasis = mm(b_in[...], (dl0 * slope0[k]))[:8]
            x, u, du, inv = row(b, 4, k), row(b, 5, k), row(b, 6, k), row(b, 7, k)
            ix = 1.0 / x
            sine, cosine = sine_parts(order * x)
            slope = cosine * order * (math.pi * u * ix) + sine * ((du - u * ix) * ix)
            dx = jnp.sum(dbasis * slope, axis=0, keepdims=True) + dw * row(b, 10, k)
            dr = dx * row(b, 9, k)
            along = (ys[0] * dy[0] + ys[1] * dy[1] + ys[2] * dy[2]) * inv
            force = [ys[m] * (dr - along) + dy[m] * inv for m in range(3)]
            centre_acc[...] += folded(jnp.concatenate(force + [jnp.zeros((5, SPAN), F32)], axis=0))
            index = side_by_side(
                [near[pl.ds(k * TOGETHER + i, 1), pl.ds(start, WIDE)] for i in range(TOGETHER)])
            low = jnp.bitwise_and(index, LANES - 1)
            high = jnp.right_shift(index, 7)
            picker = (lax.broadcasted_iota(jnp.int32, (LANES, SPAN), 0) == low).astype(F32).astype(BF16)
            places = lax.broadcasted_iota(jnp.int32, (16, SPAN), 0) == high
            spread = [jnp.where(places, f, 0.0) for f in force]
            spread = jnp.concatenate(spread, axis=0)
            top = spread.astype(BF16)
            rest = (spread - top.astype(F32)).astype(BF16)
            both = jnp.concatenate([top, rest], axis=0)
            ghost_acc[...] += lax.dot_general(
                both, picker, (((1,), (1,)), ((), ())), preferred_element_type=F32)

        lanes = pl.ds(start, WIDE)
        grad[:, lanes] = -centre_acc[...]
        energies[:, lanes] = energy_acc[...]

    grad[:, slots:] = jnp.zeros_like(grad[:, slots:])
    for comp in range(3):
        for h in range(sub):
            lanes = slice(h * LANES, (h + 1) * LANES)
            grad[comp:comp + 1, lanes] += (
                ghost_acc[16 * comp + h:16 * comp + h + 1] + ghost_acc[48 + 16 * comp + h:49 + 16 * comp + h])
    copies = [
        send(grad.at[:, pl.ds(slots, ghosts)], back_in.at[0], back_send.at[0], back_recv.at[0], before),
        send(grad.at[:, pl.ds(slots + ghosts, ghosts)], back_in.at[1], back_send.at[1], back_recv.at[1], after),
    ]

    def settle(box, rows, sem):
        most = box.at[pl.ds(0, 63 * rows)]
        pltpu.make_async_copy(most, most, sem).wait()

    early_in[pl.ds(pl.multiple_of(dom * EARLY, 8), EARLY)] = early_out[pl.ds(pl.multiple_of(dom * EARLY, 8), EARLY)]
    late_in[pl.ds(pl.multiple_of(dom * LATE, 8), LATE)] = late_out[pl.ds(pl.multiple_of(dom * LATE, 8), LATE)]

    def select(box, rows, ranks, hots):
        found = []
        for t in range(3):
            value = jnp.concatenate([box[pl.ds(3 * r + t, 64, stride=rows), :] for r in range(ranks)], axis=0)
            found.append(sum(tn(piece, hots) for piece in parts_of(value, 2)))
        return found

    settle(early_in, EARLY, early_recv)
    for t, value in enumerate(select(early_in, EARLY, 8, home_hots[0:512])):
        feature_out[t * LANES:(t + 1) * LANES] = value

    for copy in copies:
        copy.wait()
    total = grad[:, 0:slots]
    for i in range(2):
        total = total + sum(nt(piece, picks[1 - i]) for piece in parts_of(back_in[i], 2))
    square[...] = jnp.zeros_like(square)
    rows = [-total[comp:comp + 1] for comp in range(3)] + [energies[0:1]]
    for comp in range(4):
        for p in range(slots // LANES):
            piece = rows[comp][:, p * LANES:(p + 1) * LANES]
            square[16 * comp + 2 * p:16 * comp + 2 * p + 1] = piece
            square[16 * comp + 2 * p + 1:16 * comp + 2 * p + 2] = pltpu.roll(piece, 64, 1)
    flat = square[...].T
    for d in range(64):
        force_box[d] = flat[d:d + 1]
    force_in[dom] = force_box[dom]

    @pl.loop(1, doms)
    def _(step):
        other = lax.rem(dom + step, doms)
        send(force_box.at[other], force_in.at[dom], force_send, force_recv, (slab, other))

    settle(late_in, LATE, late_recv)
    for t, value in enumerate(select(late_in, LATE, 4, home_hots[512:768])):
        feature_out[t * LANES:(t + 1) * LANES] += value
    settle(early_out, EARLY, early_send)
    settle(late_out, LATE, late_send)

    settle(force_in, 1, force_recv)
    for d in range(64):
        square[d:d + 1] = force_in[d]
    picked = sum(tn(piece, home_hot[...]) for piece in parts_of(square[0:64], 2))
    right = home_rank[...]
    result = [jnp.sum(picked[16 * comp:16 * comp + 16] * right, axis=0, keepdims=True) for comp in range(4)]
    for comp in range(3):
        force_out[comp:comp + 1] = result[comp]
    energy_out[...] = result[3].reshape(atoms)
    settle(force_box, 1, force_send)


def local(
    positions, species, domain, neighbours, ghost_lists,
    embed_weight, tensor_weight, env_weight, scalar_mix, vector_mix, latent_weight, energy_weight,
):
    slots, ghosts, atoms = neighbours.shape[1], ghost_lists.shape[1], positions.shape[1]
    blocks = slots // WIDE
    v = lambda shape, dtype=F32: pltpu.VMEM(shape, dtype)
    dma = pltpu.SemaphoreType.DMA
    scratch = [
        v((64, 1, LANES)), v((64, 1, LANES)), v((LANES, LANES)), v((2, 8, ghosts)), v((2, 8, ghosts)),
        dma, dma, dma((2,)), dma((2,)),
        v((8, 2 * slots)), v((NEIGH, slots), jnp.int32), v((2, slots, ghosts), BF16),
        v((64, atoms), BF16), v((slots, atoms), BF16), v((16, atoms)), v((WIDE, 384)),
        v((8, 2 * slots)), v((8, slots)), v((2, 8, ghosts)),
        v((64 * EARLY, LANES)), v((64 * EARLY, LANES)), v((64 * LATE, LANES)), v((64 * LATE, LANES)),
        v((64, 1, LANES)), v((64, 1, LANES)),
        dma, dma, dma, dma, dma, dma, dma((2,)), dma((2,)),
        v((256, 32), BF16), v((320, 256), BF16), v((384, 160), BF16), v((288, 256), BF16), v((256, 64), BF16),
        v((256, WIDE)), v((320, 256), BF16), v((416, 160), BF16), v((320, 256), BF16), v((256, 64), BF16),
        v((16, 256), BF16), v((128, 256)),
        v((blocks, 11, NEIGH, WIDE)), v((8, SPAN)),
        v((ROUNDS, 256, SPAN), BF16), v((ROUNDS, 256, SPAN), BF16), v((ROUNDS, 256, SPAN), BF16),
        v((ROUNDS, 64, SPAN)), v((ROUNDS, 128, SPAN)), v((ROUNDS, 32, SPAN)),
        v((ROUNDS, 256, SPAN), BF16), v((ROUNDS, 256, SPAN), BF16), v((ROUNDS, 256, SPAN), BF16),
        v((ROUNDS, 256, SPAN), BF16), v((ROUNDS, 64, SPAN)), v((ROUNDS, 32, SPAN)), v((ROUNDS, 8, SPAN)),
        v((4, 32, WIDE)), v((4, 32, WIDE)), v((4, 32, WIDE)), v((4, 32, WIDE)),
        v((256, WIDE)), v((96, LANES)), v((8, WIDE)), v((8, WIDE)),
    ]
    forces, atom_energy, atom_features = pl.pallas_call(
        whole_kernel,
        out_shape=(
            jax.ShapeDtypeStruct((3, atoms), F32),
            jax.ShapeDtypeStruct((atoms,), F32),
            jax.ShapeDtypeStruct((384, atoms), F32),
        ),
        in_specs=[pl.BlockSpec(memory_space=pltpu.VMEM)] * 12,
        out_specs=[pl.BlockSpec(memory_space=pltpu.VMEM)] * 3,
        scratch_shapes=scratch,
        compiler_params=pltpu.CompilerParams(
            collective_id=0, has_side_effects=True, vmem_limit_bytes=56 * 1024 * 1024),
    )(positions, species, domain.T, neighbours, ghost_lists, embed_weight, tensor_weight.T,
      env_weight.transpose(0, 2, 1), scalar_mix.T, vector_mix, latent_weight, energy_weight)
    return forces, atom_energy, atom_features


def solution(mesh):
    both = ("slab", "dom")
    in_specs = (P(None, both), P(both), P(both, None), P(None, both), P(None, both)) + (P(),) * 7
    out_specs = (P(None, both), P(both), P(None, both))
    return jax.shard_map(local, mesh=mesh, in_specs=in_specs, out_specs=out_specs, check_vma=False)
```

```python
import math

import jax
import jax.numpy as jnp
from jax import lax
from jax.experimental import pallas as pl
from jax.experimental.pallas import tpu as pltpu
from jax.sharding import PartitionSpec as P

F32 = jnp.float32
BF16 = jnp.bfloat16
LANES = 128
SINE = [(-1) ** i * math.pi ** (2 * i + 1) / math.factorial(2 * i + 1) for i in range(6)]
COSINE = [(-1) ** i * math.pi ** (2 * i) / math.factorial(2 * i) for i in range(7)]
WIDE = 256
NEIGH = 16
UNROLL = 2
TOGETHER = 4
SPAN = TOGETHER * WIDE
ROUNDS = NEIGH // TOGETHER
MESH = pl.DeviceIdType.MESH
EXACT_PARTS = 3
RANKS = 12
PARTS = (8, 16, 16)
SENDS = 7


def mm(a, b):
    return jnp.dot(a, b, preferred_element_type=F32)


def sine_parts(turns):
    whole = jnp.floor(turns + 0.5)
    part = turns - whole
    sign = 1.0 - 2.0 * (whole - 2.0 * jnp.floor(whole * 0.5))
    square = part * part
    sine = jnp.full_like(part, SINE[-1])
    for coefficient in SINE[-2::-1]:
        sine = sine * square + coefficient
    cosine = jnp.full_like(part, COSINE[-1])
    for coefficient in COSINE[-2::-1]:
        cosine = cosine * square + coefficient
    return sine * part * sign, cosine * sign


def silu_parts(half):
    half = half.astype(BF16)
    gate = jnp.tanh(half)
    rise = 1.0 + gate
    value = half * rise
    slope = rise + value * (1.0 - gate)
    return value, slope


def parts_of(value, count):
    found = []
    for _ in range(count):
        piece = value.astype(BF16)
        found.append(piece)
        value = value - piece.astype(F32)
    return found


def tn(a, b):
    return lax.dot_general(a, b, (((0,), (0,)), ((), ())), preferred_element_type=F32)


def nt(a, b):
    return lax.dot_general(a, b, (((1,), (1,)), ((), ())), preferred_element_type=F32)


def partners():
    slab, dom = lax.axis_index("slab"), lax.axis_index("dom")
    slabs, doms = lax.axis_size("slab"), lax.axis_size("dom")
    linear = slab * doms + dom
    after = lax.rem(linear + 1, slabs * doms)
    before = lax.rem(linear + slabs * doms - 1, slabs * doms)
    split = lambda index: (index // doms, lax.rem(index, doms))
    return slab, dom, doms, split(before), split(after)


def greet(slab, dom, doms, before, after):
    barrier = pltpu.get_barrier_semaphore()

    @pl.loop(1, doms, unroll=SENDS)
    def _(step):
        pl.semaphore_signal(
            barrier, inc=1, device_id=(slab, lax.rem(dom + step, doms)), device_id_type=MESH)

    for other in (before, after):
        pl.semaphore_signal(barrier, inc=1, device_id=other, device_id_type=MESH)
    return barrier


def send(source, target, send_sem, recv_sem, device):
    copy = pltpu.make_async_remote_copy(
        src_ref=source, dst_ref=target, send_sem=send_sem, recv_sem=recv_sem,
        device_id=device, device_id_type=MESH)
    copy.start()
    return copy


def reordered(slot):
    source = jnp.right_shift(slot * 43691, 19)
    return (slot - 12 * source) * 64 + source


def arrange_weights(
    embed_weight, tensor_turned, env_turned, scalar_turned, vector_mix, latent_weight, energy_weight,
    w_in, w_first, w_mix, w_second, w_third, w_energy, b_second, b_mix, b_first, b_amp, b_in, stage,
):
    chan, width = tensor_turned.shape
    lat0, lat1 = latent_weight[0].astype(F32) * 0.5, latent_weight[1].astype(F32) * 0.5
    b_first[...] = lat0.astype(BF16)
    b_second[...] = lat1.astype(BF16)
    w_first[0:32] = tensor_turned[...]
    w_first[32:64] = env_turned[0]
    w_second[0:32] = env_turned[1]
    small = jnp.concatenate(
        [tensor_turned[...], env_turned[0], env_turned[1], jnp.zeros((chan, width), BF16)], axis=0)
    small = small.astype(F32).T.astype(BF16)
    b_amp[...] = small[:, :64]
    w_first[64:] = lat0[:width].T.astype(BF16)
    w_second[32:] = lat1[:width].T.astype(BF16)
    w_third[...] = lat1[width:].T.astype(BF16)
    embed = embed_weight[...].astype(F32) * 0.5
    b_in[...] = embed[:16].astype(BF16)
    w_in[...] = jnp.concatenate([embed, jnp.zeros((8, width), F32)], axis=0).T.astype(BF16)
    energy = jnp.broadcast_to(energy_weight[...].astype(F32).reshape(1, width), (8, width))
    w_energy[...] = energy.T[:, 0:1] + jnp.zeros((width, WIDE), F32)
    stage[...] = jnp.zeros_like(stage)
    stage[0:32, 0:32] = vector_mix[...]
    turned = stage[:, 0:LANES].T[0:32, 0:32]
    stage[0:32, 0:64] = scalar_turned[...]
    for m in range(3):
        stage[32 + 32 * m:64 + 32 * m, 64 + 32 * m:96 + 32 * m] = turned
    core = stage[...]
    b_mix[...] = jnp.zeros_like(b_mix)
    b_mix[0:width, 0:32] = small[:, 64:96]
    b_mix[width:, 32:] = core.T[0:160].astype(BF16)
    w_mix[...] = jnp.zeros_like(w_mix)
    w_mix[0:width, 0:64] = lat0[width:].T.astype(BF16)
    w_mix[width:] = core[:, 0:160].astype(BF16)


def locate(row):
    part = 0 if row < 8 else 1 if row < 24 else 2
    return part, row - (0, 8, 24)[part]


def whole_kernel(
    positions, species, domain, neighbours, ghost_lists,
    embed_weight, tensor_turned, env_turned, scalar_turned, vector_mix, latent_weight, energy_weight,
    force_out, energy_out, feature_out,
    outbox, inbox, square, lend, arrive, box_send, box_recv, ghost_send, ghost_recv,
    ext, near, picks, home_hot, home_hots, home_rank, flipped, grad, energies, back_in,
    out_a, out_b, out_c, in_a, in_b, in_c, force_box, force_in,
    part_send, part_recv, force_send, force_recv, back_send, back_recv,
    w_in, w_first, w_mix, w_second, w_third, w_energy, b_second, b_mix, b_first, b_amp, b_in, stage,
    geo, kind_hot, lat0, slope0, half0, amp, tens, envl, lat1, slope1, half1, dlat, dscal, damp, back,
    dens0, dens1, ddens0, ddens1, summary, ghost_acc, centre_acc, energy_acc,
):
    part_out, part_in = (out_a, out_b, out_c), (in_a, in_b, in_c)
    slab, dom, doms, before, after = partners()
    barrier = greet(slab, dom, doms, before, after)
    atoms = positions.shape[1]
    slots = neighbours.shape[1]
    ghosts = ghost_lists.shape[1]

    spread = jnp.broadcast_to(domain[...].astype(F32), (8, atoms))
    target = spread.T[:, 0:1].astype(jnp.int32)
    hot = (lax.broadcasted_iota(jnp.int32, (atoms, doms), 1) == target).astype(F32)
    hot16 = hot.astype(BF16)
    lower = (lax.broadcasted_iota(jnp.int32, (atoms, atoms), 0)
             > lax.broadcasted_iota(jnp.int32, (atoms, atoms), 1)).astype(F32).astype(BF16)
    rank = jnp.sum(hot * mm(lower, hot16), axis=1, keepdims=True)
    values = jnp.concatenate(
        [positions[...], species[...].astype(F32).reshape(1, atoms) + 1.0, jnp.zeros((4, atoms), F32)], axis=0).T
    lane = lax.broadcasted_iota(jnp.int32, (atoms, LANES), 1)
    lane_rank = jnp.bitwise_and(lane, 15).astype(F32)
    lane_comp = jnp.right_shift(lane, 4)
    packed = jnp.zeros((atoms, LANES), F32)
    for c in range(4):
        packed = jnp.where((lane_comp == c) & (lane_rank == rank), values[:, c:c + 1], packed)
    message = sum(tn(hot16, piece) for piece in parts_of(packed, EXACT_PARTS))
    for d in range(64):
        outbox[d] = message[d:d + 1]
    inbox[dom] = outbox[dom]

    pl.semaphore_wait(barrier, doms + 1)

    @pl.loop(1, doms, unroll=SENDS)
    def _(step):
        other = lax.rem(dom + step, doms)
        send(outbox.at[other], inbox.at[dom], box_send, box_recv, (slab, other))

    code = jnp.where(lane == 0, target.astype(F32), jnp.where(lane == 1, rank, 0.0))
    code = code.T
    target, rank = code[0:1], code[1:2]
    index = neighbours[...]
    pieces = jnp.concatenate(
        [jnp.right_shift(index, 7).astype(F32), jnp.bitwise_and(index, LANES - 1).astype(F32)], axis=0)
    place = lax.broadcasted_iota(jnp.int32, (slots, slots), 1)
    place = jnp.bitwise_and(place, 63) * 12 + jnp.right_shift(place, 6)
    mover = (lax.broadcasted_iota(jnp.int32, (slots, slots), 0) == place).astype(F32).astype(BF16)
    moved = mm(pieces.astype(BF16), mover).astype(jnp.int32)
    index = moved[:16] * LANES + moved[16:]
    near[...] = jnp.where(index < slots, reordered(index), index)
    lists = reordered(ghost_lists[...])
    rows = lax.broadcasted_iota(jnp.int32, (slots, ghosts), 0)
    for i in range(2):
        picks[i] = (rows == lists[i:i + 1]).astype(F32).astype(BF16)

    arrived = pltpu.make_async_copy(inbox.at[pl.ds(0, 63)], inbox.at[pl.ds(0, 63)], box_recv)
    arrived.wait()
    square[...] = jnp.zeros_like(square)
    for s in range(64):
        square[s:s + 1] = inbox[s]
    turned = square[...].T
    rolled = pltpu.roll(turned, 64, 1)
    first = lax.broadcasted_iota(jnp.int32, (1, LANES), 1) < 64
    ext[4:8, 0:slots] = jnp.zeros((4, slots), F32)
    for c in range(4):
        for p in range(slots // LANES):
            even = turned[16 * c + 2 * p:16 * c + 2 * p + 1]
            odd = rolled[16 * c + 2 * p + 1:16 * c + 2 * p + 2]
            both = jnp.where(first, even, odd)
            ext[c:c + 1, p * LANES:(p + 1) * LANES] = both - 1.0 if c == 3 else both
    own = jnp.concatenate(parts_of(ext[:, 0:slots], EXACT_PARTS), axis=0)
    copies = []
    for i, other in ((0, before), (1, after)):
        value = mm(own, picks[i])
        lend[i] = value[0:8] + value[8:16] + value[16:24]
        copies.append(send(lend.at[i], arrive.at[i], ghost_send.at[i], ghost_recv.at[i], other))
    hot = (lax.broadcasted_iota(jnp.int32, (64, atoms), 0).astype(F32) == target).astype(F32)
    home_hot[...] = hot.astype(BF16)
    for r in range(RANKS):
        home_hots[64 * r:64 * r + 64] = jnp.where(rank == float(r), hot, 0.0).astype(BF16)
    home_rank[...] = (lax.broadcasted_iota(jnp.int32, (16, atoms), 0).astype(F32) == rank).astype(F32)
    arrange_weights(
        embed_weight, tensor_turned, env_turned, scalar_turned, vector_mix, latent_weight, energy_weight,
        w_in, w_first, w_mix, w_second, w_third, w_energy, b_second, b_mix, b_first, b_amp, b_in, stage)
    pltpu.make_async_copy(outbox.at[pl.ds(0, 63)], outbox.at[pl.ds(0, 63)], box_send).wait()
    for copy in copies:
        copy.wait()
    ext[:, slots:slots + ghosts] = arrive[1]
    ext[:, slots + ghosts:] = arrive[0]
    blocks = geo.shape[0]
    sub = ext.shape[1] // LANES
    own = ext
    ghost_acc[...] = jnp.zeros_like(ghost_acc)

    for piece in range(blocks * WIDE // LANES):
        b, half = piece // 2, piece % 2
        lanes = pl.ds(half * LANES, LANES)
        index = near[:, piece * LANES:(piece + 1) * LANES]
        low = jnp.bitwise_and(index, LANES - 1)
        high = jnp.right_shift(index, 7)
        got = []
        for comp in range(4):
            value = jnp.zeros((NEIGH, LANES), F32)
            for h in range(sub):
                row = jnp.broadcast_to(ext[comp:comp + 1, h * LANES:(h + 1) * LANES], (NEIGH, LANES))
                taken = jnp.take_along_axis(row, low, axis=1)
                value = jnp.where(high == h, taken, value)
            got.append(value)
        mine = [own[c:c + 1, piece * LANES:(piece + 1) * LANES] for c in range(4)]
        off = [got[c] - mine[c] for c in range(3)]
        radius = jnp.sqrt(off[0] * off[0] + off[1] * off[1] + off[2] * off[2] + 0.25)
        inv = 1.0 / radius
        x = jnp.minimum(radius * 0.2, 1.0)
        x2 = x * x
        x3 = x2 * x
        x5 = x2 * x3
        u = 1.0 + x3 * x3 * (-28.0 + x * (48.0 - 21.0 * x))
        du = -168.0 * x5 * (1.0 - x) * (1.0 - x)
        du = jnp.where(radius < 5.0, du, 0.0)
        slot = piece * LANES + lax.broadcasted_iota(jnp.int32, (NEIGH, LANES), 1)
        live = (mine[3] >= 0.0) & (got[3] >= 0.0) & (index != slot)
        w = jnp.where(live, u, 0.0)
        items = [w, off[0] * inv, off[1] * inv, off[2] * inv, x, u, du, inv, got[3],
                 jnp.where(radius < 5.0, 0.2, 0.0), jnp.where(live, du, 0.0)]
        for c, item in enumerate(items):
            geo[b, c, :, lanes] = item

    def side_by_side(pieces):
        return jnp.concatenate(pieces, axis=1)

    def row(b, c, k):
        return side_by_side([geo[b, c, pl.ds(k * TOGETHER + i, 1), :] for i in range(TOGETHER)])

    def tiled(value):
        return side_by_side([value] * TOGETHER)

    def folded(value):
        return sum(value[:, i * WIDE:(i + 1) * WIDE] for i in range(TOGETHER))

    @pl.loop(0, blocks)
    def _(b):
        start = pl.multiple_of(b * WIDE, WIDE)
        eight = lax.broadcasted_iota(jnp.int32, (8, SPAN), 0).astype(F32)
        my_kind = tiled(own[3:4, pl.ds(start, WIDE)])
        kind_hot[...] = (jnp.broadcast_to(my_kind, (8, SPAN)) == eight).astype(F32)
        order = eight + 1.0
        at, base = b * ROUNDS, 4 * b
        for ref in (dens0, dens1, ddens1):
            ref[pl.ds(base, 4)] = jnp.zeros((4,) + ref.shape[1:], F32)
        for ref in (summary, energy_acc):
            ref[...] = jnp.zeros_like(ref)


        def harmonics(k):
            return row(b, 0, k), [row(b, 1 + m, k) for m in range(3)]

        @pl.loop(0, ROUNDS, unroll=UNROLL)
        def _(k):
            w, ys = harmonics(k)
            x = row(b, 4, k)
            scale = row(b, 5, k) / x
            basis = sine_parts(order * x)[0] * scale
            hot = (jnp.broadcast_to(row(b, 8, k), (8, SPAN)) == eight).astype(F32)
            inputs = jnp.concatenate([basis, kind_hot[...], hot, jnp.zeros_like(hot)], axis=0)
            half = mm(w_in[...], inputs.astype(BF16))
            value, slope = silu_parts(half)
            latent = value.astype(BF16)
            lat0[k] = latent
            slope0[at + k] = slope.astype(BF16)
            result = mm(w_first[...], latent)
            amp[at + k] = result[:64]
            half0[k] = result[64:].astype(BF16)
            env = result[32:64] * (w * 0.25)
            dens0[base + 0] += folded(env)
            for m in range(3):
                dens0[base + m + 1] += folded(env * ys[m])

        @pl.loop(0, ROUNDS, unroll=UNROLL)
        def _(k):
            w, ys = harmonics(k)
            a = amp[at + k, 0:32]
            d = [tiled(dens0[base + m]) for m in range(4)]
            inner = d[1] * ys[0] + d[2] * ys[1] + d[3] * ys[2]
            pieces = [a * d[0], a * inner] + [a * (d[m + 1] + ys[m] * d[0]) for m in range(3)]
            joined = jnp.concatenate(pieces, axis=0).astype(BF16)
            result = mm(w_mix[...], joined)
            tens[k] = result[256:]
            value, slope = silu_parts(half0[k] + result[:256].astype(BF16))
            slope1[at + k] = slope.astype(BF16)
            latent = lat0[k] + value
            lat1[k] = latent
            result = mm(w_second[...], latent)
            envl[at + k] = result[:32]
            half1[k] = result[32:].astype(BF16)
            env = result[:32] * (w * 0.25)
            dens1[base + 0] += folded(env)
            for m in range(3):
                dens1[base + m + 1] += folded(env * ys[m])

        @pl.loop(0, ROUNDS, unroll=UNROLL)
        def _(k):
            w, ys = harmonics(k)
            t = [tens[k, 32 * m:32 * m + 32] for m in range(4)]
            d = [tiled(dens1[base + m]) for m in range(4)]
            joined = jnp.concatenate(
                [t[0] * d[0], t[1] * d[1] + t[2] * d[2] + t[3] * d[3]], axis=0).astype(BF16)
            value, slope = silu_parts(half1[k] + mm(w_third[...], joined).astype(BF16))
            latent = (lat1[k] + value).astype(BF16).astype(F32)
            summary[...] += folded(latent * w)
            weigh = tiled(w_energy[...])
            edge = jnp.sum(latent * weigh, axis=0, keepdims=True)
            back[at + k, 0:1] = edge
            energy_acc[...] += jnp.broadcast_to(folded(edge * w), (8, WIDE))
            dl2 = (weigh * w).astype(BF16)
            result = mm(b_second[...], (dl2 * slope).astype(BF16))
            dlat[at + k] = dl2 + result[:256].astype(BF16)
            dscal[at + k] = result[256:]
            ddens1[base + 0] += folded(result[256:288] * t[0])
            for m in range(3):
                ddens1[base + m + 1] += folded(result[288:320] * t[m + 1])

        for p in range(WIDE // LANES):
            lanes = slice(p * LANES, (p + 1) * LANES)
            for half in range(2):
                flipped[lanes, half * LANES:(half + 1) * LANES] = (
                    summary[half * LANES:(half + 1) * LANES, lanes] * 0.25).T
            flipped[lanes, 2 * LANES:] = jnp.concatenate([dens1[base + m, :, lanes] for m in range(4)], axis=0).T

        def pack(place):
            for r in range(4):
                for t in range(3):
                    part, row = place(3 * r + t)
                    rows = PARTS[part]
                    for i in range(8):
                        part_out[part][pl.ds(rows * 8 * i + row, 8, stride=rows), :] = (
                            flipped[64 * r + 8 * i:64 * r + 8 * i + 8, t * LANES:(t + 1) * LANES])

        def post(part):
            rows = PARTS[part]

            @pl.loop(1, doms, unroll=SENDS)
            def _(step):
                other = lax.rem(dom + step, doms)
                send(part_out[part].at[pl.ds(pl.multiple_of(other * rows, 8), rows)],
                     part_in[part].at[pl.ds(pl.multiple_of(dom * rows, 8), rows)],
                     part_send.at[part], part_recv.at[part], (slab, other))

        for block in range(3):
            @pl.when(b == block)
            def _(block=block):
                pack(lambda row: locate(12 * block + row))
                post(block)

        energies[:, pl.ds(start, WIDE)] = energy_acc[...]

    @pl.loop(0, blocks)
    def _(b):
        start = pl.multiple_of(b * WIDE, WIDE)
        eight = lax.broadcasted_iota(jnp.int32, (8, SPAN), 0).astype(F32)
        order = eight + 1.0
        at, base = b * ROUNDS, 4 * b
        for ref in (ddens0, centre_acc):
            ref[...] = jnp.zeros_like(ref)


        def harmonics(k):
            return row(b, 0, k), [row(b, 1 + m, k) for m in range(3)]

        @pl.loop(0, ROUNDS, unroll=UNROLL)
        def _(k):
            w, ys = harmonics(k)
            q = [tiled(ddens1[base + m] * 0.25) for m in range(4)]
            env = envl[at + k]
            total = q[0] + q[1] * ys[0] + q[2] * ys[1] + q[3] * ys[2]
            dw = jnp.sum(env * total, axis=0, keepdims=True)
            env = env * w
            dy = [env * q[m + 1] for m in range(3)]
            da, db = dscal[at + k, 0:32], dscal[at + k, 32:64]
            pieces = [total * w, da * tiled(dens1[base + 0])] + [db * tiled(dens1[base + m + 1]) for m in range(3)]
            mixed = mm(b_mix[...], jnp.concatenate(pieces, axis=0).astype(BF16))
            dl1 = dlat[at + k] + mixed[:256].astype(BF16)
            result = mm(b_first[...], (dl1 * slope1[at + k]))
            dlat[at + k] = dl1 + result[:256].astype(BF16)
            da = result[256:288] + mixed[256:288]
            db = result[288:320] + mixed[288:320]
            dv = [mixed[320 + 32 * m:352 + 32 * m] for m in range(3)]
            a = amp[at + k, 0:32]
            d = [tiled(dens0[base + m]) for m in range(4)]
            inner = d[1] * ys[0] + d[2] * ys[1] + d[3] * ys[2]
            damp[k] = da * d[0] + db * inner + sum(dv[m] * (d[m + 1] + ys[m] * d[0]) for m in range(3))
            ba = db * a
            va = [dv[m] * a for m in range(3)]
            ddens0[0] += folded(da * a + va[0] * ys[0] + va[1] * ys[1] + va[2] * ys[2])
            for m in range(3):
                ddens0[m + 1] += folded(ba * ys[m] + va[m])
                dy[m] += ba * d[m + 1] + va[m] * d[0]
            back[at + k, 0:1] += dw
            for m in range(3):
                back[at + k, m + 1:m + 2] = jnp.sum(dy[m], axis=0, keepdims=True)

        @pl.loop(0, ROUNDS, unroll=UNROLL)
        def _(k):
            w, ys = harmonics(k)
            q = [tiled(ddens0[m] * 0.25) for m in range(4)]
            env = amp[at + k, 32:64]
            total = q[0] + q[1] * ys[0] + q[2] * ys[1] + q[3] * ys[2]
            dw = back[at + k, 0:1] + jnp.sum(env * total, axis=0, keepdims=True)
            env = env * w
            dy = [back[at + k, m + 1:m + 2] + jnp.sum(env * q[m + 1], axis=0, keepdims=True) for m in range(3)]
            joined = jnp.concatenate([damp[k], total * w], axis=0).astype(BF16)
            dl0 = dlat[at + k] + mm(b_amp[...], joined).astype(BF16)
            dbasis = mm(b_in[...], (dl0 * slope0[at + k]))[:8]
            x, u, du, inv = row(b, 4, k), row(b, 5, k), row(b, 6, k), row(b, 7, k)
            ix = 1.0 / x
            sine, cosine = sine_parts(order * x)
            slope = cosine * order * (math.pi * u * ix) + sine * ((du - u * ix) * ix)
            dx = jnp.sum(dbasis * slope, axis=0, keepdims=True) + dw * row(b, 10, k)
            dr = dx * row(b, 9, k)
            along = (ys[0] * dy[0] + ys[1] * dy[1] + ys[2] * dy[2]) * inv
            force = [ys[m] * (dr - along) + dy[m] * inv for m in range(3)]
            centre_acc[...] += folded(jnp.concatenate(force + [jnp.zeros((5, SPAN), F32)], axis=0))
            index = side_by_side(
                [near[pl.ds(k * TOGETHER + i, 1), pl.ds(start, WIDE)] for i in range(TOGETHER)])
            low = jnp.bitwise_and(index, LANES - 1)
            high = jnp.right_shift(index, 7)
            picker = (lax.broadcasted_iota(jnp.int32, (LANES, SPAN), 0) == low).astype(F32).astype(BF16)
            places = lax.broadcasted_iota(jnp.int32, (16, SPAN), 0) == high
            spread = [jnp.where(places, f, 0.0) for f in force]
            spread = jnp.concatenate(spread, axis=0)
            top = spread.astype(BF16)
            rest = (spread - top.astype(F32)).astype(BF16)
            both = jnp.concatenate([top, rest], axis=0)
            ghost_acc[...] += lax.dot_general(
                both, picker, (((1,), (1,)), ((), ())), preferred_element_type=F32)

        grad[:, pl.ds(start, WIDE)] = -centre_acc[...]

    grad[:, slots:] = jnp.zeros_like(grad[:, slots:])
    for comp in range(3):
        for h in range(sub):
            lanes = slice(h * LANES, (h + 1) * LANES)
            grad[comp:comp + 1, lanes] += (
                ghost_acc[16 * comp + h:16 * comp + h + 1] + ghost_acc[48 + 16 * comp + h:49 + 16 * comp + h])
    copies = [
        send(grad.at[:, pl.ds(slots, ghosts)], back_in.at[0], back_send.at[0], back_recv.at[0], before),
        send(grad.at[:, pl.ds(slots + ghosts, ghosts)], back_in.at[1], back_send.at[1], back_recv.at[1], after),
    ]

    def settle(box, rows, sem):
        most = box.at[pl.ds(0, 63 * rows)]
        pltpu.make_async_copy(most, most, sem).wait()

    for part, rows in enumerate(PARTS):
        mine = pl.ds(pl.multiple_of(dom * rows, 8), rows)
        part_in[part][mine] = part_out[part][mine]

    def select(ranks):
        found = []
        for t in range(3):
            pieces = []
            for r in ranks:
                part, row = locate(3 * r + t)
                pieces.append(part_in[part][pl.ds(row, 64, stride=PARTS[part]), :])
            found += parts_of(jnp.concatenate(pieces, axis=0), 2)
        hots = home_hots[64 * ranks[0]:64 * ranks[-1] + 64]
        value = tn(jnp.concatenate(found, axis=1), hots)
        return [value[2 * t * LANES:(2 * t + 1) * LANES] + value[(2 * t + 1) * LANES:(2 * t + 2) * LANES]
                for t in range(3)]

    settle(in_a, PARTS[0], part_recv.at[0])
    settle(in_b, PARTS[1], part_recv.at[1])
    for t, value in enumerate(select(range(8))):
        feature_out[t * LANES:(t + 1) * LANES] = value

    for copy in copies:
        copy.wait()
    total = grad[:, 0:slots]
    for i in range(2):
        value = nt(jnp.concatenate(parts_of(back_in[i], 2), axis=0), picks[1 - i])
        total = total + value[:8] + value[8:]
    square[...] = jnp.zeros_like(square)
    rows = [-total[comp:comp + 1] for comp in range(3)] + [energies[0:1]]
    for comp in range(4):
        for p in range(slots // LANES):
            piece = rows[comp][:, p * LANES:(p + 1) * LANES]
            square[16 * comp + 2 * p:16 * comp + 2 * p + 1] = piece
            square[16 * comp + 2 * p + 1:16 * comp + 2 * p + 2] = pltpu.roll(piece, 64, 1)
    flat = square[...].T
    for d in range(64):
        force_box[d] = flat[d:d + 1]
    force_in[dom] = force_box[dom]

    @pl.loop(1, doms, unroll=SENDS)
    def _(step):
        other = lax.rem(dom + step, doms)
        send(force_box.at[other], force_in.at[dom], force_send, force_recv, (slab, other))

    settle(in_c, PARTS[2], part_recv.at[2])
    for t, value in enumerate(select(range(8, RANKS))):
        feature_out[t * LANES:(t + 1) * LANES] += value
    for part, rows in enumerate(PARTS):
        settle(part_out[part], rows, part_send.at[part])

    settle(force_in, 1, force_recv)
    for d in range(64):
        square[d:d + 1] = force_in[d]
    picked = sum(tn(piece, home_hot[...]) for piece in parts_of(square[0:64], 2))
    right = home_rank[...]
    result = [jnp.sum(picked[16 * comp:16 * comp + 16] * right, axis=0, keepdims=True) for comp in range(4)]
    for comp in range(3):
        force_out[comp:comp + 1] = result[comp]
    energy_out[...] = result[3].reshape(atoms)
    settle(force_box, 1, force_send)


def local(
    positions, species, domain, neighbours, ghost_lists,
    embed_weight, tensor_weight, env_weight, scalar_mix, vector_mix, latent_weight, energy_weight,
):
    slots, ghosts, atoms = neighbours.shape[1], ghost_lists.shape[1], positions.shape[1]
    blocks = slots // WIDE
    v = lambda shape, dtype=F32: pltpu.VMEM(shape, dtype)
    dma = pltpu.SemaphoreType.DMA
    scratch = [
        v((64, 1, LANES)), v((64, 1, LANES)), v((LANES, LANES)), v((2, 8, ghosts)), v((2, 8, ghosts)),
        dma, dma, dma((2,)), dma((2,)),
        v((8, 2 * slots)), v((NEIGH, slots), jnp.int32), v((2, slots, ghosts), BF16),
        v((64, atoms), BF16), v((slots, atoms), BF16), v((16, atoms)), v((WIDE, 384)),
        v((8, 2 * slots)), v((8, slots)), v((2, 8, ghosts)),
        *[v((64 * rows, LANES)) for rows in PARTS], *[v((64 * rows, LANES)) for rows in PARTS],
        v((64, 1, LANES)), v((64, 1, LANES)),
        dma((3,)), dma((3,)), dma, dma, dma((2,)), dma((2,)),
        v((256, 32), BF16), v((320, 256), BF16), v((384, 160), BF16), v((288, 256), BF16), v((256, 64), BF16),
        v((256, WIDE)), v((320, 256), BF16), v((416, 160), BF16), v((320, 256), BF16), v((256, 64), BF16),
        v((16, 256), BF16), v((128, 256)),
        v((blocks, 11, NEIGH, WIDE)), v((8, SPAN)),
        v((ROUNDS, 256, SPAN), BF16), v((blocks * ROUNDS, 256, SPAN), BF16), v((ROUNDS, 256, SPAN), BF16),
        v((blocks * ROUNDS, 64, SPAN)), v((ROUNDS, 128, SPAN)), v((blocks * ROUNDS, 32, SPAN)),
        v((ROUNDS, 256, SPAN), BF16), v((blocks * ROUNDS, 256, SPAN), BF16), v((ROUNDS, 256, SPAN), BF16),
        v((blocks * ROUNDS, 256, SPAN), BF16), v((blocks * ROUNDS, 64, SPAN)), v((ROUNDS, 32, SPAN)),
        v((blocks * ROUNDS, 8, SPAN)),
        v((4 * blocks, 32, WIDE)), v((4 * blocks, 32, WIDE)), v((4, 32, WIDE)), v((4 * blocks, 32, WIDE)),
        v((256, WIDE)), v((96, LANES)), v((8, WIDE)), v((8, WIDE)),
    ]
    forces, atom_energy, atom_features = pl.pallas_call(
        whole_kernel,
        out_shape=(
            jax.ShapeDtypeStruct((3, atoms), F32),
            jax.ShapeDtypeStruct((atoms,), F32),
            jax.ShapeDtypeStruct((384, atoms), F32),
        ),
        in_specs=[pl.BlockSpec(memory_space=pltpu.VMEM)] * 12,
        out_specs=[pl.BlockSpec(memory_space=pltpu.VMEM)] * 3,
        scratch_shapes=scratch,
        compiler_params=pltpu.CompilerParams(
            collective_id=0, has_side_effects=True, vmem_limit_bytes=56 * 1024 * 1024),
    )(positions, species, domain.T, neighbours, ghost_lists, embed_weight, tensor_weight.T,
      env_weight.transpose(0, 2, 1), scalar_mix.T, vector_mix, latent_weight, energy_weight)
    return forces, atom_energy, atom_features


def solution(mesh):
    both = ("slab", "dom")
    in_specs = (P(None, both), P(both), P(both, None), P(None, both), P(None, both)) + (P(),) * 7
    out_specs = (P(None, both), P(both), P(None, both))
    return jax.shard_map(local, mesh=mesh, in_specs=in_specs, out_specs=out_specs, check_vma=False)
```

```python
import math

import jax
import jax.numpy as jnp
from jax import lax
from jax.experimental import pallas as pl
from jax.experimental.pallas import tpu as pltpu
from jax.sharding import PartitionSpec as P

F32 = jnp.float32
BF16 = jnp.bfloat16
LANES = 128
SINE = [(-1) ** i * math.pi ** (2 * i + 1) / math.factorial(2 * i + 1) for i in range(6)]
COSINE = [(-1) ** i * math.pi ** (2 * i) / math.factorial(2 * i) for i in range(7)]
WIDE = 256
NEIGH = 16
UNROLL = 1
TOGETHER = 8
SPAN = TOGETHER * WIDE
ROUNDS = NEIGH // TOGETHER
MESH = pl.DeviceIdType.MESH
EXACT_PARTS = 3
RANKS = 12
PARTS = (8, 16, 16)
SENDS = 7


def mm(a, b):
    return jnp.dot(a, b, preferred_element_type=F32)


def sine_parts(turns):
    whole = jnp.floor(turns + 0.5)
    part = turns - whole
    sign = 1.0 - 2.0 * (whole - 2.0 * jnp.floor(whole * 0.5))
    square = part * part
    sine = jnp.full_like(part, SINE[-1])
    for coefficient in SINE[-2::-1]:
        sine = sine * square + coefficient
    cosine = jnp.full_like(part, COSINE[-1])
    for coefficient in COSINE[-2::-1]:
        cosine = cosine * square + coefficient
    return sine * part * sign, cosine * sign


def silu_parts(half):
    half = half.astype(BF16)
    gate = jnp.tanh(half)
    rise = 1.0 + gate
    value = half * rise
    slope = rise + value * (1.0 - gate)
    return value, slope


def parts_of(value, count):
    found = []
    for _ in range(count):
        piece = value.astype(BF16)
        found.append(piece)
        value = value - piece.astype(F32)
    return found


def tn(a, b):
    return lax.dot_general(a, b, (((0,), (0,)), ((), ())), preferred_element_type=F32)


def nt(a, b):
    return lax.dot_general(a, b, (((1,), (1,)), ((), ())), preferred_element_type=F32)


def partners():
    slab, dom = lax.axis_index("slab"), lax.axis_index("dom")
    slabs, doms = lax.axis_size("slab"), lax.axis_size("dom")
    linear = slab * doms + dom
    after = lax.rem(linear + 1, slabs * doms)
    before = lax.rem(linear + slabs * doms - 1, slabs * doms)
    split = lambda index: (index // doms, lax.rem(index, doms))
    return slab, dom, doms, split(before), split(after)


def greet(slab, dom, doms, before, after):
    barrier = pltpu.get_barrier_semaphore()

    @pl.loop(1, doms, unroll=SENDS)
    def _(step):
        pl.semaphore_signal(
            barrier, inc=1, device_id=(slab, lax.rem(dom + step, doms)), device_id_type=MESH)

    for other in (before, after):
        pl.semaphore_signal(barrier, inc=1, device_id=other, device_id_type=MESH)
    return barrier


def send(source, target, send_sem, recv_sem, device):
    copy = pltpu.make_async_remote_copy(
        src_ref=source, dst_ref=target, send_sem=send_sem, recv_sem=recv_sem,
        device_id=device, device_id_type=MESH)
    copy.start()
    return copy


def reordered(slot):
    source = jnp.right_shift(slot * 43691, 19)
    return (slot - 12 * source) * 64 + source


def arrange_weights(
    embed_weight, tensor_turned, env_turned, scalar_turned, vector_mix, latent_weight, energy_weight,
    w_in, w_first, w_mix, w_second, w_third, w_energy, b_second, b_mix, b_first, b_amp, b_in, stage,
):
    chan, width = tensor_turned.shape
    lat0, lat1 = latent_weight[0].astype(F32) * 0.5, latent_weight[1].astype(F32) * 0.5
    b_first[...] = lat0.astype(BF16)
    b_second[...] = lat1.astype(BF16)
    w_first[0:32] = tensor_turned[...]
    w_first[32:64] = env_turned[0]
    w_second[0:32] = env_turned[1]
    small = jnp.concatenate(
        [tensor_turned[...], env_turned[0], env_turned[1], jnp.zeros((chan, width), BF16)], axis=0)
    small = small.astype(F32).T.astype(BF16)
    b_amp[...] = small[:, :64]
    w_first[64:] = lat0[:width].T.astype(BF16)
    w_second[32:] = lat1[:width].T.astype(BF16)
    w_third[...] = lat1[width:].T.astype(BF16)
    embed = embed_weight[...].astype(F32) * 0.5
    b_in[...] = embed[:16].astype(BF16)
    w_in[...] = jnp.concatenate([embed, jnp.zeros((8, width), F32)], axis=0).T.astype(BF16)
    energy = jnp.broadcast_to(energy_weight[...].astype(F32).reshape(1, width), (8, width))
    w_energy[...] = energy.T[:, 0:1] + jnp.zeros((width, WIDE), F32)
    stage[...] = jnp.zeros_like(stage)
    stage[0:32, 0:32] = vector_mix[...]
    turned = stage[:, 0:LANES].T[0:32, 0:32]
    stage[0:32, 0:64] = scalar_turned[...]
    for m in range(3):
        stage[32 + 32 * m:64 + 32 * m, 64 + 32 * m:96 + 32 * m] = turned
    core = stage[...]
    b_mix[...] = jnp.zeros_like(b_mix)
    b_mix[0:width, 0:32] = small[:, 64:96]
    b_mix[width:, 32:] = core.T[0:160].astype(BF16)
    w_mix[...] = jnp.zeros_like(w_mix)
    w_mix[0:width, 0:64] = lat0[width:].T.astype(BF16)
    w_mix[width:] = core[:, 0:160].astype(BF16)


def locate(row):
    part = 0 if row < 8 else 1 if row < 24 else 2
    return part, row - (0, 8, 24)[part]


def whole_kernel(
    positions, species, domain, neighbours, ghost_lists,
    embed_weight, tensor_turned, env_turned, scalar_turned, vector_mix, latent_weight, energy_weight,
    force_out, energy_out, feature_out,
    outbox, inbox, square, lend, arrive, box_send, box_recv, ghost_send, ghost_recv,
    ext, near, picks, home_hot, home_hots, home_rank, flipped, grad, energies, back_in,
    out_a, out_b, out_c, in_a, in_b, in_c, force_box, force_in,
    part_send, part_recv, force_send, force_recv, back_send, back_recv,
    w_in, w_first, w_mix, w_second, w_third, w_energy, b_second, b_mix, b_first, b_amp, b_in, stage,
    geo, kind_hot, lat0, slope0, half0, amp, tens, envl, lat1, slope1, half1, dlat, dscal, damp, back,
    dens0, dens1, ddens0, ddens1, summary, ghost_acc, centre_acc, energy_acc,
):
    part_out, part_in = (out_a, out_b, out_c), (in_a, in_b, in_c)
    slab, dom, doms, before, after = partners()
    barrier = greet(slab, dom, doms, before, after)
    atoms = positions.shape[1]
    slots = neighbours.shape[1]
    ghosts = ghost_lists.shape[1]

    spread = jnp.broadcast_to(domain[...].astype(F32), (8, atoms))
    target = spread.T[:, 0:1].astype(jnp.int32)
    hot = (lax.broadcasted_iota(jnp.int32, (atoms, doms), 1) == target).astype(F32)
    hot16 = hot.astype(BF16)
    lower = (lax.broadcasted_iota(jnp.int32, (atoms, atoms), 0)
             > lax.broadcasted_iota(jnp.int32, (atoms, atoms), 1)).astype(F32).astype(BF16)
    rank = jnp.sum(hot * mm(lower, hot16), axis=1, keepdims=True)
    values = jnp.concatenate(
        [positions[...], species[...].astype(F32).reshape(1, atoms) + 1.0, jnp.zeros((4, atoms), F32)], axis=0).T
    lane = lax.broadcasted_iota(jnp.int32, (atoms, LANES), 1)
    lane_rank = jnp.bitwise_and(lane, 15).astype(F32)
    lane_comp = jnp.right_shift(lane, 4)
    packed = jnp.zeros((atoms, LANES), F32)
    for c in range(4):
        packed = jnp.where((lane_comp == c) & (lane_rank == rank), values[:, c:c + 1], packed)
    message = sum(tn(hot16, piece) for piece in parts_of(packed, EXACT_PARTS))
    for d in range(64):
        outbox[d] = message[d:d + 1]
    inbox[dom] = outbox[dom]

    pl.semaphore_wait(barrier, doms + 1)

    @pl.loop(1, doms, unroll=SENDS)
    def _(step):
        other = lax.rem(dom + step, doms)
        send(outbox.at[other], inbox.at[dom], box_send, box_recv, (slab, other))

    code = jnp.where(lane == 0, target.astype(F32), jnp.where(lane == 1, rank, 0.0))
    code = code.T
    target, rank = code[0:1], code[1:2]
    index = neighbours[...]
    pieces = jnp.concatenate(
        [jnp.right_shift(index, 7).astype(F32), jnp.bitwise_and(index, LANES - 1).astype(F32)], axis=0)
    place = lax.broadcasted_iota(jnp.int32, (slots, slots), 1)
    place = jnp.bitwise_and(place, 63) * 12 + jnp.right_shift(place, 6)
    mover = (lax.broadcasted_iota(jnp.int32, (slots, slots), 0) == place).astype(F32).astype(BF16)
    moved = mm(pieces.astype(BF16), mover).astype(jnp.int32)
    index = moved[:16] * LANES + moved[16:]
    near[...] = jnp.where(index < slots, reordered(index), index)
    lists = reordered(ghost_lists[...])
    rows = lax.broadcasted_iota(jnp.int32, (slots, ghosts), 0)
    for i in range(2):
        picks[i] = (rows == lists[i:i + 1]).astype(F32).astype(BF16)

    arrived = pltpu.make_async_copy(inbox.at[pl.ds(0, 63)], inbox.at[pl.ds(0, 63)], box_recv)
    arrived.wait()
    square[...] = jnp.zeros_like(square)
    for s in range(64):
        square[s:s + 1] = inbox[s]
    turned = square[...].T
    rolled = pltpu.roll(turned, 64, 1)
    first = lax.broadcasted_iota(jnp.int32, (1, LANES), 1) < 64
    ext[4:8, 0:slots] = jnp.zeros((4, slots), F32)
    for c in range(4):
        for p in range(slots // LANES):
            even = turned[16 * c + 2 * p:16 * c + 2 * p + 1]
            odd = rolled[16 * c + 2 * p + 1:16 * c + 2 * p + 2]
            both = jnp.where(first, even, odd)
            ext[c:c + 1, p * LANES:(p + 1) * LANES] = both - 1.0 if c == 3 else both
    own = jnp.concatenate(parts_of(ext[:, 0:slots], EXACT_PARTS), axis=0)
    copies = []
    for i, other in ((0, before), (1, after)):
        value = mm(own, picks[i])
        lend[i] = value[0:8] + value[8:16] + value[16:24]
        copies.append(send(lend.at[i], arrive.at[i], ghost_send.at[i], ghost_recv.at[i], other))
    hot = (lax.broadcasted_iota(jnp.int32, (64, atoms), 0).astype(F32) == target).astype(F32)
    home_hot[...] = hot.astype(BF16)
    for r in range(RANKS):
        home_hots[64 * r:64 * r + 64] = jnp.where(rank == float(r), hot, 0.0).astype(BF16)
    home_rank[...] = (lax.broadcasted_iota(jnp.int32, (16, atoms), 0).astype(F32) == rank).astype(F32)
    arrange_weights(
        embed_weight, tensor_turned, env_turned, scalar_turned, vector_mix, latent_weight, energy_weight,
        w_in, w_first, w_mix, w_second, w_third, w_energy, b_second, b_mix, b_first, b_amp, b_in, stage)
    pltpu.make_async_copy(outbox.at[pl.ds(0, 63)], outbox.at[pl.ds(0, 63)], box_send).wait()
    for copy in copies:
        copy.wait()
    ext[:, slots:slots + ghosts] = arrive[1]
    ext[:, slots + ghosts:] = arrive[0]
    blocks = geo.shape[0]
    sub = ext.shape[1] // LANES
    own = ext
    ghost_acc[...] = jnp.zeros_like(ghost_acc)

    for piece in range(blocks * WIDE // LANES):
        b, half = piece // 2, piece % 2
        lanes = pl.ds(half * LANES, LANES)
        index = near[:, piece * LANES:(piece + 1) * LANES]
        low = jnp.bitwise_and(index, LANES - 1)
        high = jnp.right_shift(index, 7)
        got = []
        for comp in range(4):
            value = jnp.zeros((NEIGH, LANES), F32)
            for h in range(sub):
                row = jnp.broadcast_to(ext[comp:comp + 1, h * LANES:(h + 1) * LANES], (NEIGH, LANES))
                taken = jnp.take_along_axis(row, low, axis=1)
                value = jnp.where(high == h, taken, value)
            got.append(value)
        mine = [own[c:c + 1, piece * LANES:(piece + 1) * LANES] for c in range(4)]
        off = [got[c] - mine[c] for c in range(3)]
        radius = jnp.sqrt(off[0] * off[0] + off[1] * off[1] + off[2] * off[2] + 0.25)
        inv = 1.0 / radius
        x = jnp.minimum(radius * 0.2, 1.0)
        x2 = x * x
        x3 = x2 * x
        x5 = x2 * x3
        u = 1.0 + x3 * x3 * (-28.0 + x * (48.0 - 21.0 * x))
        du = -168.0 * x5 * (1.0 - x) * (1.0 - x)
        du = jnp.where(radius < 5.0, du, 0.0)
        slot = piece * LANES + lax.broadcasted_iota(jnp.int32, (NEIGH, LANES), 1)
        live = (mine[3] >= 0.0) & (got[3] >= 0.0) & (index != slot)
        w = jnp.where(live, u, 0.0)
        items = [w, off[0] * inv, off[1] * inv, off[2] * inv, x, u, du, inv, got[3],
                 jnp.where(radius < 5.0, 0.2, 0.0), jnp.where(live, du, 0.0)]
        for c, item in enumerate(items):
            geo[b, c, :, lanes] = item

    def side_by_side(pieces):
        return jnp.concatenate(pieces, axis=1)

    def row(b, c, k):
        return side_by_side([geo[b, c, pl.ds(k * TOGETHER + i, 1), :] for i in range(TOGETHER)])

    def tiled(value):
        return side_by_side([value] * TOGETHER)

    def folded(value):
        return sum(value[:, i * WIDE:(i + 1) * WIDE] for i in range(TOGETHER))

    @pl.loop(0, blocks)
    def _(b):
        start = pl.multiple_of(b * WIDE, WIDE)
        eight = lax.broadcasted_iota(jnp.int32, (8, SPAN), 0).astype(F32)
        my_kind = tiled(own[3:4, pl.ds(start, WIDE)])
        kind_hot[...] = (jnp.broadcast_to(my_kind, (8, SPAN)) == eight).astype(F32)
        order = eight + 1.0
        at, base = b * ROUNDS, 4 * b
        for ref in (dens0, dens1, ddens1):
            ref[pl.ds(base, 4)] = jnp.zeros((4,) + ref.shape[1:], F32)
        for ref in (summary, energy_acc):
            ref[...] = jnp.zeros_like(ref)


        def harmonics(k):
            return row(b, 0, k), [row(b, 1 + m, k) for m in range(3)]

        @pl.loop(0, ROUNDS, unroll=UNROLL)
        def _(k):
            w, ys = harmonics(k)
            x = row(b, 4, k)
            scale = row(b, 5, k) / x
            basis = sine_parts(order * x)[0] * scale
            hot = (jnp.broadcast_to(row(b, 8, k), (8, SPAN)) == eight).astype(F32)
            inputs = jnp.concatenate([basis, kind_hot[...], hot, jnp.zeros_like(hot)], axis=0)
            half = mm(w_in[...], inputs.astype(BF16))
            value, slope = silu_parts(half)
            latent = value.astype(BF16)
            lat0[k] = latent
            slope0[at + k] = slope.astype(BF16)
            result = mm(w_first[...], latent)
            amp[at + k] = result[:64]
            half0[k] = result[64:].astype(BF16)
            env = result[32:64] * (w * 0.25)
            dens0[base + 0] += folded(env)
            for m in range(3):
                dens0[base + m + 1] += folded(env * ys[m])

        @pl.loop(0, ROUNDS, unroll=UNROLL)
        def _(k):
            w, ys = harmonics(k)
            a = amp[at + k, 0:32]
            d = [tiled(dens0[base + m]) for m in range(4)]
            inner = d[1] * ys[0] + d[2] * ys[1] + d[3] * ys[2]
            pieces = [a * d[0], a * inner] + [a * (d[m + 1] + ys[m] * d[0]) for m in range(3)]
            joined = jnp.concatenate(pieces, axis=0).astype(BF16)
            result = mm(w_mix[...], joined)
            tens[k] = result[256:]
            value, slope = silu_parts(half0[k] + result[:256].astype(BF16))
            slope1[at + k] = slope.astype(BF16)
            latent = lat0[k] + value
            lat1[k] = latent
            result = mm(w_second[...], latent)
            envl[at + k] = result[:32]
            half1[k] = result[32:].astype(BF16)
            env = result[:32] * (w * 0.25)
            dens1[base + 0] += folded(env)
            for m in range(3):
                dens1[base + m + 1] += folded(env * ys[m])

        @pl.loop(0, ROUNDS, unroll=UNROLL)
        def _(k):
            w, ys = harmonics(k)
            t = [tens[k, 32 * m:32 * m + 32] for m in range(4)]
            d = [tiled(dens1[base + m]) for m in range(4)]
            joined = jnp.concatenate(
                [t[0] * d[0], t[1] * d[1] + t[2] * d[2] + t[3] * d[3]], axis=0).astype(BF16)
            value, slope = silu_parts(half1[k] + mm(w_third[...], joined).astype(BF16))
            latent = (lat1[k] + value).astype(BF16).astype(F32)
            summary[...] += folded(latent * w)
            weigh = tiled(w_energy[...])
            edge = jnp.sum(latent * weigh, axis=0, keepdims=True)
            back[at + k, 0:1] = edge
            energy_acc[...] += jnp.broadcast_to(folded(edge * w), (8, WIDE))
            dl2 = (weigh * w).astype(BF16)
            result = mm(b_second[...], (dl2 * slope).astype(BF16))
            dlat[at + k] = dl2 + result[:256].astype(BF16)
            dscal[at + k] = result[256:]
            ddens1[base + 0] += folded(result[256:288] * t[0])
            for m in range(3):
                ddens1[base + m + 1] += folded(result[288:320] * t[m + 1])

        for p in range(WIDE // LANES):
            lanes = slice(p * LANES, (p + 1) * LANES)
            for half in range(2):
                flipped[lanes, half * LANES:(half + 1) * LANES] = (
                    summary[half * LANES:(half + 1) * LANES, lanes] * 0.25).T
            flipped[lanes, 2 * LANES:] = jnp.concatenate([dens1[base + m, :, lanes] for m in range(4)], axis=0).T

        def pack(place):
            for r in range(4):
                for t in range(3):
                    part, row = place(3 * r + t)
                    rows = PARTS[part]
                    for i in range(8):
                        part_out[part][pl.ds(rows * 8 * i + row, 8, stride=rows), :] = (
                            flipped[64 * r + 8 * i:64 * r + 8 * i + 8, t * LANES:(t + 1) * LANES])

        def post(part):
            rows = PARTS[part]

            @pl.loop(1, doms, unroll=SENDS)
            def _(step):
                other = lax.rem(dom + step, doms)
                send(part_out[part].at[pl.ds(pl.multiple_of(other * rows, 8), rows)],
                     part_in[part].at[pl.ds(pl.multiple_of(dom * rows, 8), rows)],
                     part_send.at[part], part_recv.at[part], (slab, other))

        for block in range(3):
            @pl.when(b == block)
            def _(block=block):
                pack(lambda row: locate(12 * block + row))
                post(block)

        energies[:, pl.ds(start, WIDE)] = energy_acc[...]

    @pl.loop(0, blocks)
    def _(b):
        start = pl.multiple_of(b * WIDE, WIDE)
        eight = lax.broadcasted_iota(jnp.int32, (8, SPAN), 0).astype(F32)
        order = eight + 1.0
        at, base = b * ROUNDS, 4 * b
        for ref in (ddens0, centre_acc):
            ref[...] = jnp.zeros_like(ref)


        def harmonics(k):
            return row(b, 0, k), [row(b, 1 + m, k) for m in range(3)]

        @pl.loop(0, ROUNDS, unroll=UNROLL)
        def _(k):
            w, ys = harmonics(k)
            q = [tiled(ddens1[base + m] * 0.25) for m in range(4)]
            env = envl[at + k]
            total = q[0] + q[1] * ys[0] + q[2] * ys[1] + q[3] * ys[2]
            dw = jnp.sum(env * total, axis=0, keepdims=True)
            env = env * w
            dy = [env * q[m + 1] for m in range(3)]
            da, db = dscal[at + k, 0:32], dscal[at + k, 32:64]
            pieces = [total * w, da * tiled(dens1[base + 0])] + [db * tiled(dens1[base + m + 1]) for m in range(3)]
            mixed = mm(b_mix[...], jnp.concatenate(pieces, axis=0).astype(BF16))
            dl1 = dlat[at + k] + mixed[:256].astype(BF16)
            result = mm(b_first[...], (dl1 * slope1[at + k]))
            dlat[at + k] = dl1 + result[:256].astype(BF16)
            da = result[256:288] + mixed[256:288]
            db = result[288:320] + mixed[288:320]
            dv = [mixed[320 + 32 * m:352 + 32 * m] for m in range(3)]
            a = amp[at + k, 0:32]
            d = [tiled(dens0[base + m]) for m in range(4)]
            inner = d[1] * ys[0] + d[2] * ys[1] + d[3] * ys[2]
            damp[k] = da * d[0] + db * inner + sum(dv[m] * (d[m + 1] + ys[m] * d[0]) for m in range(3))
            ba = db * a
            va = [dv[m] * a for m in range(3)]
            ddens0[0] += folded(da * a + va[0] * ys[0] + va[1] * ys[1] + va[2] * ys[2])
            for m in range(3):
                ddens0[m + 1] += folded(ba * ys[m] + va[m])
                dy[m] += ba * d[m + 1] + va[m] * d[0]
            back[at + k, 0:1] += dw
            for m in range(3):
                back[at + k, m + 1:m + 2] = jnp.sum(dy[m], axis=0, keepdims=True)

        @pl.loop(0, ROUNDS, unroll=UNROLL)
        def _(k):
            w, ys = harmonics(k)
            q = [tiled(ddens0[m] * 0.25) for m in range(4)]
            env = amp[at + k, 32:64]
            total = q[0] + q[1] * ys[0] + q[2] * ys[1] + q[3] * ys[2]
            dw = back[at + k, 0:1] + jnp.sum(env * total, axis=0, keepdims=True)
            env = env * w
            dy = [back[at + k, m + 1:m + 2] + jnp.sum(env * q[m + 1], axis=0, keepdims=True) for m in range(3)]
            joined = jnp.concatenate([damp[k], total * w], axis=0).astype(BF16)
            dl0 = dlat[at + k] + mm(b_amp[...], joined).astype(BF16)
            dbasis = mm(b_in[...], (dl0 * slope0[at + k]))[:8]
            x, u, du, inv = row(b, 4, k), row(b, 5, k), row(b, 6, k), row(b, 7, k)
            ix = 1.0 / x
            sine, cosine = sine_parts(order * x)
            slope = cosine * order * (math.pi * u * ix) + sine * ((du - u * ix) * ix)
            dx = jnp.sum(dbasis * slope, axis=0, keepdims=True) + dw * row(b, 10, k)
            dr = dx * row(b, 9, k)
            along = (ys[0] * dy[0] + ys[1] * dy[1] + ys[2] * dy[2]) * inv
            force = [ys[m] * (dr - along) + dy[m] * inv for m in range(3)]
            centre_acc[...] += folded(jnp.concatenate(force + [jnp.zeros((5, SPAN), F32)], axis=0))
            index = side_by_side(
                [near[pl.ds(k * TOGETHER + i, 1), pl.ds(start, WIDE)] for i in range(TOGETHER)])
            low = jnp.bitwise_and(index, LANES - 1)
            high = jnp.right_shift(index, 7)
            picker = (lax.broadcasted_iota(jnp.int32, (LANES, SPAN), 0) == low).astype(F32).astype(BF16)
            places = lax.broadcasted_iota(jnp.int32, (16, SPAN), 0) == high
            spread = [jnp.where(places, f, 0.0) for f in force]
            spread = jnp.concatenate(spread, axis=0)
            top = spread.astype(BF16)
            rest = (spread - top.astype(F32)).astype(BF16)
            both = jnp.concatenate([top, rest], axis=0)
            ghost_acc[...] += lax.dot_general(
                both, picker, (((1,), (1,)), ((), ())), preferred_element_type=F32)

        grad[:, pl.ds(start, WIDE)] = -centre_acc[...]

    grad[:, slots:] = jnp.zeros_like(grad[:, slots:])
    for comp in range(3):
        for h in range(sub):
            lanes = slice(h * LANES, (h + 1) * LANES)
            grad[comp:comp + 1, lanes] += (
                ghost_acc[16 * comp + h:16 * comp + h + 1] + ghost_acc[48 + 16 * comp + h:49 + 16 * comp + h])
    copies = [
        send(grad.at[:, pl.ds(slots, ghosts)], back_in.at[0], back_send.at[0], back_recv.at[0], before),
        send(grad.at[:, pl.ds(slots + ghosts, ghosts)], back_in.at[1], back_send.at[1], back_recv.at[1], after),
    ]

    def settle(box, rows, sem):
        most = box.at[pl.ds(0, 63 * rows)]
        pltpu.make_async_copy(most, most, sem).wait()

    for part, rows in enumerate(PARTS):
        mine = pl.ds(pl.multiple_of(dom * rows, 8), rows)
        part_in[part][mine] = part_out[part][mine]

    def select(ranks):
        found = []
        for t in range(3):
            pieces = []
            for r in ranks:
                part, row = locate(3 * r + t)
                pieces.append(part_in[part][pl.ds(row, 64, stride=PARTS[part]), :])
            found += parts_of(jnp.concatenate(pieces, axis=0), 2)
        hots = home_hots[64 * ranks[0]:64 * ranks[-1] + 64]
        value = tn(jnp.concatenate(found, axis=1), hots)
        return [value[2 * t * LANES:(2 * t + 1) * LANES] + value[(2 * t + 1) * LANES:(2 * t + 2) * LANES]
                for t in range(3)]

    settle(in_a, PARTS[0], part_recv.at[0])
    settle(in_b, PARTS[1], part_recv.at[1])
    for t, value in enumerate(select(range(8))):
        feature_out[t * LANES:(t + 1) * LANES] = value

    for copy in copies:
        copy.wait()
    total = grad[:, 0:slots]
    for i in range(2):
        value = nt(jnp.concatenate(parts_of(back_in[i], 2), axis=0), picks[1 - i])
        total = total + value[:8] + value[8:]
    square[...] = jnp.zeros_like(square)
    rows = [-total[comp:comp + 1] for comp in range(3)] + [energies[0:1]]
    for comp in range(4):
        for p in range(slots // LANES):
            piece = rows[comp][:, p * LANES:(p + 1) * LANES]
            square[16 * comp + 2 * p:16 * comp + 2 * p + 1] = piece
            square[16 * comp + 2 * p + 1:16 * comp + 2 * p + 2] = pltpu.roll(piece, 64, 1)
    flat = square[...].T
    for d in range(64):
        force_box[d] = flat[d:d + 1]
    force_in[dom] = force_box[dom]

    @pl.loop(1, doms, unroll=SENDS)
    def _(step):
        other = lax.rem(dom + step, doms)
        send(force_box.at[other], force_in.at[dom], force_send, force_recv, (slab, other))

    settle(in_c, PARTS[2], part_recv.at[2])
    for t, value in enumerate(select(range(8, RANKS))):
        feature_out[t * LANES:(t + 1) * LANES] += value
    for part, rows in enumerate(PARTS):
        settle(part_out[part], rows, part_send.at[part])

    settle(force_in, 1, force_recv)
    for d in range(64):
        square[d:d + 1] = force_in[d]
    picked = sum(tn(piece, home_hot[...]) for piece in parts_of(square[0:64], 2))
    right = home_rank[...]
    result = [jnp.sum(picked[16 * comp:16 * comp + 16] * right, axis=0, keepdims=True) for comp in range(4)]
    for comp in range(3):
        force_out[comp:comp + 1] = result[comp]
    energy_out[...] = result[3].reshape(atoms)
    settle(force_box, 1, force_send)


def local(
    positions, species, domain, neighbours, ghost_lists,
    embed_weight, tensor_weight, env_weight, scalar_mix, vector_mix, latent_weight, energy_weight,
):
    slots, ghosts, atoms = neighbours.shape[1], ghost_lists.shape[1], positions.shape[1]
    blocks = slots // WIDE
    v = lambda shape, dtype=F32: pltpu.VMEM(shape, dtype)
    dma = pltpu.SemaphoreType.DMA
    scratch = [
        v((64, 1, LANES)), v((64, 1, LANES)), v((LANES, LANES)), v((2, 8, ghosts)), v((2, 8, ghosts)),
        dma, dma, dma((2,)), dma((2,)),
        v((8, 2 * slots)), v((NEIGH, slots), jnp.int32), v((2, slots, ghosts), BF16),
        v((64, atoms), BF16), v((slots, atoms), BF16), v((16, atoms)), v((WIDE, 384)),
        v((8, 2 * slots)), v((8, slots)), v((2, 8, ghosts)),
        *[v((64 * rows, LANES)) for rows in PARTS], *[v((64 * rows, LANES)) for rows in PARTS],
        v((64, 1, LANES)), v((64, 1, LANES)),
        dma((3,)), dma((3,)), dma, dma, dma((2,)), dma((2,)),
        v((256, 32), BF16), v((320, 256), BF16), v((384, 160), BF16), v((288, 256), BF16), v((256, 64), BF16),
        v((256, WIDE)), v((320, 256), BF16), v((416, 160), BF16), v((320, 256), BF16), v((256, 64), BF16),
        v((16, 256), BF16), v((128, 256)),
        v((blocks, 11, NEIGH, WIDE)), v((8, SPAN)),
        v((ROUNDS, 256, SPAN), BF16), v((blocks * ROUNDS, 256, SPAN), BF16), v((ROUNDS, 256, SPAN), BF16),
        v((blocks * ROUNDS, 64, SPAN)), v((ROUNDS, 128, SPAN)), v((blocks * ROUNDS, 32, SPAN)),
        v((ROUNDS, 256, SPAN), BF16), v((blocks * ROUNDS, 256, SPAN), BF16), v((ROUNDS, 256, SPAN), BF16),
        v((blocks * ROUNDS, 256, SPAN), BF16), v((blocks * ROUNDS, 64, SPAN)), v((ROUNDS, 32, SPAN)),
        v((blocks * ROUNDS, 8, SPAN)),
        v((4 * blocks, 32, WIDE)), v((4 * blocks, 32, WIDE)), v((4, 32, WIDE)), v((4 * blocks, 32, WIDE)),
        v((256, WIDE)), v((96, LANES)), v((8, WIDE)), v((8, WIDE)),
    ]
    forces, atom_energy, atom_features = pl.pallas_call(
        whole_kernel,
        out_shape=(
            jax.ShapeDtypeStruct((3, atoms), F32),
            jax.ShapeDtypeStruct((atoms,), F32),
            jax.ShapeDtypeStruct((384, atoms), F32),
        ),
        in_specs=[pl.BlockSpec(memory_space=pltpu.VMEM)] * 12,
        out_specs=[pl.BlockSpec(memory_space=pltpu.VMEM)] * 3,
        scratch_shapes=scratch,
        compiler_params=pltpu.CompilerParams(
            collective_id=0, has_side_effects=True, vmem_limit_bytes=56 * 1024 * 1024),
    )(positions, species, domain.T, neighbours, ghost_lists, embed_weight, tensor_weight.T,
      env_weight.transpose(0, 2, 1), scalar_mix.T, vector_mix, latent_weight, energy_weight)
    return forces, atom_energy, atom_features


def solution(mesh):
    both = ("slab", "dom")
    in_specs = (P(None, both), P(both), P(both, None), P(None, both), P(None, both)) + (P(),) * 7
    out_specs = (P(None, both), P(both), P(None, both))
    return jax.shard_map(local, mesh=mesh, in_specs=in_specs, out_specs=out_specs, check_vma=False)
```

```python
import math

import jax
import jax.numpy as jnp
from jax import lax
from jax.experimental import pallas as pl
from jax.experimental.pallas import tpu as pltpu
from jax.sharding import PartitionSpec as P

F32 = jnp.float32
BF16 = jnp.bfloat16
LANES = 128
SINE = [(-1) ** i * math.pi ** (2 * i + 1) / math.factorial(2 * i + 1) for i in range(6)]
COSINE = [(-1) ** i * math.pi ** (2 * i) / math.factorial(2 * i) for i in range(7)]
WIDE = 256
NEIGH = 16
UNROLL = 1
TOGETHER = 8
SPAN = TOGETHER * WIDE
ROUNDS = NEIGH // TOGETHER
MESH = pl.DeviceIdType.MESH
EXACT_PARTS = 3
RANKS = 12
PARTS = (8, 16, 16)
SENDS = 7


def mm(a, b):
    return jnp.dot(a, b, preferred_element_type=F32)


def sine_parts(turns):
    whole = jnp.floor(turns + 0.5)
    part = turns - whole
    sign = 1.0 - 2.0 * (whole - 2.0 * jnp.floor(whole * 0.5))
    square = part * part
    sine = jnp.full_like(part, SINE[-1])
    for coefficient in SINE[-2::-1]:
        sine = sine * square + coefficient
    cosine = jnp.full_like(part, COSINE[-1])
    for coefficient in COSINE[-2::-1]:
        cosine = cosine * square + coefficient
    return sine * part * sign, cosine * sign


def silu_parts(half):
    half = half.astype(BF16)
    gate = jnp.tanh(half)
    rise = 1.0 + gate
    value = half * rise
    slope = rise + value * (1.0 - gate)
    return value, slope


def parts_of(value, count):
    found = []
    for _ in range(count):
        piece = value.astype(BF16)
        found.append(piece)
        value = value - piece.astype(F32)
    return found


def tn(a, b):
    return lax.dot_general(a, b, (((0,), (0,)), ((), ())), preferred_element_type=F32)


def nt(a, b):
    return lax.dot_general(a, b, (((1,), (1,)), ((), ())), preferred_element_type=F32)


def partners():
    slab, dom = lax.axis_index("slab"), lax.axis_index("dom")
    slabs, doms = lax.axis_size("slab"), lax.axis_size("dom")
    linear = slab * doms + dom
    after = lax.rem(linear + 1, slabs * doms)
    before = lax.rem(linear + slabs * doms - 1, slabs * doms)
    split = lambda index: (index // doms, lax.rem(index, doms))
    return slab, dom, doms, split(before), split(after)


def greet(slab, dom, doms, before, after):
    barrier = pltpu.get_barrier_semaphore()

    @pl.loop(1, doms, unroll=SENDS)
    def _(step):
        pl.semaphore_signal(
            barrier, inc=1, device_id=(slab, lax.rem(dom + step, doms)), device_id_type=MESH)

    for other in (before, after):
        pl.semaphore_signal(barrier, inc=1, device_id=other, device_id_type=MESH)
    return barrier


def send(source, target, send_sem, recv_sem, device):
    copy = pltpu.make_async_remote_copy(
        src_ref=source, dst_ref=target, send_sem=send_sem, recv_sem=recv_sem,
        device_id=device, device_id_type=MESH)
    copy.start()
    return copy


def reordered(slot):
    source = jnp.right_shift(slot * 43691, 19)
    return (slot - 12 * source) * 64 + source


def arrange_weights(
    embed_weight, tensor_turned, env_turned, scalar_turned, vector_mix, latent_weight, energy_weight,
    w_in, w_first, w_mix, w_second, w_third, w_energy, b_second, b_mix, b_first, b_amp, b_in, stage,
):
    chan, width = tensor_turned.shape
    lat0, lat1 = latent_weight[0].astype(F32) * 0.5, latent_weight[1].astype(F32) * 0.5
    b_first[...] = lat0.astype(BF16)
    b_second[...] = lat1.astype(BF16)
    w_first[0:32] = tensor_turned[...]
    w_first[32:64] = env_turned[0]
    w_second[0:32] = env_turned[1]
    small = jnp.concatenate(
        [tensor_turned[...], env_turned[0], env_turned[1], jnp.zeros((chan, width), BF16)], axis=0)
    small = small.astype(F32).T.astype(BF16)
    b_amp[...] = small[:, :64]
    w_first[64:] = lat0[:width].T.astype(BF16)
    w_second[32:] = lat1[:width].T.astype(BF16)
    w_third[...] = lat1[width:].T.astype(BF16)
    embed = embed_weight[...].astype(F32) * 0.5
    b_in[...] = embed[:16].astype(BF16)
    w_in[...] = jnp.concatenate([embed, jnp.zeros((8, width), F32)], axis=0).T.astype(BF16)
    energy = jnp.broadcast_to(energy_weight[...].astype(F32).reshape(1, width), (8, width))
    w_energy[...] = energy.T[:, 0:1] + jnp.zeros((width, WIDE), F32)
    stage[...] = jnp.zeros_like(stage)
    stage[0:32, 0:32] = vector_mix[...]
    turned = stage[:, 0:LANES].T[0:32, 0:32]
    stage[0:32, 0:64] = scalar_turned[...]
    for m in range(3):
        stage[32 + 32 * m:64 + 32 * m, 64 + 32 * m:96 + 32 * m] = turned
    core = stage[...]
    b_mix[...] = jnp.zeros_like(b_mix)
    b_mix[0:width, 0:32] = small[:, 64:96]
    b_mix[width:, 32:] = core.T[0:160].astype(BF16)
    w_mix[...] = jnp.zeros_like(w_mix)
    w_mix[0:width, 0:64] = lat0[width:].T.astype(BF16)
    w_mix[width:] = core[:, 0:160].astype(BF16)


def locate(row):
    part = 0 if row < 8 else 1 if row < 24 else 2
    return part, row - (0, 8, 24)[part]


def whole_kernel(
    positions, species, domain, neighbours, ghost_lists,
    embed_weight, tensor_turned, env_turned, scalar_turned, vector_mix, latent_weight, energy_weight,
    force_out, energy_out, feature_out,
    outbox, inbox, square, lend, arrive, box_send, box_recv, ghost_send, ghost_recv,
    ext, near, picks, home_hot, home_hots, home_rank, flipped, grad, energies, back_in,
    out_a, out_b, out_c, in_a, in_b, in_c, force_box, force_in,
    part_send, part_recv, force_send, force_recv, back_send, back_recv,
    w_in, w_first, w_mix, w_second, w_third, w_energy, b_second, b_mix, b_first, b_amp, b_in, stage,
    geo, kind_hot, lat0, slope0, half0, amp, tens, envl, lat1, slope1, half1, dlat, dscal, damp, back,
    dens0, dens1, ddens0, ddens1, summary, ghost_acc, centre_acc, energy_acc,
):
    part_out, part_in = (out_a, out_b, out_c), (in_a, in_b, in_c)
    slab, dom, doms, before, after = partners()
    barrier = greet(slab, dom, doms, before, after)
    atoms = positions.shape[1]
    slots = neighbours.shape[1]
    ghosts = ghost_lists.shape[1]

    spread = jnp.broadcast_to(domain[...].astype(F32), (8, atoms))
    target = spread.T[:, 0:1].astype(jnp.int32)
    hot = (lax.broadcasted_iota(jnp.int32, (atoms, doms), 1) == target).astype(F32)
    hot16 = hot.astype(BF16)
    lower = (lax.broadcasted_iota(jnp.int32, (atoms, atoms), 0)
             > lax.broadcasted_iota(jnp.int32, (atoms, atoms), 1)).astype(F32).astype(BF16)
    rank = jnp.sum(hot * mm(lower, hot16), axis=1, keepdims=True)
    values = jnp.concatenate(
        [positions[...], species[...].astype(F32).reshape(1, atoms) + 1.0, jnp.zeros((4, atoms), F32)], axis=0).T
    lane = lax.broadcasted_iota(jnp.int32, (atoms, LANES), 1)
    lane_rank = jnp.bitwise_and(lane, 15).astype(F32)
    lane_comp = jnp.right_shift(lane, 4)
    packed = jnp.zeros((atoms, LANES), F32)
    for c in range(4):
        packed = jnp.where((lane_comp == c) & (lane_rank == rank), values[:, c:c + 1], packed)
    message = sum(tn(hot16, piece) for piece in parts_of(packed, EXACT_PARTS))
    for d in range(64):
        outbox[d] = message[d:d + 1]
    inbox[dom] = outbox[dom]

    pl.semaphore_wait(barrier, doms + 1)

    @pl.loop(1, doms, unroll=SENDS)
    def _(step):
        other = lax.rem(dom + step, doms)
        send(outbox.at[other], inbox.at[dom], box_send, box_recv, (slab, other))

    code = jnp.where(lane == 0, target.astype(F32), jnp.where(lane == 1, rank, 0.0))
    code = code.T
    target, rank = code[0:1], code[1:2]
    index = neighbours[...]
    pieces = jnp.concatenate(
        [jnp.right_shift(index, 7).astype(F32), jnp.bitwise_and(index, LANES - 1).astype(F32)], axis=0)
    place = lax.broadcasted_iota(jnp.int32, (slots, slots), 1)
    place = jnp.bitwise_and(place, 63) * 12 + jnp.right_shift(place, 6)
    mover = (lax.broadcasted_iota(jnp.int32, (slots, slots), 0) == place).astype(F32).astype(BF16)
    moved = mm(pieces.astype(BF16), mover).astype(jnp.int32)
    index = moved[:16] * LANES + moved[16:]
    near[...] = jnp.where(index < slots, reordered(index), index)
    lists = reordered(ghost_lists[...])
    rows = lax.broadcasted_iota(jnp.int32, (slots, ghosts), 0)
    for i in range(2):
        picks[i] = (rows == lists[i:i + 1]).astype(F32).astype(BF16)

    arrived = pltpu.make_async_copy(inbox.at[pl.ds(0, 63)], inbox.at[pl.ds(0, 63)], box_recv)
    arrived.wait()
    square[...] = jnp.zeros_like(square)
    for s in range(64):
        square[s:s + 1] = inbox[s]
    turned = square[...].T
    rolled = pltpu.roll(turned, 64, 1)
    first = lax.broadcasted_iota(jnp.int32, (1, LANES), 1) < 64
    ext[4:8, 0:slots] = jnp.zeros((4, slots), F32)
    for c in range(4):
        for p in range(slots // LANES):
            even = turned[16 * c + 2 * p:16 * c + 2 * p + 1]
            odd = rolled[16 * c + 2 * p + 1:16 * c + 2 * p + 2]
            both = jnp.where(first, even, odd)
            ext[c:c + 1, p * LANES:(p + 1) * LANES] = both - 1.0 if c == 3 else both
    own = jnp.concatenate(parts_of(ext[:, 0:slots], EXACT_PARTS), axis=0)
    copies = []
    for i, other in ((0, before), (1, after)):
        value = mm(own, picks[i])
        lend[i] = value[0:8] + value[8:16] + value[16:24]
        copies.append(send(lend.at[i], arrive.at[i], ghost_send.at[i], ghost_recv.at[i], other))
    hot = (lax.broadcasted_iota(jnp.int32, (64, atoms), 0).astype(F32) == target).astype(F32)
    home_hot[...] = hot.astype(BF16)
    for r in range(RANKS):
        home_hots[64 * r:64 * r + 64] = jnp.where(rank == float(r), hot, 0.0).astype(BF16)
    home_rank[...] = (lax.broadcasted_iota(jnp.int32, (16, atoms), 0).astype(F32) == rank).astype(F32)
    arrange_weights(
        embed_weight, tensor_turned, env_turned, scalar_turned, vector_mix, latent_weight, energy_weight,
        w_in, w_first, w_mix, w_second, w_third, w_energy, b_second, b_mix, b_first, b_amp, b_in, stage)
    pltpu.make_async_copy(outbox.at[pl.ds(0, 63)], outbox.at[pl.ds(0, 63)], box_send).wait()
    for copy in copies:
        copy.wait()
    ext[:, slots:slots + ghosts] = arrive[1]
    ext[:, slots + ghosts:] = arrive[0]
    blocks = geo.shape[0]
    sub = ext.shape[1] // LANES
    own = ext
    ghost_acc[...] = jnp.zeros_like(ghost_acc)

    for piece in range(blocks * WIDE // LANES):
        b, half = piece // 2, piece % 2
        lanes = pl.ds(half * LANES, LANES)
        index = near[:, piece * LANES:(piece + 1) * LANES]
        low = jnp.bitwise_and(index, LANES - 1)
        high = jnp.right_shift(index, 7)
        got = []
        for comp in range(4):
            value = jnp.zeros((NEIGH, LANES), F32)
            for h in range(sub):
                row = jnp.broadcast_to(ext[comp:comp + 1, h * LANES:(h + 1) * LANES], (NEIGH, LANES))
                taken = jnp.take_along_axis(row, low, axis=1)
                value = jnp.where(high == h, taken, value)
            got.append(value)
        mine = [own[c:c + 1, piece * LANES:(piece + 1) * LANES] for c in range(4)]
        off = [got[c] - mine[c] for c in range(3)]
        radius = jnp.sqrt(off[0] * off[0] + off[1] * off[1] + off[2] * off[2] + 0.25)
        inv = 1.0 / radius
        x = jnp.minimum(radius * 0.2, 1.0)
        x2 = x * x
        x3 = x2 * x
        x5 = x2 * x3
        u = 1.0 + x3 * x3 * (-28.0 + x * (48.0 - 21.0 * x))
        du = -168.0 * x5 * (1.0 - x) * (1.0 - x)
        du = jnp.where(radius < 5.0, du, 0.0)
        slot = piece * LANES + lax.broadcasted_iota(jnp.int32, (NEIGH, LANES), 1)
        live = (mine[3] >= 0.0) & (got[3] >= 0.0) & (index != slot)
        w = jnp.where(live, u, 0.0)
        items = [w, off[0] * inv, off[1] * inv, off[2] * inv, x, u, du, inv, got[3],
                 jnp.where(radius < 5.0, 0.2, 0.0), jnp.where(live, du, 0.0)]
        for c, item in enumerate(items):
            geo[b, c, :, lanes] = item

    def side_by_side(pieces):
        return jnp.concatenate(pieces, axis=1)

    def row(b, c, k):
        return side_by_side([geo[b, c, pl.ds(k * TOGETHER + i, 1), :] for i in range(TOGETHER)])

    def tiled(value):
        return side_by_side([value] * TOGETHER)

    def folded(value):
        return sum(value[:, i * WIDE:(i + 1) * WIDE] for i in range(TOGETHER))

    @pl.loop(0, blocks)
    def _(b):
        start = pl.multiple_of(b * WIDE, WIDE)
        eight = lax.broadcasted_iota(jnp.int32, (8, SPAN), 0).astype(F32)
        my_kind = tiled(own[3:4, pl.ds(start, WIDE)])
        kind_hot[...] = (jnp.broadcast_to(my_kind, (8, SPAN)) == eight).astype(F32)
        order = eight + 1.0
        at, base = b * ROUNDS, 4 * b
        for ref in (dens0, dens1, ddens1):
            ref[pl.ds(base, 4)] = jnp.zeros((4,) + ref.shape[1:], F32)
        for ref in (summary, energy_acc):
            ref[...] = jnp.zeros_like(ref)


        def harmonics(k):
            return row(b, 0, k), [row(b, 1 + m, k) for m in range(3)]

        @pl.loop(0, ROUNDS, unroll=UNROLL)
        def _(k):
            w, ys = harmonics(k)
            x = row(b, 4, k)
            scale = row(b, 5, k) / x
            basis = sine_parts(order * x)[0] * scale
            hot = (jnp.broadcast_to(row(b, 8, k), (8, SPAN)) == eight).astype(F32)
            inputs = jnp.concatenate([basis, kind_hot[...], hot, jnp.zeros_like(hot)], axis=0)
            half = mm(w_in[...], inputs.astype(BF16))
            value, slope = silu_parts(half)
            latent = value.astype(BF16)
            lat0[k] = latent
            slope0[at + k] = slope.astype(BF16)
            result = mm(w_first[...], latent)
            amp[at + k] = result[:64]
            half0[k] = result[64:].astype(BF16)
            env = result[32:64] * (w * 0.25)
            dens0[base + 0] += folded(env)
            for m in range(3):
                dens0[base + m + 1] += folded(env * ys[m])

        @pl.loop(0, ROUNDS, unroll=UNROLL)
        def _(k):
            w, ys = harmonics(k)
            a = amp[at + k, 0:32]
            d = [tiled(dens0[base + m]) for m in range(4)]
            inner = d[1] * ys[0] + d[2] * ys[1] + d[3] * ys[2]
            pieces = [a * d[0], a * inner] + [a * (d[m + 1] + ys[m] * d[0]) for m in range(3)]
            joined = jnp.concatenate(pieces, axis=0).astype(BF16)
            result = mm(w_mix[...], joined)
            tens[k] = result[256:]
            value, slope = silu_parts(half0[k] + result[:256].astype(BF16))
            slope1[at + k] = slope.astype(BF16)
            latent = lat0[k] + value
            lat1[k] = latent
            result = mm(w_second[...], latent)
            envl[at + k] = result[:32]
            half1[k] = result[32:].astype(BF16)
            env = result[:32] * (w * 0.25)
            dens1[base + 0] += folded(env)
            for m in range(3):
                dens1[base + m + 1] += folded(env * ys[m])

        @pl.loop(0, ROUNDS, unroll=UNROLL)
        def _(k):
            w, ys = harmonics(k)
            t = [tens[k, 32 * m:32 * m + 32] for m in range(4)]
            d = [tiled(dens1[base + m]) for m in range(4)]
            joined = jnp.concatenate(
                [t[0] * d[0], t[1] * d[1] + t[2] * d[2] + t[3] * d[3]], axis=0).astype(BF16)
            value, slope = silu_parts(half1[k] + mm(w_third[...], joined).astype(BF16))
            latent = (lat1[k] + value).astype(BF16).astype(F32)
            summary[...] += folded(latent * w)
            weigh = tiled(w_energy[...])
            edge = jnp.sum(latent * weigh, axis=0, keepdims=True)
            back[at + k, 0:1] = edge
            energy_acc[...] += jnp.broadcast_to(folded(edge * w), (8, WIDE))
            dl2 = (weigh * w).astype(BF16)
            result = mm(b_second[...], (dl2 * slope).astype(BF16))
            dlat[at + k] = dl2 + result[:256].astype(BF16)
            dscal[at + k] = result[256:]
            ddens1[base + 0] += folded(result[256:288] * t[0])
            for m in range(3):
                ddens1[base + m + 1] += folded(result[288:320] * t[m + 1])

        for p in range(WIDE // LANES):
            lanes = slice(p * LANES, (p + 1) * LANES)
            for half in range(2):
                flipped[lanes, half * LANES:(half + 1) * LANES] = (
                    summary[half * LANES:(half + 1) * LANES, lanes] * 0.25).T
            flipped[lanes, 2 * LANES:] = jnp.concatenate([dens1[base + m, :, lanes] for m in range(4)], axis=0).T

        def pack(place):
            for r in range(4):
                for t in range(3):
                    part, row = place(3 * r + t)
                    rows = PARTS[part]
                    for i in range(8):
                        part_out[part][pl.ds(rows * 8 * i + row, 8, stride=rows), :] = (
                            flipped[64 * r + 8 * i:64 * r + 8 * i + 8, t * LANES:(t + 1) * LANES])

        def post(part):
            rows = PARTS[part]

            @pl.loop(1, doms, unroll=SENDS)
            def _(step):
                other = lax.rem(dom + step, doms)
                send(part_out[part].at[pl.ds(pl.multiple_of(other * rows, 8), rows)],
                     part_in[part].at[pl.ds(pl.multiple_of(dom * rows, 8), rows)],
                     part_send.at[part], part_recv.at[part], (slab, other))

        for block in range(3):
            @pl.when(b == block)
            def _(block=block):
                pack(lambda row: locate(12 * block + row))
                post(block)

        energies[:, pl.ds(start, WIDE)] = energy_acc[...]

    @pl.loop(0, blocks)
    def _(b):
        start = pl.multiple_of(b * WIDE, WIDE)
        eight = lax.broadcasted_iota(jnp.int32, (8, SPAN), 0).astype(F32)
        order = eight + 1.0
        at, base = b * ROUNDS, 4 * b
        for ref in (ddens0, centre_acc):
            ref[...] = jnp.zeros_like(ref)


        def harmonics(k):
            return row(b, 0, k), [row(b, 1 + m, k) for m in range(3)]

        @pl.loop(0, ROUNDS, unroll=UNROLL)
        def _(k):
            w, ys = harmonics(k)
            q = [tiled(ddens1[base + m] * 0.25) for m in range(4)]
            env = envl[at + k]
            total = q[0] + q[1] * ys[0] + q[2] * ys[1] + q[3] * ys[2]
            dw = jnp.sum(env * total, axis=0, keepdims=True)
            env = env * w
            dy = [env * q[m + 1] for m in range(3)]
            da, db = dscal[at + k, 0:32], dscal[at + k, 32:64]
            pieces = [total * w, da * tiled(dens1[base + 0])] + [db * tiled(dens1[base + m + 1]) for m in range(3)]
            mixed = mm(b_mix[...], jnp.concatenate(pieces, axis=0).astype(BF16))
            dl1 = dlat[at + k] + mixed[:256].astype(BF16)
            result = mm(b_first[...], (dl1 * slope1[at + k]))
            dlat[at + k] = dl1 + result[:256].astype(BF16)
            da = result[256:288] + mixed[256:288]
            db = result[288:320] + mixed[288:320]
            dv = [mixed[320 + 32 * m:352 + 32 * m] for m in range(3)]
            a = amp[at + k, 0:32]
            d = [tiled(dens0[base + m]) for m in range(4)]
            inner = d[1] * ys[0] + d[2] * ys[1] + d[3] * ys[2]
            damp[k] = da * d[0] + db * inner + sum(dv[m] * (d[m + 1] + ys[m] * d[0]) for m in range(3))
            ba = db * a
            va = [dv[m] * a for m in range(3)]
            ddens0[0] += folded(da * a + va[0] * ys[0] + va[1] * ys[1] + va[2] * ys[2])
            for m in range(3):
                ddens0[m + 1] += folded(ba * ys[m] + va[m])
                dy[m] += ba * d[m + 1] + va[m] * d[0]
            back[at + k, 0:1] += dw
            for m in range(3):
                back[at + k, m + 1:m + 2] = jnp.sum(dy[m], axis=0, keepdims=True)

        @pl.loop(0, ROUNDS, unroll=UNROLL)
        def _(k):
            w, ys = harmonics(k)
            q = [tiled(ddens0[m] * 0.25) for m in range(4)]
            env = amp[at + k, 32:64]
            total = q[0] + q[1] * ys[0] + q[2] * ys[1] + q[3] * ys[2]
            dw = back[at + k, 0:1] + jnp.sum(env * total, axis=0, keepdims=True)
            env = env * w
            dy = [back[at + k, m + 1:m + 2] + jnp.sum(env * q[m + 1], axis=0, keepdims=True) for m in range(3)]
            joined = jnp.concatenate([damp[k], total * w], axis=0).astype(BF16)
            dl0 = dlat[at + k] + mm(b_amp[...], joined).astype(BF16)
            dbasis = mm(b_in[...], (dl0 * slope0[at + k]))[:8]
            x, u, du, inv = row(b, 4, k), row(b, 5, k), row(b, 6, k), row(b, 7, k)
            ix = 1.0 / x
            sine, cosine = sine_parts(order * x)
            slope = cosine * order * (math.pi * u * ix) + sine * ((du - u * ix) * ix)
            dx = jnp.sum(dbasis * slope, axis=0, keepdims=True) + dw * row(b, 10, k)
            dr = dx * row(b, 9, k)
            along = (ys[0] * dy[0] + ys[1] * dy[1] + ys[2] * dy[2]) * inv
            force = [ys[m] * (dr - along) + dy[m] * inv for m in range(3)]
            centre_acc[...] += folded(jnp.concatenate(force + [jnp.zeros((5, SPAN), F32)], axis=0))
            index = side_by_side(
                [near[pl.ds(k * TOGETHER + i, 1), pl.ds(start, WIDE)] for i in range(TOGETHER)])
            low = jnp.bitwise_and(index, LANES - 1)
            high = jnp.right_shift(index, 7)
            picker = (lax.broadcasted_iota(jnp.int32, (LANES, SPAN), 0) == low).astype(F32).astype(BF16)
            places = lax.broadcasted_iota(jnp.int32, (16, SPAN), 0) == high
            spread = [jnp.where(places, f, 0.0) for f in force]
            spread = jnp.concatenate(spread, axis=0)
            top = spread.astype(BF16)
            rest = (spread - top.astype(F32)).astype(BF16)
            both = jnp.concatenate([top, rest], axis=0)
            ghost_acc[...] += lax.dot_general(
                both, picker, (((1,), (1,)), ((), ())), preferred_element_type=F32)

        grad[:, pl.ds(start, WIDE)] = -centre_acc[...]

    grad[:, slots:] = jnp.zeros_like(grad[:, slots:])
    for comp in range(3):
        for h in range(sub):
            lanes = slice(h * LANES, (h + 1) * LANES)
            grad[comp:comp + 1, lanes] += (
                ghost_acc[16 * comp + h:16 * comp + h + 1] + ghost_acc[48 + 16 * comp + h:49 + 16 * comp + h])
    copies = [
        send(grad.at[:, pl.ds(slots, ghosts)], back_in.at[0], back_send.at[0], back_recv.at[0], before),
        send(grad.at[:, pl.ds(slots + ghosts, ghosts)], back_in.at[1], back_send.at[1], back_recv.at[1], after),
    ]

    def settle(box, rows, sem):
        most = box.at[pl.ds(0, 63 * rows)]
        pltpu.make_async_copy(most, most, sem).wait()

    for part, rows in enumerate(PARTS):
        mine = pl.ds(pl.multiple_of(dom * rows, 8), rows)
        part_in[part][mine] = part_out[part][mine]

    def select(ranks):
        found = []
        for t in range(3):
            pieces = []
            for r in ranks:
                part, row = locate(3 * r + t)
                pieces.append(part_in[part][pl.ds(row, 64, stride=PARTS[part]), :])
            found.append(jnp.concatenate(pieces, axis=0).astype(BF16))
        hots = home_hots[64 * ranks[0]:64 * ranks[-1] + 64]
        value = tn(jnp.concatenate(found, axis=1), hots)
        return [value[t * LANES:(t + 1) * LANES] for t in range(3)]

    settle(in_a, PARTS[0], part_recv.at[0])
    settle(in_b, PARTS[1], part_recv.at[1])
    for t, value in enumerate(select(range(8))):
        feature_out[t * LANES:(t + 1) * LANES] = value

    for copy in copies:
        copy.wait()
    total = grad[:, 0:slots]
    for i in range(2):
        value = nt(jnp.concatenate(parts_of(back_in[i], 2), axis=0), picks[1 - i])
        total = total + value[:8] + value[8:]
    square[...] = jnp.zeros_like(square)
    rows = [-total[comp:comp + 1] for comp in range(3)] + [energies[0:1]]
    for comp in range(4):
        for p in range(slots // LANES):
            piece = rows[comp][:, p * LANES:(p + 1) * LANES]
            square[16 * comp + 2 * p:16 * comp + 2 * p + 1] = piece
            square[16 * comp + 2 * p + 1:16 * comp + 2 * p + 2] = pltpu.roll(piece, 64, 1)
    flat = square[...].T
    for d in range(64):
        force_box[d] = flat[d:d + 1]
    force_in[dom] = force_box[dom]

    @pl.loop(1, doms, unroll=SENDS)
    def _(step):
        other = lax.rem(dom + step, doms)
        send(force_box.at[other], force_in.at[dom], force_send, force_recv, (slab, other))

    settle(in_c, PARTS[2], part_recv.at[2])
    for t, value in enumerate(select(range(8, RANKS))):
        feature_out[t * LANES:(t + 1) * LANES] += value
    for part, rows in enumerate(PARTS):
        settle(part_out[part], rows, part_send.at[part])

    settle(force_in, 1, force_recv)
    for d in range(64):
        square[d:d + 1] = force_in[d]
    picked = sum(tn(piece, home_hot[...]) for piece in parts_of(square[0:64], 2))
    right = home_rank[...]
    result = [jnp.sum(picked[16 * comp:16 * comp + 16] * right, axis=0, keepdims=True) for comp in range(4)]
    for comp in range(3):
        force_out[comp:comp + 1] = result[comp]
    energy_out[...] = result[3].reshape(atoms)
    settle(force_box, 1, force_send)


def local(
    positions, species, domain, neighbours, ghost_lists,
    embed_weight, tensor_weight, env_weight, scalar_mix, vector_mix, latent_weight, energy_weight,
):
    slots, ghosts, atoms = neighbours.shape[1], ghost_lists.shape[1], positions.shape[1]
    blocks = slots // WIDE
    v = lambda shape, dtype=F32: pltpu.VMEM(shape, dtype)
    dma = pltpu.SemaphoreType.DMA
    scratch = [
        v((64, 1, LANES)), v((64, 1, LANES)), v((LANES, LANES)), v((2, 8, ghosts)), v((2, 8, ghosts)),
        dma, dma, dma((2,)), dma((2,)),
        v((8, 2 * slots)), v((NEIGH, slots), jnp.int32), v((2, slots, ghosts), BF16),
        v((64, atoms), BF16), v((slots, atoms), BF16), v((16, atoms)), v((WIDE, 384)),
        v((8, 2 * slots)), v((8, slots)), v((2, 8, ghosts)),
        *[v((64 * rows, LANES)) for rows in PARTS], *[v((64 * rows, LANES)) for rows in PARTS],
        v((64, 1, LANES)), v((64, 1, LANES)),
        dma((3,)), dma((3,)), dma, dma, dma((2,)), dma((2,)),
        v((256, 32), BF16), v((320, 256), BF16), v((384, 160), BF16), v((288, 256), BF16), v((256, 64), BF16),
        v((256, WIDE)), v((320, 256), BF16), v((416, 160), BF16), v((320, 256), BF16), v((256, 64), BF16),
        v((16, 256), BF16), v((128, 256)),
        v((blocks, 11, NEIGH, WIDE)), v((8, SPAN)),
        v((ROUNDS, 256, SPAN), BF16), v((blocks * ROUNDS, 256, SPAN), BF16), v((ROUNDS, 256, SPAN), BF16),
        v((blocks * ROUNDS, 64, SPAN)), v((ROUNDS, 128, SPAN)), v((blocks * ROUNDS, 32, SPAN)),
        v((ROUNDS, 256, SPAN), BF16), v((blocks * ROUNDS, 256, SPAN), BF16), v((ROUNDS, 256, SPAN), BF16),
        v((blocks * ROUNDS, 256, SPAN), BF16), v((blocks * ROUNDS, 64, SPAN)), v((ROUNDS, 32, SPAN)),
        v((blocks * ROUNDS, 8, SPAN)),
        v((4 * blocks, 32, WIDE)), v((4 * blocks, 32, WIDE)), v((4, 32, WIDE)), v((4 * blocks, 32, WIDE)),
        v((256, WIDE)), v((96, LANES)), v((8, WIDE)), v((8, WIDE)),
    ]
    forces, atom_energy, atom_features = pl.pallas_call(
        whole_kernel,
        out_shape=(
            jax.ShapeDtypeStruct((3, atoms), F32),
            jax.ShapeDtypeStruct((atoms,), F32),
            jax.ShapeDtypeStruct((384, atoms), F32),
        ),
        in_specs=[pl.BlockSpec(memory_space=pltpu.VMEM)] * 12,
        out_specs=[pl.BlockSpec(memory_space=pltpu.VMEM)] * 3,
        scratch_shapes=scratch,
        compiler_params=pltpu.CompilerParams(
            collective_id=0, has_side_effects=True, vmem_limit_bytes=56 * 1024 * 1024),
    )(positions, species, domain.T, neighbours, ghost_lists, embed_weight, tensor_weight.T,
      env_weight.transpose(0, 2, 1), scalar_mix.T, vector_mix, latent_weight, energy_weight)
    return forces, atom_energy, atom_features


def solution(mesh):
    both = ("slab", "dom")
    in_specs = (P(None, both), P(both), P(both, None), P(None, both), P(None, both)) + (P(),) * 7
    out_specs = (P(None, both), P(both), P(None, both))
    return jax.shard_map(local, mesh=mesh, in_specs=in_specs, out_specs=out_specs, check_vma=False)
```
